128 devices in a mesh: dp: 128 (over x, z, y, core).
Axes of the slice: x: 4, y: 4, z: 4, core: 2. Of those that a mesh axis runs over, the one named last changes fastest.
Arguments:
- block_input: bfloat16 [16384, 512], P('dp')
- cotangent: bfloat16 [16384, 512], P('dp'), may hold values from -6 to 6
- segment_ids: int32 [128, 128], P('dp'), may hold values from 0 to 4, never falling along the last dimension, each value on 1 to 32 neighbouring positions
- attn_master: float32 [4, 512, 512], P(None, 'dp')
- up_master: float32 [512, 2048], P('dp'), may hold values from -0.25 to 0.25
- down_master: float32 [2048, 512], P('dp'), may hold values from -0.25 to 0.25
- vec_master: float32 [12, 512], P(None, 'dp')
- attn_moment: float32 [4, 512, 512], P(None, 'dp'), may hold values from -0.0078125 to 0.0078125
- up_moment: float32 [512, 2048], P('dp'), may hold values from -0.0078125 to 0.0078125
- down_moment: float32 [2048, 512], P('dp'), may hold values from -0.0078125 to 0.0078125
- vec_moment: float32 [12, 512], P(None, 'dp'), may hold values from -0.0024414062 to 0.0024414062
- vec_second: float32 [12, 512], P(None, 'dp'), may hold values from 1.4277229e-09 to 2.2843567e-08
Outputs:
- layer_out: bfloat16 [16384, 512], P('dp')
- input_grad: bfloat16 [16384, 512], P('dp')
- clip_norm: float32 [], replicated
- attn_momentum_new: float32 [4, 512, 512], P(None, 'dp')
- up_momentum_new: float32 [512, 2048], P('dp')
- down_momentum_new: float32 [2048, 512], P('dp')
- attn_new: float32 [4, 512, 512], P(None, 'dp')
- up_new: float32 [512, 2048], P('dp')
- down_new: float32 [2048, 512], P('dp')
- attn_copy: bfloat16 [4, 512, 512], P(None, 'dp')
- up_copy: bfloat16 [512, 2048], P('dp')
- down_copy: bfloat16 [2048, 512], P('dp')
- vec_moment_new: float32 [12, 512], P(None, 'dp')
- vec_second_new: float32 [12, 512], P(None, 'dp')
- vec_new: float32 [12, 512], P(None, 'dp')
- vec_copy: bfloat16 [12, 512], P(None, 'dp')
The draws below stay inside these ranges and needn't reach their ends.
Inputs may be any that keep to these rules, and one draw needn't show every extreme that they name: `segment_ids`: in each packed row the sentence numbers start at 0 and never fall; each of the 5 sentences has 1 to 32 tokens, and one sentence of each row has exactly 32.
All inputs are finite; a program needn't handle non-finite values.
Results may differ from the reference program's by a relative error of at most 0.014.
The reference program's roundings to bfloat16 on the way count: a program that leaves them out, or rounds other values in their place, can miss the bound.
Values may be sent and summed in bfloat16 or wider, within the bound.
No kernel may reach another device: no remote copies, remote signals or barrier semaphores. Data moves between devices by JAX's collectives and lax.ppermute only.
A program may use at most 128 MiB of HBM per device.

```python
import math
import jax
import jax.numpy as jnp
import numpy as np
from jax import lax

D = 512
FF = 2048
H = 8
HD = 64
ROW = 128
STEP = 10
NS_ITERS = 5
SENTS = 5
MOST = 32
TOKENS = 16384
VROWS = 12
NPARAM = 3151872
N_DP = 128


def draw_block_input(key, part):
    key = jax.random.fold_in(key, 11)
    first_key = jax.random.fold_in(key, 0)
    column_pos = jnp.arange(D, dtype=jnp.float32) / (D - 1) - 0.5
    rising = jnp.exp(math.log(3.0) * column_pos)
    noise_draw = jax.random.normal(first_key, (TOKENS, D), jnp.float32)
    return (noise_draw * rising[None, :]).astype(jnp.bfloat16)


def draw_attn_master(key, part):
    key = jax.random.fold_in(key, 12)
    noise_draw = jax.random.normal(key, (4, D, D), jnp.float32)
    factors = jnp.array([1.2, 1.2, 1.0, 3.0], jnp.float32) * D ** (-0.5)
    return noise_draw * factors[:, None, None]


def draw_vec_master(key, part):
    key = jax.random.fold_in(key, 13)
    column_pos = jnp.arange(D, dtype=jnp.float32) / (D - 1) - 0.5
    rising = jnp.exp(math.log(3.0) * column_pos)
    noise_draw = jax.random.normal(key, (VROWS, D), jnp.float32)
    row_index = jnp.arange(VROWS)[:, None]
    gain_first = rising[None, :] * (1.0 + 0.1 * noise_draw)
    gain_second = 1.0 + 0.1 * noise_draw
    return jnp.where(row_index == 4, gain_first, jnp.where(row_index == 6, gain_second, 0.3 * noise_draw))


def levels(stream_key, shape, shards, smallest, top_value):
    def one(dim, parts):
        draws = jax.random.uniform(jax.random.fold_in(jax.random.fold_in(stream_key, 6), dim), (parts,), jnp.float32, smallest / len(shards), top_value / len(shards))
        return jnp.repeat(jnp.exp(draws), shape[dim] // parts).reshape((-1,) + (1,) * (len(shape) - dim - 1))

    loudness = one(*shards[0])
    for cut in shards[1:]:
        loudness = loudness * one(*cut)
    return loudness


def profile(count, total, limit, skew):
    portions = [(1 << 20) // math.isqrt(grade ** skew) + 1 for grade in range(2, count + 1)]
    surplus, counts = total - limit - (count - 1), [1] * (count - 1)
    while surplus > 0:
        free = [i for i in range(count - 1) if counts[i] < limit]
        mass, remaining = sum([portions[i] for i in free]), surplus
        for i in free:
            more = min(limit - counts[i], max(1, remaining * portions[i] // mass), surplus)
            counts[i] = counts[i] + more
            surplus = surplus - more
    return np.array([limit] + counts)


def ragged(stream_key, amount, total, limit, skew):
    if amount == 2:
        one = jax.random.randint(stream_key, (), max(1, total - limit), min(limit, total - 1) + 1)
        return jnp.stack([one, total - one])
    lengths = jnp.asarray(profile(amount, total, limit, skew), jnp.int32)
    couples = (amount - 1) // 2
    donor, receiver = lengths[1:1 + 2 * couples:2], lengths[2:2 + 2 * couples:2]
    slack = jnp.minimum(donor - 1, limit - receiver)
    moved = jax.random.randint(jax.random.fold_in(stream_key, 1), (couples,), 0, 1 << 20) % (slack + 1)
    lengths = lengths.at[1:1 + 2 * couples:2].set(donor - moved).at[2:2 + 2 * couples:2].set(receiver + moved)
    return lengths[jax.random.permutation(jax.random.fold_in(stream_key, 2), amount)]


def scatter_about(key, dims, width, reach, pieces=(), kind=jnp.bfloat16):
    factor_of = levels(key, dims, pieces, -0.22, 0.18) if pieces else 1.0
    entries = jax.random.normal(key, dims, jnp.float32) * width * factor_of
    return jnp.minimum(jnp.maximum(entries, -reach), reach).astype(kind)


def setup_inputs(seed: int = 0) -> dict:
    splits = jax.random.split(jax.random.key(seed), 13)
    return {
        "block_input": draw_block_input(jax.random.fold_in(splits[12], 71), 0),
        "cotangent": scatter_about(splits[1], (TOKENS, D), 1.0, 6.0, ((0, 128),)),
        "segment_ids": jax.vmap(lambda own: jnp.searchsorted(jnp.cumsum(ragged(own, SENTS, ROW, MOST, 1)), jnp.arange(ROW), side="right"))(jax.random.split(splits[2], N_DP)).reshape((N_DP, ROW)).astype(jnp.int32),
        "attn_master": draw_attn_master(jax.random.fold_in(splits[12], 71), 0),
        "up_master": scatter_about(splits[4], (D, FF), D ** -0.5, 0.25, ((0, 128),), jnp.float32),
        "down_master": scatter_about(splits[5], (FF, D), (FF // 4) ** -0.5, 0.25, ((0, 128),), jnp.float32),
        "vec_master": draw_vec_master(jax.random.fold_in(splits[12], 71), 0),
        "attn_moment": scatter_about(splits[7], (4, D, D), (NPARAM ** -0.5), 0.0078125, ((1, 128),), jnp.float32),
        "up_moment": scatter_about(splits[8], (D, FF), (NPARAM ** -0.5), 0.0078125, ((0, 128),), jnp.float32),
        "down_moment": scatter_about(splits[9], (FF, D), (NPARAM ** -0.5), 0.0078125, ((0, 128),), jnp.float32),
        "vec_moment": scatter_about(splits[10], (VROWS, D), (0.3 * NPARAM ** -0.5), 0.0024414062, ((1, 128),), jnp.float32),
        "vec_second": jnp.clip(jnp.exp(math.log(2.284356703796675e-08) - 2.7725887 * jax.random.uniform(splits[11], (VROWS, D), jnp.float32) ** levels(splits[11], (VROWS, D), ((1, 128),), -0.2, 0.2)), 1.4277229398729219e-09, 2.284356703796675e-08),
    }


@jax.custom_vjp
def low(v):
    return lax.optimization_barrier(v.astype(jnp.bfloat16)).astype(jnp.float32)

@jax.custom_vjp
def low_back(v):
    return v

def low_keep(v):
    return (low(v), None)

def low_pass(kept, grad):
    return (grad,)

def back_keep(v):
    return (v, None)

def back_low(kept, grad):
    return (low(grad),)
low.defvjp(low_keep, low_pass)
low_back.defvjp(back_keep, back_low)
HIGHEST = lax.Precision.HIGHEST
MASKED_SCORE = -1e+30
NORM_EPSILON = 1e-05
CLIP_LIMIT = 1.0
MOMENTUM_DECAY = 0.95
RATE_MATRIX = 0.5
DECAY_MATRIX = 0.01
BETA_FIRST = 0.9
BETA_SECOND = 0.999
RATE_VECTOR = 0.2
ADAM_EPSILON = 1e-08
NEWTON_FIRST = 3.4445
NEWTON_SECOND = -4.775
NEWTON_THIRD = 2.0315

def layer_norm(values):
    centred = values - lax.optimization_barrier(jnp.mean(values, axis=-1, keepdims=True))
    return centred * lax.rsqrt(lax.optimization_barrier(jnp.mean(centred * centred, axis=-1, keepdims=True)) + NORM_EPSILON)

def rounded(values):
    return low_back(low(values))

def matmul(left, right):
    return jnp.dot(left, right, precision=HIGHEST)

def split_heads(values):
    return values.reshape(values.shape[0], H, HD).transpose(1, 0, 2)

def forward_row(params, inputs):
    w_query, w_key, w_value, w_out, w_up, w_down, vectors = params
    tokens, segment = inputs
    queries = rounded(matmul(tokens, w_query) + vectors[0])
    keys_all = rounded(matmul(tokens, w_key))
    values_all = rounded(matmul(tokens, w_value) + vectors[1])
    scores = jnp.einsum('hqd,hkd->hqk', split_heads(queries), split_heads(keys_all), precision=HIGHEST)
    scores = low_back(scores * HD ** (-0.5))
    same_sentence = segment[:, None] == segment[None, :]
    scores = jnp.where(same_sentence[None], scores, MASKED_SCORE)
    top_score = lax.optimization_barrier(jnp.max(scores, axis=-1, keepdims=True))
    expo_scores = jnp.exp(scores - top_score)
    soft_weights = expo_scores / lax.optimization_barrier(jnp.sum(expo_scores, axis=-1, keepdims=True))
    attended = jnp.einsum('hqk,hkd->hqd', low(soft_weights), split_heads(values_all), precision=HIGHEST)
    attended = rounded(attended.transpose(1, 0, 2).reshape(ROW, D))
    branch = low_back(matmul(attended, w_out) + vectors[2])
    first = layer_norm(tokens + branch) * vectors[4] + vectors[5]
    inner = low_back(matmul(low(first), w_up) + vectors[8:].reshape(FF))
    activated = low(jax.nn.gelu(inner, approximate=True))
    feed = low_back(matmul(activated, w_down) + vectors[3])
    return layer_norm(feed + first + tokens) * vectors[6] + vectors[7]

def orthogonal(matrix):
    tall_shape = matrix.shape[0] > matrix.shape[1]
    work = matrix.T if tall_shape else matrix
    work = work / (jnp.sqrt(jnp.sum(work * work)) + 1e-07)
    for turn in range(NS_ITERS):
        gram = jnp.dot(work, work.T, precision=HIGHEST)
        poly = NEWTON_SECOND * gram + NEWTON_THIRD * jnp.dot(gram, gram, precision=HIGHEST)
        work = NEWTON_FIRST * work + jnp.dot(poly, work, precision=HIGHEST)
    return work.T if tall_shape else work

def muon_update(master, momentum):
    ratio = math.sqrt(max(1.0, momentum.shape[1] / momentum.shape[0]))
    return master * (1.0 - RATE_MATRIX * DECAY_MATRIX) - RATE_MATRIX * ratio * orthogonal(momentum)

def reference(block_input, cotangent, segment_ids, attn_master, up_master, down_master, vec_master, attn_moment, up_moment, down_moment, vec_moment, vec_second):

    def forward(attn_w, up_w, down_w, vectors, tokens):
        params = (low(attn_w[0]), low(attn_w[1]), low(attn_w[2]), low(attn_w[3]), low(up_w), low(down_w), low(vectors))

        def one_row(inputs):
            return jax.checkpoint(forward_row)(params, inputs)
        rows = tokens.reshape(N_DP, ROW, D)
        outputs = lax.map(one_row, (rows, segment_ids))
        return outputs.reshape(N_DP * ROW, D)
    inputs = block_input.astype(jnp.float32)
    outputs, pullback = jax.vjp(forward, attn_master, up_master, down_master, vec_master, inputs)
    grad_attn, grad_up, grad_down, grad_vec, grad_input = pullback(cotangent.astype(jnp.float32))
    total_squares = jnp.sum(grad_attn * grad_attn) + jnp.sum(grad_up * grad_up) + jnp.sum(grad_down * grad_down) + jnp.sum(grad_vec * grad_vec)
    clip_norm = jnp.sqrt(total_squares)
    factor = CLIP_LIMIT / jnp.maximum(clip_norm, CLIP_LIMIT)
    attn_momentum = MOMENTUM_DECAY * attn_moment + factor * grad_attn
    up_momentum = MOMENTUM_DECAY * up_moment + factor * grad_up
    down_momentum = MOMENTUM_DECAY * down_moment + factor * grad_down
    attn_new = jnp.stack([muon_update(attn_master[index], attn_momentum[index]) for index in range(4)])
    up_new = muon_update(up_master, up_momentum)
    down_new = muon_update(down_master, down_momentum)
    clipped = factor * grad_vec
    first_moment = BETA_FIRST * vec_moment + (1.0 - BETA_FIRST) * clipped
    second_moment = BETA_SECOND * vec_second + (1.0 - BETA_SECOND) * clipped * clipped
    first_hat = first_moment / (1.0 - BETA_FIRST ** STEP)
    second_hat = second_moment / (1.0 - BETA_SECOND ** STEP)
    vec_new = vec_master - RATE_VECTOR * first_hat / (jnp.sqrt(second_hat) + ADAM_EPSILON)
    return (outputs.astype(jnp.bfloat16), grad_input.astype(jnp.bfloat16), clip_norm, attn_momentum, up_momentum, down_momentum, attn_new, up_new, down_new, attn_new.astype(jnp.bfloat16), up_new.astype(jnp.bfloat16), down_new.astype(jnp.bfloat16), first_moment, second_moment, vec_new, vec_new.astype(jnp.bfloat16))
```

```python
import math

import jax
import jax.numpy as jnp
from jax import lax
from jax.experimental import pallas as pl
from jax.experimental.pallas import tpu as pltpu
from jax.sharding import Mesh, PartitionSpec as P

D = 512
FF = 2048
H = 8
HD = 64
ROW = 128
STEP = 10
NS_ITERS = 5
HALF = 256

MASKED_SCORE = -1e30
NORM_EPSILON = 1e-05
CLIP_LIMIT = 1.0
MOMENTUM_DECAY = 0.95
RATE_MATRIX = 0.5
DECAY_MATRIX = 0.01
BETA_FIRST = 0.9
BETA_SECOND = 0.999
RATE_VECTOR = 0.2
ADAM_EPSILON = 1e-08
NEWTON_FIRST = 3.4445
NEWTON_SECOND = -4.775
NEWTON_THIRD = 2.0315

CHIPS = ("x", "z", "y")
ALL = ("x", "z", "y", "c")
BF = jnp.bfloat16
F32 = jnp.float32
VMEM_LIMIT = 56 * 1024 * 1024


def call(kernel, outs, ins, scratch=(), smem=(), flops=0):
    spec = [
        pl.BlockSpec(memory_space=pltpu.SMEM if i in smem else pltpu.VMEM) for i in range(len(ins))
    ]
    shapes = [jax.ShapeDtypeStruct(s, t) for s, t in outs]
    moved = sum(math.prod(a.shape) * a.dtype.itemsize for a in list(ins) + shapes)
    return pl.pallas_call(
        kernel,
        out_shape=shapes,
        in_specs=spec,
        out_specs=[pl.BlockSpec(memory_space=pltpu.VMEM) for _ in shapes],
        scratch_shapes=list(scratch),
        compiler_params=pltpu.CompilerParams(vmem_limit_bytes=VMEM_LIMIT),
        cost_estimate=pl.CostEstimate(flops=flops, bytes_accessed=moved, transcendentals=0),
    )(*ins)


def dot(a, b):
    return jnp.dot(a, b, preferred_element_type=F32)


def dot_t(a, b):
    return lax.dot_general(a, b, (((1,), (1,)), ((), ())), preferred_element_type=F32)


def dot_in(a, b):
    return lax.dot_general(a, b, (((0,), (0,)), ((), ())), preferred_element_type=F32)


def attend_kernel(x, w, seg, q_out, k_out, v_out, p_out, o_out, vec_out):
    vec = w[:, 2048:2176].astype(F32).T[:16]
    vec_out[...] = vec
    tokens = x[...]
    q_out[...] = (dot(tokens, w[:, 0:512]) + vec[0:1]).astype(BF)
    k_out[...] = dot(tokens, w[:, 512:1024]).astype(BF)
    v_out[...] = (dot(tokens, w[:, 1024:1536]) + vec[1:2]).astype(BF)
    names = jnp.broadcast_to(seg[...].astype(F32), (ROW, ROW))
    same = names == names.T
    lane = lax.broadcasted_iota(jnp.int32, (ROW, ROW), 1)
    low = lane < HD
    parts = (low.astype(F32).astype(BF), (1.0 - low.astype(F32)).astype(BF))
    for pair in range(H // 2):
        cols = slice(128 * pair, 128 * pair + 128)
        q, k, v = q_out[:, cols], k_out[:, cols], v_out[:, cols]
        heads = []
        for h in range(2):
            scores = dot_t(q * parts[h], k) * (HD ** (-0.5))
            scores = jnp.where(same, scores, MASKED_SCORE)
            expo = jnp.exp(scores - jnp.max(scores, axis=-1, keepdims=True))
            soft = expo / jnp.sum(expo, axis=-1, keepdims=True)
            p_out[2 * pair + h] = soft
            heads.append(dot(soft.astype(BF), v))
        o_out[:, cols] = jnp.where(low, heads[0], heads[1]).astype(BF)


def norm_parts(values):
    centred = values - jnp.mean(values, axis=-1, keepdims=True)
    scale = lax.rsqrt(jnp.mean(centred * centred, axis=-1, keepdims=True) + NORM_EPSILON)
    return centred * scale, scale


def norm_back(grad, gain, normed, scale):
    grad = grad * gain
    return scale * (
        grad
        - jnp.mean(grad, axis=-1, keepdims=True)
        - normed * jnp.mean(grad * normed, axis=-1, keepdims=True)
    )


Z0, H0, O0, DF0, DU0, DA0, WIDE = 0, 2048, 2560, 3072, 3328, 4352, 4608


def middle_kernel(
    core, x, o, w, wu, wd, vec_in, cot, out, keep, send, do_out, base_out, vg, u_scr, gp_scr, df_scr, du_scr, da_scr
):
    c = core[0]
    vec = vec_in[...]
    tokens = x[...].astype(F32)
    residual = tokens + dot(o[...], w[:, 1536:2048]) + vec[2:3]
    normed1, scale1 = norm_parts(residual)
    first = normed1 * vec[4:5] + vec[5:6]
    first_low = first.astype(BF)
    keep[:, H0 : H0 + D] = first_low
    send[:, H0 : H0 + D] = first_low
    keep[:, O0 : O0 + D] = o[...]
    send[:, O0 : O0 + D] = o[...]
    root = math.sqrt(2.0 / math.pi)
    feed = jnp.zeros((ROW, D), F32)
    for part in range(4):
        cols = slice(512 * part, 512 * part + 512)
        u = dot(first_low, wu[:, cols]) + vec[8 + part : 9 + part]
        square = u * u
        tanh = jnp.tanh(root * (u + 0.044715 * (square * u)))
        half = 0.5 * (1.0 + tanh)
        act = (u * half).astype(BF)
        gp_scr[:, cols] = half + 0.5 * u * (1.0 - tanh * tanh) * (root * (1.0 + 3 * 0.044715 * square))
        keep[:, cols] = act
        send[:, cols] = act
        feed = feed + dot(act, wd[cols, :])
    residual2 = feed + vec[3:4] + first + tokens
    normed2, scale2 = norm_parts(residual2)
    out[...] = (normed2 * vec[6:7] + vec[7:8]).astype(BF)

    grad = cot[...].astype(F32)
    vg[6:7, :] = jnp.sum(grad * normed2, axis=0, keepdims=True)
    vg[7:8, :] = jnp.sum(grad, axis=0, keepdims=True)
    grad2 = norm_back(grad, vec[6:7], normed2, scale2)
    dfeed = grad2.astype(BF)
    df_scr[...] = dfeed
    vg[3:4, :] = jnp.sum(dfeed.astype(F32), axis=0, keepdims=True)
    dfirst = grad2
    for part in range(4):
        cols = slice(512 * part, 512 * part + 512)
        du = (dot_t(dfeed, wd[cols, :]) * gp_scr[:, cols]).astype(BF)
        du_scr[:, cols] = du
        vg[8 + part : 9 + part, :] = jnp.sum(du.astype(F32), axis=0, keepdims=True)
        dfirst = dfirst + dot_t(du, wu[:, cols])
    vg[4:5, :] = jnp.sum(dfirst * normed1, axis=0, keepdims=True)
    vg[5:6, :] = jnp.sum(dfirst, axis=0, keepdims=True)
    dres = norm_back(dfirst, vec[4:5], normed1, scale1)
    dbranch = dres.astype(BF)
    da_scr[...] = dbranch
    vg[2:3, :] = jnp.sum(dbranch.astype(F32), axis=0, keepdims=True)
    vg[0:2, :] = jnp.zeros((2, D), F32)
    vg[12:16, :] = jnp.zeros((4, D), F32)
    do_out[...] = dot_t(dbranch, w[:, 1536:2048]).astype(BF)
    base_out[...] = grad2 + dres
    mine = pl.multiple_of(c * HALF, HALF)
    theirs = pl.multiple_of((1 - c) * HALF, HALF)
    mine4 = pl.multiple_of(c * 1024, 1024)
    theirs4 = pl.multiple_of((1 - c) * 1024, 1024)
    keep[:, DF0:DU0] = df_scr[:, pl.ds(mine, HALF)]
    send[:, DF0:DU0] = df_scr[:, pl.ds(theirs, HALF)]
    keep[:, DU0:DA0] = du_scr[:, pl.ds(mine4, 1024)]
    send[:, DU0:DA0] = du_scr[:, pl.ds(theirs4, 1024)]
    keep[:, DA0:WIDE] = da_scr[:, pl.ds(mine, HALF)]
    send[:, DA0:WIDE] = da_scr[:, pl.ds(theirs, HALF)]


def weights_early_kernel(keep, got, out):
    def both(first, last):
        return jnp.concatenate([keep[:, first:last], got[:, first:last]], axis=0)

    out[:, 0:1024] = dot_in(both(H0, O0), both(DU0, DA0)).astype(BF)
    out[:, 1024:1280] = dot_in(both(O0, DF0), both(DA0, WIDE)).astype(BF)
    down = dot_in(both(Z0, H0), both(DF0, DU0)).reshape(64, 4, 8, HALF)
    for k in range(4):
        out[:, 1280 + HALF * k : 1280 + HALF * (k + 1)] = down[:, k].reshape(D, HALF).astype(BF)


def attend_back_kernel(
    core, q_in, k_in, v_in, p_in, do_in, base, w, vg_in, grad_out, keep, send, vg, dq_scr, dk_scr, dv_scr
):
    c = core[0]
    lane = lax.broadcasted_iota(jnp.int32, (ROW, ROW), 1)
    low = lane < HD
    parts = (low.astype(F32).astype(BF), (1.0 - low.astype(F32)).astype(BF))
    scale = HD ** (-0.5)
    for pair in range(H // 2):
        cols = slice(128 * pair, 128 * pair + 128)
        q, k, v, do = q_in[:, cols], k_in[:, cols], v_in[:, cols], do_in[:, cols]
        dqs, dks, dvs = [], [], []
        for h in range(2):
            soft = p_in[2 * pair + h]
            dsoft = dot_t(do * parts[h], v)
            ds = (soft * (dsoft - jnp.sum(soft * dsoft, axis=-1, keepdims=True))).astype(BF)
            dqs.append(dot(ds, k) * scale)
            dks.append(dot_in(ds, q) * scale)
            dvs.append(dot_in(soft.astype(BF), do))
        dq_scr[:, cols] = jnp.where(low, dqs[0], dqs[1]).astype(BF)
        dk_scr[:, cols] = jnp.where(low, dks[0], dks[1]).astype(BF)
        dv_scr[:, cols] = jnp.where(low, dvs[0], dvs[1]).astype(BF)
    vg[...] = vg_in[...]
    vg[0:1, :] = jnp.sum(dq_scr[...].astype(F32), axis=0, keepdims=True)
    vg[1:2, :] = jnp.sum(dv_scr[...].astype(F32), axis=0, keepdims=True)
    mine = pl.multiple_of(c * HALF, HALF)
    theirs = pl.multiple_of((1 - c) * HALF, HALF)
    for i, ref in enumerate((dq_scr, dk_scr, dv_scr)):
        keep[:, HALF * i : HALF * (i + 1)] = ref[:, pl.ds(mine, HALF)]
        send[:, HALF * i : HALF * (i + 1)] = ref[:, pl.ds(theirs, HALF)]
    total = (
        base[...]
        + dot_t(dq_scr[...], w[:, 0:512])
        + dot_t(dk_scr[...], w[:, 512:1024])
        + dot_t(dv_scr[...], w[:, 1024:1536])
    )
    grad_out[...] = total.astype(BF)


def weights_late_kernel(x, x_other, keep, got, vg, vg_other, out):
    tokens = jnp.concatenate([x[...], x_other[...]], axis=0)
    grads = jnp.concatenate([keep[...], got[...]], axis=0)
    out[:, 0:768] = dot_in(tokens, grads).astype(BF)
    vec = jnp.concatenate([vg[...] + vg_other[...], jnp.zeros((112, D), F32)], axis=0)
    out[:, 768:896] = vec.T.astype(BF)
    out[:, 896:1024] = jnp.zeros((D, 128), BF)


def add_up(ref, width):
    total = ref[0].astype(F32)
    for i in range(1, 64):
        total = total + ref[i].astype(F32)
    return total


def split3(value):
    one = value.astype(BF)
    rest = value - one.astype(F32)
    two = rest.astype(BF)
    three = (rest - two.astype(F32)).astype(BF)
    return one, two, three


def reduce_kernel(core, early, late, grads, pay):
    first = add_up(early, 2304)
    second = add_up(late, 1024)
    grads[:, 0:768] = second[:, 0:768]
    grads[:, 768:1024] = first[:, 1024:1280]
    grads[:, 1024:2048] = first[:, 0:1024]
    grads[:, 2048:3072] = first[:, 1280:2304]
    vec = second[:, 768:896]
    grads[:, 3072:3200] = vec
    square = jnp.sum(first * first) + jnp.sum(second[:, 0:768] * second[:, 0:768])
    square = square + jnp.where(core[0] == 0, 1.0, 0.0) * jnp.sum(vec * vec)
    row = lax.broadcasted_iota(jnp.int32, (8, 128), 0)
    lane = lax.broadcasted_iota(jnp.int32, (8, 128), 1)
    full = jnp.full((8, 128), square, F32)
    one, two, three = split3(full)
    note = jnp.where(lane == 0, one.astype(F32), jnp.where(lane == 1, two.astype(F32), three.astype(F32)))
    note = jnp.where((row == 0) & (lane < 3), note, 0.0).astype(BF)
    low = grads[:, 0:3072].astype(BF)
    rows = [
        jnp.concatenate([low[:, 0:512], jnp.zeros((8, 512), BF), note], axis=1),
        jnp.concatenate([low[:, 512:1024], jnp.zeros((8, 512), BF), note], axis=1),
        jnp.concatenate([low[:, 1024:2048], note], axis=1),
        jnp.concatenate([low[:, 2048:3072], note], axis=1),
    ]
    for i in range(64):
        pay[i] = rows[i % 4]


def halves(value):
    high = value.astype(BF)
    return high, (value - high.astype(F32)).astype(BF)


def fine(a, b, product=dot):
    ah, al = a
    bh, bl = b
    return product(ah, bh) + (product(ah, bl) + product(al, bh))


def newton_kernel(
    where, got, got_other, mom, mom_other, out, stats, m_high, m_low, gram, poly_high, poly_low, q_scr
):
    core, role, plane = where[0], where[1], where[2]
    note = jnp.sum(got[:, 1024:1152].astype(F32)) + jnp.sum(got_other[:, 1024:1152].astype(F32))
    clip = jnp.sqrt(note)
    factor = CLIP_LIMIT / jnp.maximum(clip, CLIP_LIMIT)
    row = lax.broadcasted_iota(jnp.int32, (8, 128), 0)
    stats[...] = jnp.where(row == 0, clip, factor)
    is_left = core == 0

    def chunk(first):
        cols = slice(first, first + HALF)
        mine = MOMENTUM_DECAY * mom[:, cols].astype(F32) + factor * got[:, cols].astype(F32)
        other = MOMENTUM_DECAY * mom_other[:, cols].astype(F32) + factor * got_other[:, cols].astype(F32)
        return jnp.where(is_left, mine, other), jnp.where(is_left, other, mine)

    def put(slot, value):
        high, low = halves(value)
        m_high[slot] = high
        m_low[slot] = low
        return jnp.sum(value * value)

    def gram_inner(blocks):
        for a, b in ((0, 0), (0, 1), (1, 1)):
            total = jnp.zeros((HALF, HALF), F32)
            for k in range(blocks):
                left = (m_high[2 * k + a], m_low[2 * k + a])
                right = (m_high[2 * k + b], m_low[2 * k + b])
                total = total + fine(left, right, dot_in)
            gram[HALF * a : HALF * (a + 1), HALF * b : HALF * (b + 1)] = total
            if a != b:
                gram[HALF * b : HALF * (b + 1), HALF * a : HALF * (a + 1)] = total.T

    def finish(square):
        size = jnp.sqrt(square) + 1e-07
        q_scr[0:8, 0:128] = jnp.full((8, 128), 1.0 / size, F32)
        gram[...] = gram[...] * (1.0 / (size * size))

    @pl.when(role < 2)
    def _():
        left0, right0 = chunk(0)
        left1, right1 = chunk(HALF)
        left = jnp.where(is_left, left0, left1)
        right = jnp.where(is_left, right0, right1)
        square = put(0, left) + put(1, right)
        gram_inner(1)
        finish(square)

    @pl.when(role == 2)
    def _():
        square = jnp.float32(0.0)
        for k in range(4):
            left, right = chunk(HALF * k)
            square = square + put(k, left) + put(4 + k, right)
        total = jnp.zeros((D, D), F32)
        for k in range(8):
            block = (m_high[k], m_low[k])
            total = total + fine(block, block, dot_t)
        gram[...] = total
        finish(square)

    @pl.when(role == 3)
    def _():
        square = jnp.float32(0.0)
        for k in range(4):
            left, right = chunk(HALF * k)
            square = square + put(2 * k, left) + put(2 * k + 1, right)
        gram_inner(4)
        finish(square)

    diagonal = (
        lax.broadcasted_iota(jnp.int32, (D, D), 0) == lax.broadcasted_iota(jnp.int32, (D, D), 1)
    )
    for turn in range(NS_ITERS):
        own = halves(gram[...])
        square = fine(own, own)
        poly = NEWTON_SECOND * gram[...] + NEWTON_THIRD * square
        poly = jnp.where(diagonal, poly + NEWTON_FIRST, poly)
        if turn < NS_ITERS - 1:
            poly = halves(poly)
            poly_high[turn] = poly[0]
            poly_low[turn] = poly[1]
            gram[...] = fine(poly, halves(fine(poly, own)))
        else:
            gram[...] = poly
            poly_high[turn], poly_low[turn] = halves(poly)

    inverse = q_scr[0:1, 0:1]

    def chain(rows):
        for turn in range(NS_ITERS):
            rows = fine(halves(rows), (poly_high[turn], poly_low[turn]))
        return rows

    chips = pl.ds(pl.multiple_of(plane * 32, 32), 32)

    def rows_of(slot):
        return m_high[slot, chips, :].astype(F32) + m_low[slot, chips, :].astype(F32)

    @pl.when(role < 2)
    def _():
        rows = jnp.concatenate([rows_of(0), rows_of(1)], axis=1) * inverse
        out[:, 0:512] = chain(rows).astype(BF)
        out[:, 512:1024] = jnp.zeros((32, 512), BF)

    @pl.when(role == 2)
    def _():
        rows = gram[chips, :]
        for turn in range(NS_ITERS - 1):
            rows = fine(halves(rows), (poly_high[turn], poly_low[turn]))
        rows = halves(rows * inverse)
        for k in range(4):
            slot = k + 4 * core
            out[:, HALF * k : HALF * (k + 1)] = fine(rows, (m_high[slot], m_low[slot])).astype(BF)

    @pl.when(role == 3)
    def _():
        blocks = [jnp.concatenate([rows_of(2 * k), rows_of(2 * k + 1)], axis=1) for k in range(4)]
        q_scr[...] = chain(jnp.concatenate(blocks, axis=0) * inverse)
        cols = pl.ds(pl.multiple_of(core * HALF, HALF), HALF)
        for k in range(4):
            out[:, HALF * k : HALF * (k + 1)] = q_scr[32 * k : 32 * (k + 1), cols].astype(BF)


def update_kernel(
    core, got, grads, grads_other, stats, attn, up, down, vec, attn_m, up_m, down_m, vec_m, vec_s,
    attn_mom, up_mom, down_mom, attn_new, up_new, down_new, attn_copy, up_copy, down_copy,
    vec_mom, vec_sec, vec_new, vec_copy,
):
    c = core[0]
    is_left = c == 0
    factor = stats[1:2, 0:1]
    keep_share = 1.0 - RATE_MATRIX * DECAY_MATRIX

    def rows4(value):
        return jnp.where(is_left, value[0:4], value[4:8])

    def both(first, last):
        mine, other = grads[:, first:last], grads_other[:, first:last]
        left = jnp.where(is_left, mine, other)
        right = jnp.where(is_left, other, mine)
        return left, right

    for m in range(4):
        left, right = both(HALF * m, HALF * (m + 1))
        grad = rows4(jnp.concatenate([left, right], axis=1))
        attn_mom[m] = MOMENTUM_DECAY * attn_m[m] + factor * grad
        new = attn[m] * keep_share - RATE_MATRIX * rows4(got[m, :, 0:512].astype(F32))
        attn_new[m] = new
        attn_copy[m] = new.astype(BF)
    left, right = both(1024, 2048)
    grad = rows4(jnp.concatenate([left, right], axis=1))
    up_mom[...] = MOMENTUM_DECAY * up_m[...] + factor * grad
    rate = RATE_MATRIX * math.sqrt(max(1.0, FF / D))
    step = rows4(jnp.concatenate([got[4].astype(F32), got[5].astype(F32)], axis=1))
    new = up[...] * keep_share - rate * step
    up_new[...] = new
    up_copy[...] = new.astype(BF)
    left, right = both(2048, 3072)
    rate = RATE_MATRIX * math.sqrt(max(1.0, D / FF))
    low_half, high_half = got[6].astype(F32), got[7].astype(F32)
    for k in range(2):
        def pick(value):
            one = value[:, HALF * k : HALF * (k + 1)]
            two = value[:, HALF * (k + 2) : HALF * (k + 3)]
            return jnp.where(is_left, one, two)

        rows = slice(8 * k, 8 * (k + 1))
        grad = jnp.concatenate([pick(left), pick(right)], axis=1)
        down_mom[rows, :] = MOMENTUM_DECAY * down_m[rows, :] + factor * grad
        step = jnp.concatenate([pick(low_half), pick(high_half)], axis=1)
        down_new[rows, :] = down[rows, :] * keep_share - rate * step
    down_copy[...] = down_new[...].astype(BF)
    turned = jnp.concatenate([grads[:, 3072:3200], jnp.zeros((120, 128), F32)], axis=0).T
    grad = jnp.where(is_left, turned[0:12, 0:4], turned[0:12, 4:8])
    clipped = factor * grad
    first = BETA_FIRST * vec_m[...] + (1.0 - BETA_FIRST) * clipped
    second = BETA_SECOND * vec_s[...] + (1.0 - BETA_SECOND) * clipped * clipped
    vec_mom[...] = first
    vec_sec[...] = second
    first_hat = first / (1.0 - BETA_FIRST**STEP)
    second_hat = second / (1.0 - BETA_SECOND**STEP)
    new = vec[...] - RATE_VECTOR * first_hat / (jnp.sqrt(second_hat) + ADAM_EPSILON)
    vec_new[...] = new
    vec_copy[...] = new.astype(BF)


def swap(value):
    return lax.ppermute(value, "c", [(0, 1), (1, 0)])


def to_chips(value):
    return lax.all_to_all(value, CHIPS, 0, 0, tiled=True)


def spread(shard):
    own = to_chips(jnp.broadcast_to(shard[None], (64,) + shard.shape))
    other = swap(own)
    left = lax.axis_index("c") == 0
    both = jnp.concatenate(
        [jnp.where(left, own, other), jnp.where(left, other, own)], axis=1
    )
    return both.reshape(-1, shard.shape[-1])


def body(
    block_input, cotangent, segment_ids, attn_master, up_master, down_master, vec_master,
    attn_moment, up_moment, down_moment, vec_moment, vec_second,
):
    c = lax.axis_index("c")
    y = lax.axis_index("y")
    plane = lax.axis_index("x") * 4 + lax.axis_index("z")
    core = c.reshape(1).astype(jnp.int32)

    attn_low = attn_master.astype(BF)
    shard = jnp.concatenate(
        [attn_low[m] for m in range(4)] + [jnp.pad(vec_master.T.astype(BF), ((0, 0), (0, 116)))], axis=1
    )
    w = spread(shard)
    wu = spread(up_master.astype(BF))
    wd = lax.all_gather(down_master.astype(BF), ALL, axis=0, tiled=True)

    def by_core(value, axis, size):
        return lax.dynamic_slice_in_dim(value, c * size, size, axis), lax.dynamic_slice_in_dim(
            value, (1 - c) * size, size, axis
        )

    pieces = [attn_moment[m].astype(BF) for m in range(4)]
    mine, theirs = [], []
    for piece in pieces:
        a, b = by_core(piece, 1, HALF)
        mine.append(a)
        theirs.append(b)
    a, b = by_core(up_moment.astype(BF), 1, 1024)
    mine.append(a)
    theirs.append(b)
    a, b = by_core(down_moment.astype(BF), 1, HALF)
    a, b = (t.reshape(2, 8, HALF) for t in (a, b))
    got_m = swap(jnp.concatenate(theirs, axis=1))
    got_d = swap(b)
    own_m = jnp.concatenate(mine, axis=1)
    left = c == 0
    eight = jnp.concatenate([jnp.where(left, own_m, got_m), jnp.where(left, got_m, own_m)], axis=0)
    first, second = jnp.where(left, a, got_d), jnp.where(left, got_d, a)
    down8 = jnp.concatenate([first[0], first[1], second[0], second[1]], axis=1)
    gap = jnp.zeros((8, 512), BF)
    roles = jnp.stack(
        [
            jnp.concatenate([eight[:, 0:512], gap], axis=1),
            jnp.concatenate([eight[:, 512:1024], gap], axis=1),
            eight[:, 1024:2048],
            down8,
        ]
    )
    mom = to_chips(jnp.broadcast_to(roles[None], (16, 4, 8, 1024)).reshape(64, 8, 1024))
    mom_other = swap(mom)

    q, k, v, soft, o, vec = call(
        attend_kernel,
        [((ROW, D), BF)] * 3 + [((H, ROW, ROW), F32), ((ROW, D), BF), ((16, D), F32)],
        [block_input, w, segment_ids],
        flops=3 * 2 * ROW * D * D,
    )
    x_other = swap(block_input)
    layer_out, keep, send, dout, base, vg = call(
        middle_kernel,
        [((ROW, D), BF), ((ROW, WIDE), BF), ((ROW, WIDE), BF), ((ROW, D), BF), ((ROW, D), F32), ((16, D), F32)],
        [core, block_input, o, w, wu, wd, vec, cotangent],
        scratch=[
            pltpu.VMEM((ROW, FF), F32),
            pltpu.VMEM((ROW, FF), F32),
            pltpu.VMEM((ROW, D), BF),
            pltpu.VMEM((ROW, FF), BF),
            pltpu.VMEM((ROW, D), BF),
        ],
        smem=(0,),
        flops=10 * 2 * ROW * D * D,
    )
    got = swap(send)
    (early,) = call(weights_early_kernel, [((D, 2304), BF)], [keep, got], flops=2 * 256 * 512 * 2304)
    early = to_chips(early.reshape(64, 8, 2304))
    input_grad, keep, send, vg = call(
        attend_back_kernel,
        [((ROW, D), BF), ((ROW, 768), BF), ((ROW, 768), BF), ((16, D), F32)],
        [core, q, k, v, soft, dout, base, w, vg],
        scratch=[pltpu.VMEM((ROW, D), BF)] * 3,
        smem=(0,),
        flops=6 * 2 * ROW * D * D,
    )
    got = swap(send)
    vg_other = swap(vg)
    (late,) = call(
        weights_late_kernel,
        [((D, 1024), BF)],
        [block_input, x_other, keep, got, vg, vg_other],
        flops=2 * 256 * 512 * 768,
    )
    late = to_chips(late.reshape(64, 8, 1024))
    grads, pay = call(
        reduce_kernel, [((8, 3200), F32), ((64, 8, 1152), BF)], [core, early, late], smem=(0,)
    )
    grads_other = swap(grads)
    pay = to_chips(pay)
    pay_other = swap(pay)
    flat = (D, 1152)
    where = jnp.stack([c, y, plane]).astype(jnp.int32)
    orth, stats = call(
        newton_kernel,
        [((32, 1024), BF), ((8, 128), F32)],
        [where, pay.reshape(flat), pay_other.reshape(flat), mom.reshape(D, 1024), mom_other.reshape(D, 1024)],
        scratch=[
            pltpu.VMEM((8, D, HALF), BF),
            pltpu.VMEM((8, D, HALF), BF),
            pltpu.VMEM((D, D), F32),
            pltpu.VMEM((NS_ITERS, D, D), BF),
            pltpu.VMEM((NS_ITERS, D, D), BF),
            pltpu.VMEM((128, D), F32),
        ],
        smem=(0,),
        flops=16 * 3 * 2 * D * D * D,
    )
    orth = jnp.broadcast_to(orth.reshape(4, 1, 8, 1024), (4, 2, 8, 1024)).reshape(8, 8, 1024)
    orth = lax.all_to_all(orth, ("y", "c"), 0, 0, tiled=True)
    outs = call(
        update_kernel,
        [((4, 4, D), F32), ((4, FF), F32), ((16, D), F32)] * 2
        + [((4, 4, D), BF), ((4, FF), BF), ((16, D), BF)]
        + [((12, 4), F32)] * 3
        + [((12, 4), BF)],
        [
            core, orth, grads, grads_other, stats, attn_master, up_master, down_master, vec_master,
            attn_moment, up_moment, down_moment, vec_moment, vec_second,
        ],
        smem=(0,),
    )
    clip_norm = stats[0, 0]
    return (layer_out, input_grad, clip_norm, *outs)


def solution(mesh):
    grid = Mesh(mesh.devices.reshape(4, 4, 4, 2), ("x", "z", "y", "c"))
    row, mat, vec = P(ALL, None), P(None, ALL, None), P(None, ALL)
    return jax.shard_map(
        body,
        mesh=grid,
        in_specs=(row, row, row, mat, row, row, vec, mat, row, row, vec, vec),
        out_specs=(row, row, P(), mat, row, row, mat, row, row, mat, row, row, vec, vec, vec, vec),
        check_vma=False,
    )
```

```python
import math

import jax
import jax.numpy as jnp
from jax import lax
from jax.experimental import pallas as pl
from jax.experimental.pallas import tpu as pltpu
from jax.sharding import Mesh, PartitionSpec as P

D = 512
FF = 2048
H = 8
HD = 64
ROW = 128
STEP = 10
NS_ITERS = 5
HALF = 256

MASKED_SCORE = -1e30
NORM_EPSILON = 1e-05
CLIP_LIMIT = 1.0
MOMENTUM_DECAY = 0.95
RATE_MATRIX = 0.5
DECAY_MATRIX = 0.01
BETA_FIRST = 0.9
BETA_SECOND = 0.999
RATE_VECTOR = 0.2
ADAM_EPSILON = 1e-08
NEWTON_FIRST = 3.4445
NEWTON_SECOND = -4.775
NEWTON_THIRD = 2.0315

CHIPS = ("x", "z", "y")
ALL = ("x", "z", "y", "c")
BF = jnp.bfloat16
F32 = jnp.float32
VMEM_LIMIT = 20 * 1024 * 1024


def call(kernel, outs, ins, scratch=(), smem=(), args=(), far=(), results=(), flops=0, limit=VMEM_LIMIT):
    spec = [
        pl.BlockSpec(memory_space=pltpu.SMEM if i in smem else pl.ANY if i in far else pltpu.VMEM)
        for i in range(len(ins))
    ]
    placed = [
        x if i in smem or i in args or i in far else pltpu.with_memory_space_constraint(x, pltpu.VMEM)
        for i, x in enumerate(ins)
    ]
    shapes = [
        jax.ShapeDtypeStruct(s, t) if i in results else pltpu.VMEM(s, t) for i, (s, t) in enumerate(outs)
    ]
    moved = sum(math.prod(a.shape) * a.dtype.itemsize for a in ins)
    return pl.pallas_call(
        kernel,
        out_shape=shapes,
        in_specs=spec,
        out_specs=[pl.BlockSpec(memory_space=pltpu.VMEM) for _ in shapes],
        scratch_shapes=list(scratch),
        compiler_params=pltpu.CompilerParams(vmem_limit_bytes=limit),
        cost_estimate=pl.CostEstimate(flops=flops, bytes_accessed=moved, transcendentals=0),
    )(*placed)


def dot(a, b):
    return jnp.dot(a, b, preferred_element_type=F32)


def dot_t(a, b):
    return lax.dot_general(a, b, (((1,), (1,)), ((), ())), preferred_element_type=F32)


def dot_in(a, b):
    return lax.dot_general(a, b, (((0,), (0,)), ((), ())), preferred_element_type=F32)


O_LANE, UP_LANE, DOWN_LANE, VEC_LANE, BLOCK = 768, 1024, 2048, 3072, 3200
Z0, H0, O0, X0, WIDE = 0, 2048, 2560, 3072, 3584


def half_lanes(half, size):
    return pl.ds(pl.multiple_of(half * size, size), size)


def regroup():
    source = lax.broadcasted_iota(jnp.int32, (D, D), 0)
    target = lax.broadcasted_iota(jnp.int32, (D, D), 1)
    return jnp.where(target == (source & 3) * 128 + (source >> 2), 1.0, 0.0).astype(BF)


def pack_kernel(
    core, attn, up, down, vec, attn_m, up_m, down_m, keep, send,
    attn_v, up_v, down_v, vec_v, attn_mv, up_mv, down_mv, full, sems,
):
    c = core[0]
    copies = [
        pltpu.make_async_copy(source, target, sems.at[i])
        for i, (source, target) in enumerate(
            [(attn, attn_v), (up, up_v), (down, down_v), (vec, vec_v), (attn_m, attn_mv), (up_m, up_mv), (down_m, down_mv)]
        )
    ]
    for copy in copies:
        copy.start()
    move = regroup()
    for copy in copies:
        copy.wait()
    for first, attn_one, up_one, down_one in ((0, attn_v, up_v, down_v), (4, attn_mv, up_mv, down_mv)):
        rows = slice(first, first + 4)
        for m in range(4):
            full[rows, D * m : D * (m + 1)] = attn_one[m]
        for part in range(4):
            moved = dot(up_one[:, D * part : D * (part + 1)].astype(BF), move)
            for q in range(4):
                lane = FF + D * q + 128 * part
                full[rows, lane : lane + 128] = moved[:, 128 * q : 128 * (q + 1)]
        for i in range(4):
            for q in range(4):
                lane = 2 * FF + D * q
                full[first + i : first + i + 1, lane : lane + D] = down_one[4 * i + q : 4 * i + q + 1, :]
    for target, half in ((keep, c), (send, 1 - c)):
        for m in range(4):
            lanes = pl.ds(pl.multiple_of(D * m + HALF * half, HALF), HALF)
            target[:, HALF * m : HALF * (m + 1)] = full[:, lanes].astype(BF)
        lanes = pl.ds(pl.multiple_of(FF + 1024 * half, 1024), 1024)
        target[:, UP_LANE:DOWN_LANE] = full[:, lanes].astype(BF)
        for q in range(4):
            lanes = pl.ds(pl.multiple_of(2 * FF + D * q + HALF * half, HALF), HALF)
            lane = DOWN_LANE + HALF * q
            target[:, lane : lane + HALF] = full[:, lanes].astype(BF)
    full[:, 0:128] = jnp.zeros((8, 128), F32)
    full[0:4, 0:12] = vec_v[...]
    keep[:, VEC_LANE:BLOCK] = full[:, 0:128].astype(BF)
    send[:, VEC_LANE:BLOCK] = full[:, 0:128].astype(BF)


def role_lanes(block, note):
    gap = jnp.zeros((8, 512), block.dtype)
    tail = [] if note is None else [note]
    return [
        jnp.concatenate([block[:, 0:512], gap] + tail, axis=1),
        jnp.concatenate([block[:, 512:1024], gap] + tail, axis=1),
        jnp.concatenate([block[:, UP_LANE:DOWN_LANE]] + tail, axis=1),
        jnp.concatenate([block[:, DOWN_LANE:VEC_LANE]] + tail, axis=1),
    ]


def spread_kernel(core, keep, got, message, message_mom):
    mine, other = keep[...].astype(F32), got[...].astype(F32)
    is_left = core[0] == 0
    left, right = jnp.where(is_left, mine, other), jnp.where(is_left, other, mine)
    block = jnp.concatenate([left[0:4], right[0:4]], axis=0).astype(BF)
    moms = role_lanes(jnp.concatenate([left[4:8], right[4:8]], axis=0).astype(BF), None)
    for i in range(64):
        message[i] = block
        message_mom[i] = moms[i % 4]


def low_lanes():
    return lax.broadcasted_iota(jnp.int32, (ROW, ROW), 1) < HD


def norm_parts(values):
    centred = values - jnp.mean(values, axis=-1, keepdims=True)
    scale = lax.rsqrt(jnp.mean(centred * centred, axis=-1, keepdims=True) + NORM_EPSILON)
    return centred * scale, scale


def norm_back(grad, gain, normed, scale):
    grad = grad * gain
    return scale * (
        grad
        - jnp.mean(grad, axis=-1, keepdims=True)
        - normed * jnp.mean(grad * normed, axis=-1, keepdims=True)
    )


def forward_kernel(
    core, x, w_own, w_other, seg, q_out, k_out, v_out, p_out, vec_out, acts, first_out, norm_out, scale_out, slope, wide
):
    c = core[0]
    sides = ((c, w_own), (1 - c, w_other))
    vec = w_own[:, VEC_LANE:BLOCK].astype(F32).T[:16]
    vec_out[...] = vec
    moved = dot(vec[8:16].astype(BF), regroup())
    for part in range(4):
        for q in range(4):
            vec_out[8 + q : 9 + q, 128 * part : 128 * (part + 1)] = moved[part : part + 1, 128 * q : 128 * (q + 1)]
    tokens = x[...]
    acts[:, X0:WIDE] = tokens
    for i, target in enumerate((q_out, k_out, v_out)):
        for half, w in sides:
            wide[:, half_lanes(half, HALF)] = dot(tokens, w[:, HALF * i : HALF * (i + 1)])
        bias = (vec[0:1], 0.0, vec[1:2])[i]
        target[...] = (wide[...] + bias).astype(BF)
    names = jnp.broadcast_to(seg[...].astype(F32), (ROW, ROW))
    same = names == names.T
    low = low_lanes()
    parts = (low.astype(F32).astype(BF), (1.0 - low.astype(F32)).astype(BF))
    for pair in range(H // 2):
        cols = slice(128 * pair, 128 * pair + 128)
        q, k, v = q_out[:, cols], k_out[:, cols], v_out[:, cols]
        heads = []
        for h in range(2):
            scores = dot_t(q * parts[h], k) * (HD ** (-0.5))
            scores = jnp.where(same, scores, MASKED_SCORE)
            expo = jnp.exp(scores - jnp.max(scores, axis=-1, keepdims=True))
            soft = expo / jnp.sum(expo, axis=-1, keepdims=True)
            p_out[2 * pair + h] = soft
            heads.append(dot(soft.astype(BF), v))
        acts[:, O0 + 128 * pair : O0 + 128 * pair + 128] = jnp.where(low, heads[0], heads[1]).astype(BF)
    for half, w in sides:
        wide[:, half_lanes(half, HALF)] = dot(acts[:, O0:X0], w[:, O_LANE:UP_LANE])
    normed, scale = norm_parts(tokens.astype(F32) + wide[...] + vec[2:3])
    norm_out[...] = normed
    scale_out[...] = scale
    first = normed * vec[4:5] + vec[5:6]
    first_out[...] = first
    first_low = first.astype(BF)
    acts[:, H0:O0] = first_low
    root = math.sqrt(2.0 / math.pi)
    for half, w in sides:
        for k in range(2):
            bias = vec_out[pl.ds(8 + 2 * half + k, 1), :]
            u = dot(first_low, w[:, UP_LANE + D * k : UP_LANE + D * (k + 1)]) + bias
            square = u * u
            tanh = jnp.tanh(root * (u + 0.044715 * (square * u)))
            gate = 0.5 * (1.0 + tanh)
            cols = pl.ds(pl.multiple_of(1024 * half + D * k, D), D)
            slope[:, cols] = gate + 0.5 * u * (1.0 - tanh * tanh) * (root * (1.0 + 3 * 0.044715 * square))
            acts[:, cols] = (u * gate).astype(BF)


DU0, DF0, GRADS = 1024, 2048, 2304


def backward_kernel(
    core, acts, first, vec_in, w_own, w_other, cot, slope, normed_in, scale_in, q_in, k_in, v_in, p_in,
    out, grad_out, keep, send, vg, wide, du_scr, df_scr, da_scr, do_scr, dq_scr, dk_scr, dv_scr,
):
    c = core[0]
    sides = ((c, w_own), (1 - c, w_other))
    vec = vec_in[...]
    for half, w in sides:
        feed = dot(acts[:, 0:D], w[:, DOWN_LANE : DOWN_LANE + HALF])
        for q in range(1, 4):
            lane = DOWN_LANE + HALF * q
            feed = feed + dot(acts[:, D * q : D * (q + 1)], w[:, lane : lane + HALF])
        wide[:, half_lanes(half, HALF)] = feed
    residual = wide[...] + vec[3:4] + first[...] + acts[:, X0:WIDE].astype(F32)
    normed, scale = norm_parts(residual)
    out[...] = (normed * vec[6:7] + vec[7:8]).astype(BF)
    grad = cot[...].astype(F32)
    vg[...] = jnp.zeros((16, D), F32)
    vg[6:7, :] = jnp.sum(grad * normed, axis=0, keepdims=True)
    vg[7:8, :] = jnp.sum(grad, axis=0, keepdims=True)
    grad2 = norm_back(grad, vec[6:7], normed, scale)
    df_scr[...] = grad2.astype(BF)
    vg[3:4, :] = jnp.sum(df_scr[...].astype(F32), axis=0, keepdims=True)
    for q in range(4):
        lane = DOWN_LANE + HALF * q
        dz = dot_t(df_scr[:, half_lanes(c, HALF)], w_own[:, lane : lane + HALF])
        dz = dz + dot_t(df_scr[:, half_lanes(1 - c, HALF)], w_other[:, lane : lane + HALF])
        du = (dz * slope[:, D * q : D * (q + 1)]).astype(BF)
        du_scr[:, D * q : D * (q + 1)] = du
        vg[8 + q : 9 + q, :] = jnp.sum(du.astype(F32), axis=0, keepdims=True)
    dfirst = grad2
    for half, w in sides:
        dfirst = dfirst + dot_t(du_scr[:, half_lanes(half, 1024)], w[:, UP_LANE:DOWN_LANE])
    normed1 = normed_in[...]
    vg[4:5, :] = jnp.sum(dfirst * normed1, axis=0, keepdims=True)
    vg[5:6, :] = jnp.sum(dfirst, axis=0, keepdims=True)
    dres = norm_back(dfirst, vec[4:5], normed1, scale_in[...])
    da_scr[...] = dres.astype(BF)
    vg[2:3, :] = jnp.sum(da_scr[...].astype(F32), axis=0, keepdims=True)
    dattended = jnp.zeros((ROW, D), F32)
    for half, w in sides:
        dattended = dattended + dot_t(da_scr[:, half_lanes(half, HALF)], w[:, O_LANE:UP_LANE])
    do_scr[...] = dattended.astype(BF)
    low = low_lanes()
    parts = (low.astype(F32).astype(BF), (1.0 - low.astype(F32)).astype(BF))
    share = HD ** (-0.5)
    for pair in range(H // 2):
        cols = slice(128 * pair, 128 * pair + 128)
        q, k, v, do = q_in[:, cols], k_in[:, cols], v_in[:, cols], do_scr[:, cols]
        dqs, dks, dvs = [], [], []
        for h in range(2):
            soft = p_in[2 * pair + h]
            dsoft = dot_t(do * parts[h], v)
            ds = (soft * (dsoft - jnp.sum(soft * dsoft, axis=-1, keepdims=True))).astype(BF)
            dqs.append(dot(ds, k) * share)
            dks.append(dot_in(ds, q) * share)
            dvs.append(dot_in(soft.astype(BF), do))
        dq_scr[:, cols] = jnp.where(low, dqs[0], dqs[1]).astype(BF)
        dk_scr[:, cols] = jnp.where(low, dks[0], dks[1]).astype(BF)
        dv_scr[:, cols] = jnp.where(low, dvs[0], dvs[1]).astype(BF)
    vg[0:1, :] = jnp.sum(dq_scr[...].astype(F32), axis=0, keepdims=True)
    vg[1:2, :] = jnp.sum(dv_scr[...].astype(F32), axis=0, keepdims=True)
    for target, half in ((keep, c), (send, 1 - c)):
        for i, ref in enumerate((dq_scr, dk_scr, dv_scr, da_scr)):
            target[:, HALF * i : HALF * (i + 1)] = ref[:, half_lanes(half, HALF)]
        target[:, DU0:DF0] = du_scr[:, half_lanes(half, 1024)]
        target[:, DF0:GRADS] = df_scr[:, half_lanes(half, HALF)]
    total = grad2 + dres
    for half, w in sides:
        for i, ref in enumerate((dq_scr, dk_scr, dv_scr)):
            total = total + dot_t(ref[:, half_lanes(half, HALF)], w[:, HALF * i : HALF * (i + 1)])
    grad_out[...] = total.astype(BF)


def weights_kernel(acts, acts_other, keep, got, vg, vg_other, out, vec):
    def both(one, two, first, last):
        return jnp.concatenate([one[:, first:last], two[:, first:last]], axis=0)

    out[:, 0:O_LANE] = dot_in(both(acts, acts_other, X0, WIDE), both(keep, got, 0, O_LANE)).astype(BF)
    out[:, O_LANE:UP_LANE] = dot_in(both(acts, acts_other, O0, X0), both(keep, got, O_LANE, DU0)).astype(BF)
    out[:, UP_LANE:DOWN_LANE] = dot_in(both(acts, acts_other, H0, O0), both(keep, got, DU0, DF0)).astype(BF)
    down = both(keep, got, DF0, GRADS)
    for q in range(4):
        lane = DOWN_LANE + HALF * q
        out[:, lane : lane + HALF] = dot_in(both(acts, acts_other, D * q, D * (q + 1)), down).astype(BF)
    total = vg[...] + vg_other[...]
    vec[...] = jnp.zeros((128, D), F32)
    vec[0:8, :] = total[0:8]
    for part in range(4):
        for q in range(4):
            vec[8 + part : 9 + part, 128 * q : 128 * (q + 1)] = total[8 + q : 9 + q, 128 * part : 128 * (part + 1)]
    vec[8:16, :] = dot_t(vec[8:16, :].astype(BF), regroup())
    out[:, VEC_LANE:BLOCK] = vec[...].T.astype(BF)


def add_up(ref):
    total = ref[0].astype(F32)
    for i in range(1, 64):
        total = total + ref[i].astype(F32)
    return total


def split3(value):
    one = value.astype(BF)
    rest = value - one.astype(F32)
    two = rest.astype(BF)
    three = (rest - two.astype(F32)).astype(BF)
    return one, two, three


def reduce_kernel(core, got, grads, pay):
    grads[...] = add_up(got)
    vec = grads[:, VEC_LANE:BLOCK]
    square = jnp.sum(grads[:, 0:VEC_LANE] * grads[:, 0:VEC_LANE])
    square = square + jnp.where(core[0] == 0, 1.0, 0.0) * jnp.sum(vec * vec)
    row = lax.broadcasted_iota(jnp.int32, (8, 128), 0)
    lane = lax.broadcasted_iota(jnp.int32, (8, 128), 1)
    full = jnp.full((8, 128), square, F32)
    one, two, three = split3(full)
    note = jnp.where(lane == 0, one.astype(F32), jnp.where(lane == 1, two.astype(F32), three.astype(F32)))
    note = jnp.where((row == 0) & (lane < 3), note, 0.0).astype(BF)
    rows = role_lanes(grads[:, 0:VEC_LANE].astype(BF), note)
    for i in range(64):
        pay[i] = rows[i % 4]


def halves(value):
    high = value.astype(BF)
    return high, (value - high.astype(F32)).astype(BF)


def fine(a, b):
    ah, al = a
    bh, bl = b
    return dot(jnp.concatenate([ah, ah, al], axis=1), jnp.concatenate([bh, bl, bh], axis=0))


def newton_kernel(
    where, got, got_other, mom, mom_other, out, clip_out, factor_out, m_low, gram, rows_scr
):
    core, role, plane = where[0], where[1], where[2]
    note = jnp.sum(got[:, 1024:1152].astype(F32)) + jnp.sum(got_other[:, 1024:1152].astype(F32))
    clip = jnp.sqrt(jnp.full((8, 128), note, F32))
    factors = CLIP_LIMIT / jnp.maximum(clip, CLIP_LIMIT)
    clip_out[...] = clip[0:1, 0:1]
    factor_out[...] = factors
    factor = factors[0:1, 0:1]
    is_left = core == 0
    chips = pl.ds(pl.multiple_of(plane * 32, 32), 32)

    def chunk(first):
        cols = slice(first, first + HALF)
        mine = MOMENTUM_DECAY * mom[:, cols].astype(F32) + factor * got[:, cols].astype(F32)
        other = MOMENTUM_DECAY * mom_other[:, cols].astype(F32) + factor * got_other[:, cols].astype(F32)
        return jnp.where(is_left, mine, other), jnp.where(is_left, other, mine)

    def put(slot, value):
        value = value.astype(BF)
        m_low[slot] = value
        value = value.astype(F32)
        return jnp.sum(value * value)

    def gram_inner(blocks):
        for a, b in ((0, 0), (0, 1), (1, 1)):
            total = dot_in(m_low[a], m_low[b])
            for k in range(1, blocks):
                total = total + dot_in(m_low[2 * k + a], m_low[2 * k + b])
            gram[HALF * a : HALF * (a + 1), HALF * b : HALF * (b + 1)] = total
            if a != b:
                gram[HALF * b : HALF * (b + 1), HALF * a : HALF * (a + 1)] = total.T

    def scaled(square):
        size = jnp.sqrt(jnp.full((8, 128), square, F32)) + 1e-07
        inverse = (1.0 / size)[0:1, 0:1]
        gram[...] = gram[...] * (inverse * inverse)
        return inverse

    def rows_of(slot):
        return m_low[slot, chips, :].astype(F32)

    @pl.when(role < 2)
    def _():
        left0, right0 = chunk(0)
        left1, right1 = chunk(HALF)
        square = put(0, jnp.where(is_left, left0, left1)) + put(1, jnp.where(is_left, right0, right1))
        gram_inner(1)
        inverse = scaled(square)
        rows_scr[0:32, :] = jnp.concatenate([rows_of(0), rows_of(1)], axis=1) * inverse

    @pl.when(role == 2)
    def _():
        square = jnp.float32(0.0)
        for k in range(4):
            left, right = chunk(HALF * k)
            square = square + put(k, left) + put(4 + k, right)
        total = dot_t(m_low[0], m_low[0])
        for k in range(1, 8):
            total = total + dot_t(m_low[k], m_low[k])
        gram[...] = total
        inverse = scaled(square)
        here = lax.broadcasted_iota(jnp.int32, (32, D), 0) + 32 * plane
        there = lax.broadcasted_iota(jnp.int32, (32, D), 1)
        rows_scr[0:32, :] = jnp.where(here == there, 1.0, 0.0) * inverse

    @pl.when(role == 3)
    def _():
        square = jnp.float32(0.0)
        for k in range(4):
            left, right = chunk(HALF * k)
            square = square + put(2 * k, left) + put(2 * k + 1, right)
        gram_inner(4)
        inverse = scaled(square)
        for k in range(4):
            rows = jnp.concatenate([rows_of(2 * k), rows_of(2 * k + 1)], axis=1)
            rows_scr[32 * k : 32 * (k + 1), :] = rows * inverse

    diagonal = (
        lax.broadcasted_iota(jnp.int32, (D, D), 0) == lax.broadcasted_iota(jnp.int32, (D, D), 1)
    )

    def turn(_, carry):
        own = halves(gram[...])
        poly = NEWTON_SECOND * gram[...] + NEWTON_THIRD * fine(own, own)
        poly = halves(jnp.where(diagonal, poly + NEWTON_FIRST, poly))
        next_gram = halves(fine(poly, own))

        @pl.when(role < 3)
        def _():
            rows = halves(rows_scr[0:32, :])
            both = tuple(jnp.concatenate(pair, axis=0) for pair in zip(next_gram, rows))
            both = fine(both, poly)
            gram[...] = both[0:D]
            rows_scr[0:32, :] = both[D:]

        @pl.when(role == 3)
        def _():
            rows = halves(rows_scr[...])
            both = tuple(jnp.concatenate(pair, axis=0) for pair in zip(next_gram, rows))
            both = fine(both, poly)
            gram[...] = both[0:D]
            rows_scr[...] = both[D:]

        return carry

    lax.fori_loop(0, NS_ITERS - 1, turn, 0)

    def last(count):
        own = halves(gram[...])
        rows = rows_scr[0:count, :]
        once = fine(halves(rows), own)
        twice = fine(halves(once), own)
        rows_scr[0:count, :] = NEWTON_FIRST * rows + NEWTON_SECOND * once + NEWTON_THIRD * twice

    @pl.when(role < 3)
    def _():
        last(32)

    @pl.when(role == 3)
    def _():
        last(128)

    def send(cols, value):
        value = value.reshape(4, 8, value.shape[1])
        out[:, 0, :, cols] = value
        out[:, 1, :, cols] = value

    @pl.when(role < 2)
    def _():
        send(slice(0, 512), rows_scr[0:32, :].astype(BF))
        send(slice(512, 1024), jnp.zeros((32, 512), BF))

    @pl.when(role == 2)
    def _():
        rows = halves(rows_scr[0:32, :])
        for k in range(4):
            value = m_low[k + 4 * core]
            send(slice(HALF * k, HALF * (k + 1)), (dot(rows[0], value) + dot(rows[1], value)).astype(BF))

    @pl.when(role == 3)
    def _():
        cols = pl.ds(pl.multiple_of(core * HALF, HALF), HALF)
        for k in range(4):
            send(slice(HALF * k, HALF * (k + 1)), rows_scr[32 * k : 32 * (k + 1), cols].astype(BF))


def update_kernel(
    core, got, grads, grads_other, factors, attn, up, down, vec, attn_m, up_m, down_m, vec_m, vec_s,
    attn_mom, up_mom, down_mom, attn_new, up_new, down_new, attn_copy, up_copy, down_copy,
    vec_mom, vec_sec, vec_new, vec_copy, ups, downs,
):
    c = core[0]
    is_left = c == 0
    factor = factors[0:1, 0:1]
    keep_share = 1.0 - RATE_MATRIX * DECAY_MATRIX

    def rows4(value):
        return jnp.where(is_left, value[0:4], value[4:8])

    def both(first, last):
        mine, other = grads[:, first:last], grads_other[:, first:last]
        left = jnp.where(is_left, mine, other)
        right = jnp.where(is_left, other, mine)
        return left, right

    for m in range(4):
        left, right = both(HALF * m, HALF * (m + 1))
        grad = rows4(jnp.concatenate([left, right], axis=1))
        attn_mom[m] = MOMENTUM_DECAY * attn_m[m] + factor * grad
        new = attn[m] * keep_share - RATE_MATRIX * rows4(got[m, :, 0:512].astype(F32))
        attn_new[m] = new
        attn_copy[m] = new.astype(BF)
    move = regroup()
    left, right = both(UP_LANE, DOWN_LANE)
    high, low = halves(rows4(jnp.concatenate([left, right], axis=1)))
    ups[0:4, :] = high.astype(F32)
    ups[4:8, :] = low.astype(F32)
    ups[8:12, :] = rows4(jnp.concatenate([got[4].astype(F32), got[5].astype(F32)], axis=1))
    ups[12:16, :] = jnp.zeros((4, FF), F32)
    rate = RATE_MATRIX * math.sqrt(max(1.0, FF / D))
    for part in range(4):
        pieces = [ups[:, D * q + 128 * part : D * q + 128 * (part + 1)] for q in range(4)]
        moved = dot_t(jnp.concatenate(pieces, axis=1).astype(BF), move)
        cols = slice(D * part, D * (part + 1))
        up_mom[:, cols] = MOMENTUM_DECAY * up_m[:, cols] + factor * (moved[0:4] + moved[4:8])
        up_new[:, cols] = up[:, cols] * keep_share - rate * moved[8:12]
    up_copy[...] = up_new[...].astype(BF)
    left, right = both(DOWN_LANE, VEC_LANE)
    left_step, right_step = got[6].astype(F32), got[7].astype(F32)
    for q in range(4):
        cols = slice(HALF * q, HALF * (q + 1))
        grad = rows4(jnp.concatenate([left[:, cols], right[:, cols]], axis=1))
        step = rows4(jnp.concatenate([left_step[:, cols], right_step[:, cols]], axis=1))
        for i in range(4):
            downs[0, 4 * i + q : 4 * i + q + 1, :] = grad[i : i + 1]
            downs[1, 4 * i + q : 4 * i + q + 1, :] = step[i : i + 1]
    down_mom[...] = MOMENTUM_DECAY * down_m[...] + factor * downs[0]
    rate = RATE_MATRIX * math.sqrt(max(1.0, D / FF))
    down_new[...] = down[...] * keep_share - rate * downs[1]
    down_copy[...] = down_new[...].astype(BF)
    grad = rows4(grads[:, VEC_LANE:BLOCK])[:, 0:12]
    clipped = factor * grad
    first = BETA_FIRST * vec_m[...] + (1.0 - BETA_FIRST) * clipped
    second = BETA_SECOND * vec_s[...] + (1.0 - BETA_SECOND) * clipped * clipped
    vec_mom[...] = first
    vec_sec[...] = second
    first_hat = first / (1.0 - BETA_FIRST**STEP)
    second_hat = second / (1.0 - BETA_SECOND**STEP)
    new = vec[...] - RATE_VECTOR * first_hat / (jnp.sqrt(second_hat) + ADAM_EPSILON)
    vec_new[...] = new
    vec_copy[...] = new.astype(BF)


def swap(value):
    return lax.ppermute(value, "c", [(0, 1), (1, 0)])


def to_chips(value):
    return lax.all_to_all(value, CHIPS, 0, 0, tiled=True)


def body(
    block_input, cotangent, segment_ids, attn_master, up_master, down_master, vec_master,
    attn_moment, up_moment, down_moment, vec_moment, vec_second,
):
    c = lax.axis_index("c")
    y = lax.axis_index("y")
    plane = lax.axis_index("x") * 4 + lax.axis_index("z")
    core = c.reshape(1).astype(jnp.int32)

    keep, send = call(
        pack_kernel,
        [((8, BLOCK), BF)] * 2,
        [core, attn_master, up_master, down_master, vec_master.T, attn_moment, up_moment, down_moment],
        scratch=[
            pltpu.VMEM((4, 4, D), F32), pltpu.VMEM((4, FF), F32), pltpu.VMEM((16, D), F32), pltpu.VMEM((4, 12), F32),
            pltpu.VMEM((4, 4, D), F32), pltpu.VMEM((4, FF), F32), pltpu.VMEM((16, D), F32),
            pltpu.VMEM((8, 3 * FF), F32), pltpu.SemaphoreType.DMA((7,)),
        ],
        smem=(0,),
        far=range(1, 8),
    )
    message, message_mom = call(
        spread_kernel, [((64, 8, BLOCK), BF), ((64, 8, 1024), BF)], [core, keep, swap(send)], smem=(0,)
    )
    own = to_chips(message)
    own, message_mom = lax.optimization_barrier((own, message_mom))
    other = swap(own)
    mom = to_chips(message_mom).reshape(D, 1024)
    own, other = own.reshape(D, BLOCK), other.reshape(D, BLOCK)
    q, k, v, soft, vec, acts, first, normed, scale, slope = call(
        forward_kernel,
        [((ROW, D), BF)] * 3
        + [((H, ROW, ROW), F32), ((16, D), F32), ((ROW, WIDE), BF), ((ROW, D), F32), ((ROW, D), F32)]
        + [((ROW, 1), F32), ((ROW, FF), F32)],
        [core, block_input, own, other, segment_ids],
        scratch=[pltpu.VMEM((ROW, D), F32)],
        smem=(0,),
        args=(1, 4),
        flops=8 * 2 * ROW * D * D,
    )
    acts_other = swap(acts)
    layer_out, input_grad, keep, send, vg = call(
        backward_kernel,
        [((ROW, D), BF), ((ROW, D), BF), ((ROW, GRADS), BF), ((ROW, GRADS), BF), ((16, D), F32)],
        [core, acts, first, vec, own, other, cotangent, slope, normed, scale, q, k, v, soft],
        scratch=[pltpu.VMEM((ROW, D), F32), pltpu.VMEM((ROW, FF), BF)] + [pltpu.VMEM((ROW, D), BF)] * 6,
        smem=(0,),
        args=(6,),
        results=(0, 1),
        flops=18 * 2 * ROW * D * D,
    )
    (weights,) = call(
        weights_kernel,
        [((D, BLOCK), BF)],
        [acts, acts_other, keep, swap(send), vg, swap(vg)],
        scratch=[pltpu.VMEM((128, D), F32)],
        flops=2 * 256 * 512 * 3072,
    )
    weights = to_chips(weights.reshape(64, 8, BLOCK))
    grads, pay = call(
        reduce_kernel, [((8, BLOCK), F32), ((64, 8, 1152), BF)], [core, weights], smem=(0,)
    )
    grads_other = swap(grads)
    mom_other = swap(mom)
    pay, mom, mom_other = lax.optimization_barrier((pay, mom, mom_other))
    pay = to_chips(pay)
    pay_other = swap(pay)
    where = jnp.stack([c, y, plane]).astype(jnp.int32)
    orth, clip_norm, factors = call(
        newton_kernel,
        [((4, 2, 8, 1024), BF), ((1, 1), F32), ((8, 128), F32)],
        [where, pay.reshape(D, 1152), pay_other.reshape(D, 1152), mom, mom_other],
        scratch=[
            pltpu.VMEM((8, D, HALF), BF),
            pltpu.VMEM((D, D), F32),
            pltpu.VMEM((128, D), F32),
        ],
        smem=(0,),
        results=(1,),
        flops=16 * 3 * 2 * D * D * D,
        limit=24 * 1024 * 1024,
    )
    orth = orth.reshape(8, 8, 1024)
    orth = lax.all_to_all(orth, ("y", "c"), 0, 0, tiled=True)
    outs = call(
        update_kernel,
        [((4, 4, D), F32), ((4, FF), F32), ((16, D), F32)] * 2
        + [((4, 4, D), BF), ((4, FF), BF), ((16, D), BF)]
        + [((4, 12), F32)] * 3
        + [((4, 12), BF)],
        [
            core, orth, grads, grads_other, factors, attn_master, up_master, down_master, vec_master.T,
            attn_moment, up_moment, down_moment, vec_moment.T, vec_second.T,
        ],
        scratch=[pltpu.VMEM((16, FF), F32), pltpu.VMEM((2, 16, D), F32)],
        smem=(0,),
        args=range(5, 14),
        results=range(13),
    )
    return (layer_out, input_grad, clip_norm[0, 0], *outs[:9], *(t.T for t in outs[9:]))


def solution(mesh):
    grid = Mesh(mesh.devices.reshape(4, 4, 4, 2), ("x", "z", "y", "c"))
    row, mat, vec = P(ALL, None), P(None, ALL, None), P(None, ALL)
    return jax.shard_map(
        body,
        mesh=grid,
        in_specs=(row, row, row, mat, row, row, vec, mat, row, row, vec, vec),
        out_specs=(row, row, P(), mat, row, row, mat, row, row, mat, row, row, vec, vec, vec, vec),
        check_vma=False,
    )
```

```python
import math

import jax
import jax.numpy as jnp
from jax import lax
from jax.experimental import pallas as pl
from jax.experimental.pallas import tpu as pltpu
from jax.sharding import Mesh, PartitionSpec as P

D = 512
FF = 2048
H = 8
HD = 64
ROW = 128
STEP = 10
NS_ITERS = 5
HALF = 256

MASKED_SCORE = -1e30
NORM_EPSILON = 1e-05
CLIP_LIMIT = 1.0
MOMENTUM_DECAY = 0.95
RATE_MATRIX = 0.5
DECAY_MATRIX = 0.01
BETA_FIRST = 0.9
BETA_SECOND = 0.999
RATE_VECTOR = 0.2
ADAM_EPSILON = 1e-08
NEWTON_FIRST = 3.4445
NEWTON_SECOND = -4.775
NEWTON_THIRD = 2.0315

CHIPS = ("x", "z", "y")
ALL = ("x", "z", "y", "c")
BF = jnp.bfloat16
F32 = jnp.float32
VMEM_LIMIT = 20 * 1024 * 1024


def call(kernel, outs, ins, scratch=(), smem=(), args=(), far=(), results=(), away=(), flops=0, limit=VMEM_LIMIT):
    spec = [
        pl.BlockSpec(memory_space=pltpu.SMEM if i in smem else pl.ANY if i in far else pltpu.VMEM)
        for i in range(len(ins))
    ]
    placed = [
        x if i in smem or i in args
        else pltpu.with_memory_space_constraint(x, pltpu.HBM if i in far else pltpu.VMEM)
        for i, x in enumerate(ins)
    ]
    shapes = [
        jax.ShapeDtypeStruct(s, t) if i in results else pltpu.HBM(s, t) if i in away else pltpu.VMEM(s, t)
        for i, (s, t) in enumerate(outs)
    ]
    moved = sum(math.prod(a.shape) * a.dtype.itemsize for a in ins)
    return pl.pallas_call(
        kernel,
        out_shape=shapes,
        in_specs=spec,
        out_specs=[
            pl.BlockSpec(memory_space=pl.ANY if i in away else pltpu.VMEM) for i in range(len(shapes))
        ],
        scratch_shapes=list(scratch),
        compiler_params=pltpu.CompilerParams(vmem_limit_bytes=limit),
        cost_estimate=pl.CostEstimate(flops=flops, bytes_accessed=moved, transcendentals=0),
    )(*placed)


def dot(a, b):
    return jnp.dot(a, b, preferred_element_type=F32)


def dot_t(a, b):
    return lax.dot_general(a, b, (((1,), (1,)), ((), ())), preferred_element_type=F32)


def dot_in(a, b):
    return lax.dot_general(a, b, (((0,), (0,)), ((), ())), preferred_element_type=F32)


O_LANE, UP_LANE, DOWN_LANE, VEC_LANE, BLOCK = 768, 1024, 2048, 3072, 3200
Z0, H0, O0, X0, WIDE = 0, 2048, 2560, 3072, 3584


def half_lanes(half, size):
    return pl.ds(pl.multiple_of(half * size, size), size)


def regroup():
    source = lax.broadcasted_iota(jnp.int32, (D, D), 0)
    target = lax.broadcasted_iota(jnp.int32, (D, D), 1)
    return jnp.where(target == (source & 3) * 128 + (source >> 2), 1.0, 0.0).astype(BF)


def pack_kernel(
    core, attn, up, down, vec, attn_m, up_m, down_m, keep, send,
    attn_v, up_v, down_v, vec_v, attn_mv, up_mv, down_mv, full, sems,
):
    c = core[0]
    copies = [
        pltpu.make_async_copy(source, target, sems.at[i])
        for i, (source, target) in enumerate(
            [(attn, attn_v), (up, up_v), (down, down_v), (vec, vec_v), (attn_m, attn_mv), (up_m, up_mv), (down_m, down_mv)]
        )
    ]
    for copy in copies:
        copy.start()
    move = regroup()
    for copy in copies:
        copy.wait()
    for first, attn_one, up_one, down_one in ((0, attn_v, up_v, down_v), (4, attn_mv, up_mv, down_mv)):
        rows = slice(first, first + 4)
        for m in range(4):
            full[rows, D * m : D * (m + 1)] = attn_one[m]
        for part in range(4):
            moved = dot(up_one[:, D * part : D * (part + 1)].astype(BF), move)
            for q in range(4):
                lane = FF + D * q + 128 * part
                full[rows, lane : lane + 128] = moved[:, 128 * q : 128 * (q + 1)]
        for i in range(4):
            for q in range(4):
                lane = 2 * FF + D * q
                full[first + i : first + i + 1, lane : lane + D] = down_one[4 * i + q : 4 * i + q + 1, :]
    for target, half in ((keep, c), (send, 1 - c)):
        for m in range(4):
            lanes = pl.ds(pl.multiple_of(D * m + HALF * half, HALF), HALF)
            target[:, HALF * m : HALF * (m + 1)] = full[:, lanes].astype(BF)
        lanes = pl.ds(pl.multiple_of(FF + 1024 * half, 1024), 1024)
        target[:, UP_LANE:DOWN_LANE] = full[:, lanes].astype(BF)
        for q in range(4):
            lanes = pl.ds(pl.multiple_of(2 * FF + D * q + HALF * half, HALF), HALF)
            lane = DOWN_LANE + HALF * q
            target[:, lane : lane + HALF] = full[:, lanes].astype(BF)
    full[:, 0:128] = jnp.zeros((8, 128), F32)
    full[0:4, 0:12] = vec_v[...]
    keep[:, VEC_LANE:BLOCK] = full[:, 0:128].astype(BF)
    send[:, VEC_LANE:BLOCK] = full[:, 0:128].astype(BF)


def role_lanes(block, note):
    gap = jnp.zeros((8, 512), block.dtype)
    tail = [] if note is None else [note]
    return [
        jnp.concatenate([block[:, 0:512], gap] + tail, axis=1),
        jnp.concatenate([block[:, 512:1024], gap] + tail, axis=1),
        jnp.concatenate([block[:, UP_LANE:DOWN_LANE]] + tail, axis=1),
        jnp.concatenate([block[:, DOWN_LANE:VEC_LANE]] + tail, axis=1),
    ]


def spread_kernel(core, keep, got, message, message_mom):
    mine, other = keep[...].astype(F32), got[...].astype(F32)
    is_left = core[0] == 0
    left, right = jnp.where(is_left, mine, other), jnp.where(is_left, other, mine)
    block = jnp.concatenate([left[0:4], right[0:4]], axis=0).astype(BF)
    moms = role_lanes(jnp.concatenate([left[4:8], right[4:8]], axis=0).astype(BF), None)
    for i in range(64):
        message[i] = block
        message_mom[i] = moms[i % 4]


def low_lanes():
    return lax.broadcasted_iota(jnp.int32, (ROW, ROW), 1) < HD


def norm_parts(values):
    centred = values - jnp.mean(values, axis=-1, keepdims=True)
    scale = lax.rsqrt(jnp.mean(centred * centred, axis=-1, keepdims=True) + NORM_EPSILON)
    return centred * scale, scale


def norm_back(grad, gain, normed, scale):
    grad = grad * gain
    return scale * (
        grad
        - jnp.mean(grad, axis=-1, keepdims=True)
        - normed * jnp.mean(grad * normed, axis=-1, keepdims=True)
    )


def forward_kernel(
    core, x, w_own, w_far, seg, q_out, k_out, v_out, p_out, vec_out, acts, first_out, norm_out, scale_out, slope,
    w_other, wide, sems,
):
    c = core[0]
    copies = []
    for i, (first, last) in enumerate(((0, UP_LANE), (UP_LANE, DOWN_LANE), (DOWN_LANE, VEC_LANE))):
        lanes = pl.ds(first, last - first)
        copies.append(pltpu.make_async_copy(w_far.at[:, lanes], w_other.at[:, lanes], sems.at[i]))
        copies[i].start()
    sides = ((c, w_own), (1 - c, w_other))
    vec = w_own[:, VEC_LANE:BLOCK].astype(F32).T[:16]
    vec_out[...] = vec
    moved = dot(vec[8:16].astype(BF), regroup())
    for part in range(4):
        for q in range(4):
            vec_out[8 + q : 9 + q, 128 * part : 128 * (part + 1)] = moved[part : part + 1, 128 * q : 128 * (q + 1)]
    tokens = x[...]
    acts[:, X0:WIDE] = tokens
    names = jnp.broadcast_to(seg[...].astype(F32), (ROW, ROW))
    same = names == names.T
    low = low_lanes()
    parts = (low.astype(F32).astype(BF), (1.0 - low.astype(F32)).astype(BF))
    for half, w in sides:
        if w is w_other:
            copies[0].wait()
        product = dot(tokens, w[:, 0:O_LANE])
        q = (product[:, 0:HALF] + vec_out[0:1, half_lanes(half, HALF)]).astype(BF)
        k = product[:, HALF : 2 * HALF].astype(BF)
        v = (product[:, 2 * HALF : O_LANE] + vec_out[1:2, half_lanes(half, HALF)]).astype(BF)
        for target, value in ((q_out, q), (k_out, k), (v_out, v)):
            target[:, half_lanes(half, HALF)] = value
        for pair in range(2):
            cols = slice(128 * pair, 128 * pair + 128)
            heads = []
            for h in range(2):
                scores = dot_t(q[:, cols] * parts[h], k[:, cols]) * (HD ** (-0.5))
                scores = jnp.where(same, scores, MASKED_SCORE)
                expo = jnp.exp(scores - jnp.max(scores, axis=-1, keepdims=True))
                soft = expo / jnp.sum(expo, axis=-1, keepdims=True)
                p_out[4 * half + 2 * pair + h] = soft
                heads.append(dot(soft.astype(BF), v[:, cols]))
            lanes = pl.ds(pl.multiple_of(O0 + HALF * half + 128 * pair, 128), 128)
            acts[:, lanes] = jnp.where(low, heads[0], heads[1]).astype(BF)
    for half, w in sides:
        wide[:, half_lanes(half, HALF)] = dot(acts[:, O0:X0], w[:, O_LANE:UP_LANE])
    normed, scale = norm_parts(tokens.astype(F32) + wide[...] + vec[2:3])
    norm_out[...] = normed
    scale_out[...] = scale
    first = normed * vec[4:5] + vec[5:6]
    first_out[...] = first
    first_low = first.astype(BF)
    acts[:, H0:O0] = first_low
    root = math.sqrt(2.0 / math.pi)
    copies[1].wait()
    for half, w in sides:
        for k in range(2):
            bias = vec_out[pl.ds(8 + 2 * half + k, 1), :]
            u = dot(first_low, w[:, UP_LANE + D * k : UP_LANE + D * (k + 1)]) + bias
            square = u * u
            tanh = jnp.tanh(root * (u + 0.044715 * (square * u)))
            gate = 0.5 * (1.0 + tanh)
            cols = pl.ds(pl.multiple_of(1024 * half + D * k, D), D)
            slope[:, cols] = gate + 0.5 * u * (1.0 - tanh * tanh) * (root * (1.0 + 3 * 0.044715 * square))
            acts[:, cols] = (u * gate).astype(BF)
    copies[2].wait()


DU0, DF0, GRADS = 1024, 2048, 2304


def backward_kernel(
    core, acts, first, vec_in, w_own, w_other, cot, slope, normed_in, scale_in, q_in, k_in, v_in, p_in,
    out, grad_out, keep, send, vg, wide, du_scr, df_scr, da_scr, do_scr, dq_scr, dk_scr, dv_scr,
):
    c = core[0]
    sides = ((c, w_own), (1 - c, w_other))
    vec = vec_in[...]
    for half, w in sides:
        feed = dot(acts[:, 0:D], w[:, DOWN_LANE : DOWN_LANE + HALF])
        for q in range(1, 4):
            lane = DOWN_LANE + HALF * q
            feed = feed + dot(acts[:, D * q : D * (q + 1)], w[:, lane : lane + HALF])
        wide[:, half_lanes(half, HALF)] = feed
    residual = wide[...] + vec[3:4] + first[...] + acts[:, X0:WIDE].astype(F32)
    normed, scale = norm_parts(residual)
    out[...] = (normed * vec[6:7] + vec[7:8]).astype(BF)
    grad = cot[...].astype(F32)
    vg[...] = jnp.zeros((16, D), F32)
    vg[6:7, :] = jnp.sum(grad * normed, axis=0, keepdims=True)
    vg[7:8, :] = jnp.sum(grad, axis=0, keepdims=True)
    grad2 = norm_back(grad, vec[6:7], normed, scale)
    df_scr[...] = grad2.astype(BF)
    vg[3:4, :] = jnp.sum(df_scr[...].astype(F32), axis=0, keepdims=True)
    for q in range(4):
        lane = DOWN_LANE + HALF * q
        dz = dot_t(df_scr[:, half_lanes(c, HALF)], w_own[:, lane : lane + HALF])
        dz = dz + dot_t(df_scr[:, half_lanes(1 - c, HALF)], w_other[:, lane : lane + HALF])
        du = (dz * slope[:, D * q : D * (q + 1)]).astype(BF)
        du_scr[:, D * q : D * (q + 1)] = du
        vg[8 + q : 9 + q, :] = jnp.sum(du.astype(F32), axis=0, keepdims=True)
    dfirst = grad2
    for half, w in sides:
        dfirst = dfirst + dot_t(du_scr[:, half_lanes(half, 1024)], w[:, UP_LANE:DOWN_LANE])
    normed1 = normed_in[...]
    vg[4:5, :] = jnp.sum(dfirst * normed1, axis=0, keepdims=True)
    vg[5:6, :] = jnp.sum(dfirst, axis=0, keepdims=True)
    dres = norm_back(dfirst, vec[4:5], normed1, scale_in[...])
    da_scr[...] = dres.astype(BF)
    vg[2:3, :] = jnp.sum(da_scr[...].astype(F32), axis=0, keepdims=True)
    dattended = jnp.zeros((ROW, D), F32)
    for half, w in sides:
        dattended = dattended + dot_t(da_scr[:, half_lanes(half, HALF)], w[:, O_LANE:UP_LANE])
    do_scr[...] = dattended.astype(BF)
    low = low_lanes()
    parts = (low.astype(F32).astype(BF), (1.0 - low.astype(F32)).astype(BF))
    share = HD ** (-0.5)
    for pair in range(H // 2):
        cols = slice(128 * pair, 128 * pair + 128)
        q, k, v, do = q_in[:, cols], k_in[:, cols], v_in[:, cols], do_scr[:, cols]
        dqs, dks, dvs = [], [], []
        for h in range(2):
            soft = p_in[2 * pair + h]
            dsoft = dot_t(do * parts[h], v)
            ds = (soft * (dsoft - jnp.sum(soft * dsoft, axis=-1, keepdims=True))).astype(BF)
            dqs.append(dot(ds, k) * share)
            dks.append(dot_in(ds, q) * share)
            dvs.append(dot_in(soft.astype(BF), do))
        dq_scr[:, cols] = jnp.where(low, dqs[0], dqs[1]).astype(BF)
        dk_scr[:, cols] = jnp.where(low, dks[0], dks[1]).astype(BF)
        dv_scr[:, cols] = jnp.where(low, dvs[0], dvs[1]).astype(BF)
    vg[0:1, :] = jnp.sum(dq_scr[...].astype(F32), axis=0, keepdims=True)
    vg[1:2, :] = jnp.sum(dv_scr[...].astype(F32), axis=0, keepdims=True)
    for target, half in ((keep, c), (send, 1 - c)):
        for i, ref in enumerate((dq_scr, dk_scr, dv_scr, da_scr)):
            target[:, HALF * i : HALF * (i + 1)] = ref[:, half_lanes(half, HALF)]
        target[:, DU0:DF0] = du_scr[:, half_lanes(half, 1024)]
        target[:, DF0:GRADS] = df_scr[:, half_lanes(half, HALF)]
    total = grad2 + dres
    for half, w in sides:
        for i, ref in enumerate((dq_scr, dk_scr, dv_scr)):
            total = total + dot_t(ref[:, half_lanes(half, HALF)], w[:, HALF * i : HALF * (i + 1)])
    grad_out[...] = total.astype(BF)


def weights_kernel(acts, acts_other, keep, got, vg, vg_other, out, block, vec, sems):
    def both(one, two, first, last):
        return jnp.concatenate([one[:, first:last], two[:, first:last]], axis=0)

    copies = []

    def leave(first, last):
        lanes = pl.ds(first, last - first)
        copies.append(pltpu.make_async_copy(block.at[:, lanes], out.at[:, lanes], sems.at[len(copies)]))
        copies[-1].start()

    block[:, UP_LANE:DOWN_LANE] = dot_in(both(acts, acts_other, H0, O0), both(keep, got, DU0, DF0)).astype(BF)
    leave(UP_LANE, DOWN_LANE)
    down = both(keep, got, DF0, GRADS)
    for q in range(4):
        lane = DOWN_LANE + HALF * q
        block[:, lane : lane + HALF] = dot_in(both(acts, acts_other, D * q, D * (q + 1)), down).astype(BF)
    leave(DOWN_LANE, VEC_LANE)
    block[:, 0:O_LANE] = dot_in(both(acts, acts_other, X0, WIDE), both(keep, got, 0, O_LANE)).astype(BF)
    block[:, O_LANE:UP_LANE] = dot_in(both(acts, acts_other, O0, X0), both(keep, got, O_LANE, DU0)).astype(BF)
    leave(0, UP_LANE)
    total = vg[...] + vg_other[...]
    vec[...] = jnp.zeros((128, D), F32)
    vec[0:8, :] = total[0:8]
    for part in range(4):
        for q in range(4):
            vec[8 + part : 9 + part, 128 * q : 128 * (q + 1)] = total[8 + q : 9 + q, 128 * part : 128 * (part + 1)]
    vec[8:16, :] = dot_t(vec[8:16, :].astype(BF), regroup())
    block[:, VEC_LANE:BLOCK] = vec[...].T.astype(BF)
    leave(VEC_LANE, BLOCK)
    for copy in copies:
        copy.wait()


def add_up(ref):
    total = ref[0].astype(F32)
    for i in range(1, 64):
        total = total + ref[i].astype(F32)
    return total


def split3(value):
    one = value.astype(BF)
    rest = value - one.astype(F32)
    two = rest.astype(BF)
    three = (rest - two.astype(F32)).astype(BF)
    return one, two, three


def reduce_kernel(core, got, grads, pay):
    grads[...] = add_up(got)
    vec = grads[:, VEC_LANE:BLOCK]
    square = jnp.sum(grads[:, 0:VEC_LANE] * grads[:, 0:VEC_LANE])
    square = square + jnp.where(core[0] == 0, 1.0, 0.0) * jnp.sum(vec * vec)
    row = lax.broadcasted_iota(jnp.int32, (8, 128), 0)
    lane = lax.broadcasted_iota(jnp.int32, (8, 128), 1)
    full = jnp.full((8, 128), square, F32)
    one, two, three = split3(full)
    note = jnp.where(lane == 0, one.astype(F32), jnp.where(lane == 1, two.astype(F32), three.astype(F32)))
    note = jnp.where((row == 0) & (lane < 3), note, 0.0).astype(BF)
    rows = role_lanes(grads[:, 0:VEC_LANE].astype(BF), note)
    for i in range(64):
        pay[i] = rows[i % 4]


def halves(value):
    high = value.astype(BF)
    return high, (value - high.astype(F32)).astype(BF)


def fine(a, b):
    ah, al = a
    bh, bl = b
    return dot(jnp.concatenate([ah, ah, al], axis=1), jnp.concatenate([bh, bl, bh], axis=0))


def newton_kernel(
    where, got, got_other, mom_far, mom_other, out, clip_out, factor_out, mom, m_low, gram, rows_scr, sem
):
    core, role, plane = where[0], where[1], where[2]
    copy = pltpu.make_async_copy(mom_far, mom, sem)
    copy.start()
    note = jnp.sum(got[:, 1024:1152].astype(F32)) + jnp.sum(got_other[:, 1024:1152].astype(F32))
    clip = jnp.sqrt(jnp.full((8, 128), note, F32))
    factors = CLIP_LIMIT / jnp.maximum(clip, CLIP_LIMIT)
    clip_out[...] = clip[0:1, 0:1]
    factor_out[...] = factors
    factor = factors[0:1, 0:1]
    chips = pl.ds(pl.multiple_of(plane * 32, 32), 32)

    def chunk(first):
        cols = pl.ds(first, HALF)
        mine = MOMENTUM_DECAY * mom[:, cols].astype(F32) + factor * got[:, cols].astype(F32)
        other = MOMENTUM_DECAY * mom_other[:, cols].astype(F32) + factor * got_other[:, cols].astype(F32)
        return mine, other

    def put(slot, value):
        value = value.astype(BF)
        m_low[slot] = value
        value = value.astype(F32)
        return jnp.sum(value * value)

    def gram_inner(blocks):
        for a, b in ((0, 0), (0, 1), (1, 1)):
            total = dot_in(m_low[a], m_low[b])
            for k in range(1, blocks):
                total = total + dot_in(m_low[2 * k + a], m_low[2 * k + b])
            gram[HALF * a : HALF * (a + 1), HALF * b : HALF * (b + 1)] = total
            if a != b:
                gram[HALF * b : HALF * (b + 1), HALF * a : HALF * (a + 1)] = total.T

    def scaled(square):
        size = jnp.sqrt(jnp.full((8, 128), square, F32)) + 1e-07
        inverse = (1.0 / size)[0:1, 0:1]
        gram[...] = gram[...] * (inverse * inverse)
        return inverse

    def rows_of(slot):
        return m_low[slot, chips, :].astype(F32)

    copy.wait()

    @pl.when(role < 2)
    def _():
        mine, other = chunk(pl.multiple_of(HALF * core, HALF))
        square = put(0, mine) + put(1, other)
        gram_inner(1)
        inverse = scaled(square)
        rows_scr[0:32, :] = jnp.concatenate([rows_of(0), rows_of(1)], axis=1) * inverse

    @pl.when(role == 2)
    def _():
        square = jnp.float32(0.0)
        for k in range(4):
            mine, other = chunk(HALF * k)
            square = square + put(k, mine) + put(4 + k, other)
        total = dot_t(m_low[0], m_low[0])
        for k in range(1, 8):
            total = total + dot_t(m_low[k], m_low[k])
        gram[...] = total
        inverse = scaled(square)
        here = lax.broadcasted_iota(jnp.int32, (32, D), 0) + 32 * plane
        there = lax.broadcasted_iota(jnp.int32, (32, D), 1)
        rows_scr[0:32, :] = jnp.where(here == there, 1.0, 0.0) * inverse

    @pl.when(role == 3)
    def _():
        square = jnp.float32(0.0)
        for k in range(4):
            mine, other = chunk(HALF * k)
            square = square + put(2 * k, mine) + put(2 * k + 1, other)
        gram_inner(4)
        inverse = scaled(square)
        for k in range(4):
            rows = jnp.concatenate([rows_of(2 * k), rows_of(2 * k + 1)], axis=1)
            rows_scr[32 * k : 32 * (k + 1), :] = rows * inverse

    diagonal = (
        lax.broadcasted_iota(jnp.int32, (D, D), 0) == lax.broadcasted_iota(jnp.int32, (D, D), 1)
    )

    def turn(_, carry):
        own = halves(gram[...])
        poly = NEWTON_SECOND * gram[...] + NEWTON_THIRD * fine(own, own)
        poly = halves(jnp.where(diagonal, poly + NEWTON_FIRST, poly))
        next_gram = halves(fine(poly, own))

        @pl.when(role < 3)
        def _():
            rows = halves(rows_scr[0:32, :])
            both = tuple(jnp.concatenate(pair, axis=0) for pair in zip(next_gram, rows))
            both = fine(both, poly)
            gram[...] = both[0:D]
            rows_scr[0:32, :] = both[D:]

        @pl.when(role == 3)
        def _():
            rows = halves(rows_scr[...])
            both = tuple(jnp.concatenate(pair, axis=0) for pair in zip(next_gram, rows))
            both = fine(both, poly)
            gram[...] = both[0:D]
            rows_scr[...] = both[D:]

        return carry

    lax.fori_loop(0, NS_ITERS - 1, turn, 0)

    def last(count):
        own = halves(gram[...])
        rows = rows_scr[0:count, :]
        once = fine(halves(rows), own)
        twice = fine(halves(once), own)
        rows_scr[0:count, :] = NEWTON_FIRST * rows + NEWTON_SECOND * once + NEWTON_THIRD * twice

    @pl.when(role < 3)
    def _():
        last(32)

    @pl.when(role == 3)
    def _():
        last(128)

    def send(cols, value):
        value = value.reshape(4, 8, value.shape[1])
        out[:, 0, :, cols] = value
        out[:, 1, :, cols] = value

    @pl.when(role < 2)
    def _():
        send(half_lanes(core, HALF), rows_scr[0:32, 0:HALF].astype(BF))
        send(half_lanes(1 - core, HALF), rows_scr[0:32, HALF:D].astype(BF))
        send(slice(512, 1024), jnp.zeros((32, 512), BF))

    @pl.when(role == 2)
    def _():
        rows = halves(rows_scr[0:32, :])
        for k in range(4):
            value = m_low[k]
            send(slice(HALF * k, HALF * (k + 1)), (dot(rows[0], value) + dot(rows[1], value)).astype(BF))

    @pl.when(role == 3)
    def _():
        for k in range(4):
            send(slice(HALF * k, HALF * (k + 1)), rows_scr[32 * k : 32 * (k + 1), 0:HALF].astype(BF))


def update_kernel(
    core, got, grads, grads_other, factors, attn, up, down, vec, attn_m, up_m, down_m, vec_m, vec_s,
    attn_mom, up_mom, down_mom, attn_new, up_new, down_new, attn_copy, up_copy, down_copy,
    vec_mom, vec_sec, vec_new, vec_copy, ups, downs,
):
    c = core[0]
    is_left = c == 0
    factor = factors[0:1, 0:1]
    keep_share = 1.0 - RATE_MATRIX * DECAY_MATRIX

    def rows4(value):
        return jnp.where(is_left, value[0:4], value[4:8])

    def both(first, last):
        mine, other = grads[:, first:last], grads_other[:, first:last]
        left = jnp.where(is_left, mine, other)
        right = jnp.where(is_left, other, mine)
        return left, right

    for m in range(4):
        left, right = both(HALF * m, HALF * (m + 1))
        grad = rows4(jnp.concatenate([left, right], axis=1))
        attn_mom[m] = MOMENTUM_DECAY * attn_m[m] + factor * grad
        new = attn[m] * keep_share - RATE_MATRIX * rows4(got[m, :, 0:512].astype(F32))
        attn_new[m] = new
        attn_copy[m] = new.astype(BF)
    move = regroup()
    left, right = both(UP_LANE, DOWN_LANE)
    high, low = halves(rows4(jnp.concatenate([left, right], axis=1)))
    ups[0:4, :] = high.astype(F32)
    ups[4:8, :] = low.astype(F32)
    ups[8:12, :] = rows4(jnp.concatenate([got[4].astype(F32), got[5].astype(F32)], axis=1))
    ups[12:16, :] = jnp.zeros((4, FF), F32)
    rate = RATE_MATRIX * math.sqrt(max(1.0, FF / D))
    for part in range(4):
        pieces = [ups[:, D * q + 128 * part : D * q + 128 * (part + 1)] for q in range(4)]
        moved = dot_t(jnp.concatenate(pieces, axis=1).astype(BF), move)
        cols = slice(D * part, D * (part + 1))
        up_mom[:, cols] = MOMENTUM_DECAY * up_m[:, cols] + factor * (moved[0:4] + moved[4:8])
        up_new[:, cols] = up[:, cols] * keep_share - rate * moved[8:12]
    up_copy[...] = up_new[...].astype(BF)
    left, right = both(DOWN_LANE, VEC_LANE)
    left_step, right_step = got[6].astype(F32), got[7].astype(F32)
    for q in range(4):
        cols = slice(HALF * q, HALF * (q + 1))
        grad = rows4(jnp.concatenate([left[:, cols], right[:, cols]], axis=1))
        step = rows4(jnp.concatenate([left_step[:, cols], right_step[:, cols]], axis=1))
        for i in range(4):
            downs[0, 4 * i + q : 4 * i + q + 1, :] = grad[i : i + 1]
            downs[1, 4 * i + q : 4 * i + q + 1, :] = step[i : i + 1]
    down_mom[...] = MOMENTUM_DECAY * down_m[...] + factor * downs[0]
    rate = RATE_MATRIX * math.sqrt(max(1.0, D / FF))
    down_new[...] = down[...] * keep_share - rate * downs[1]
    down_copy[...] = down_new[...].astype(BF)
    grad = rows4(grads[:, VEC_LANE:BLOCK])[:, 0:12]
    clipped = factor * grad
    first = BETA_FIRST * vec_m[...] + (1.0 - BETA_FIRST) * clipped
    second = BETA_SECOND * vec_s[...] + (1.0 - BETA_SECOND) * clipped * clipped
    vec_mom[...] = first
    vec_sec[...] = second
    first_hat = first / (1.0 - BETA_FIRST**STEP)
    second_hat = second / (1.0 - BETA_SECOND**STEP)
    new = vec[...] - RATE_VECTOR * first_hat / (jnp.sqrt(second_hat) + ADAM_EPSILON)
    vec_new[...] = new
    vec_copy[...] = new.astype(BF)


def swap(value):
    return lax.ppermute(value, "c", [(0, 1), (1, 0)])


def to_chips(value):
    return lax.all_to_all(value, CHIPS, 0, 0, tiled=True)


def body(
    block_input, cotangent, segment_ids, attn_master, up_master, down_master, vec_master,
    attn_moment, up_moment, down_moment, vec_moment, vec_second,
):
    c = lax.axis_index("c")
    y = lax.axis_index("y")
    plane = lax.axis_index("x") * 4 + lax.axis_index("z")
    core = c.reshape(1).astype(jnp.int32)

    keep, send = call(
        pack_kernel,
        [((8, BLOCK), BF)] * 2,
        [core, attn_master, up_master, down_master, vec_master.T, attn_moment, up_moment, down_moment],
        scratch=[
            pltpu.VMEM((4, 4, D), F32), pltpu.VMEM((4, FF), F32), pltpu.VMEM((16, D), F32), pltpu.VMEM((4, 12), F32),
            pltpu.VMEM((4, 4, D), F32), pltpu.VMEM((4, FF), F32), pltpu.VMEM((16, D), F32),
            pltpu.VMEM((8, 3 * FF), F32), pltpu.SemaphoreType.DMA((7,)),
        ],
        smem=(0,),
        far=range(1, 8),
    )
    message, message_mom = call(
        spread_kernel, [((64, 8, BLOCK), BF), ((64, 8, 1024), BF)], [core, keep, swap(send)], smem=(0,)
    )
    own = to_chips(message)
    own, message_mom = lax.optimization_barrier((own, message_mom))
    other = swap(own)
    mom = to_chips(message_mom).reshape(D, 1024)
    own, other = own.reshape(D, BLOCK), other.reshape(D, BLOCK)
    q, k, v, soft, vec, acts, first, normed, scale, slope, other = call(
        forward_kernel,
        [((ROW, D), BF)] * 3
        + [((H, ROW, ROW), F32), ((16, D), F32), ((ROW, WIDE), BF), ((ROW, D), F32), ((ROW, D), F32)]
        + [((ROW, 1), F32), ((ROW, FF), F32), ((D, BLOCK), BF)],
        [core, block_input, own, other, segment_ids],
        scratch=[pltpu.VMEM((ROW, D), F32), pltpu.SemaphoreType.DMA((3,))],
        smem=(0,),
        args=(1, 4),
        far=(3,),
        flops=8 * 2 * ROW * D * D,
    )
    acts_other = swap(acts)
    layer_out, input_grad, keep, send, vg = call(
        backward_kernel,
        [((ROW, D), BF), ((ROW, D), BF), ((ROW, GRADS), BF), ((ROW, GRADS), BF), ((16, D), F32)],
        [core, acts, first, vec, own, other, cotangent, slope, normed, scale, q, k, v, soft],
        scratch=[pltpu.VMEM((ROW, D), F32), pltpu.VMEM((ROW, FF), BF)] + [pltpu.VMEM((ROW, D), BF)] * 6,
        smem=(0,),
        args=(6,),
        results=(0, 1),
        flops=18 * 2 * ROW * D * D,
    )
    (weights,) = call(
        weights_kernel,
        [((D, BLOCK), BF)],
        [acts, acts_other, keep, swap(send), vg, swap(vg)],
        scratch=[pltpu.VMEM((D, BLOCK), BF), pltpu.VMEM((128, D), F32), pltpu.SemaphoreType.DMA((4,))],
        away=(0,),
        flops=2 * 256 * 512 * 3072,
    )
    weights, mom = lax.optimization_barrier((weights, mom))
    weights = to_chips(weights.reshape(64, 8, BLOCK))
    grads, pay = call(
        reduce_kernel, [((8, BLOCK), F32), ((64, 8, 1152), BF)], [core, weights], smem=(0,)
    )
    pay = to_chips(pay)
    pay, mom, grads = lax.optimization_barrier((pay, mom, grads))
    pay_other, mom_other, grads_other = swap(pay), swap(mom), swap(grads)
    where = jnp.stack([c, y, plane]).astype(jnp.int32)
    orth, clip_norm, factors = call(
        newton_kernel,
        [((4, 2, 8, 1024), BF), ((1, 1), F32), ((8, 128), F32)],
        [where, pay.reshape(D, 1152), pay_other.reshape(D, 1152), mom, mom_other],
        scratch=[
            pltpu.VMEM((D, 1024), BF),
            pltpu.VMEM((8, D, HALF), BF),
            pltpu.VMEM((D, D), F32),
            pltpu.VMEM((128, D), F32),
            pltpu.SemaphoreType.DMA,
        ],
        smem=(0,),
        far=(3,),
        results=(1,),
        flops=16 * 3 * 2 * D * D * D,
        limit=24 * 1024 * 1024,
    )
    orth = orth.reshape(8, 8, 1024)
    orth, grads_other = lax.optimization_barrier((orth, grads_other))
    orth = lax.all_to_all(orth, ("y", "c"), 0, 0, tiled=True)
    outs = call(
        update_kernel,
        [((4, 4, D), F32), ((4, FF), F32), ((16, D), F32)] * 2
        + [((4, 4, D), BF), ((4, FF), BF), ((16, D), BF)]
        + [((4, 12), F32)] * 3
        + [((4, 12), BF)],
        [
            core, orth, grads, grads_other, factors, attn_master, up_master, down_master, vec_master.T,
            attn_moment, up_moment, down_moment, vec_moment.T, vec_second.T,
        ],
        scratch=[pltpu.VMEM((16, FF), F32), pltpu.VMEM((2, 16, D), F32)],
        smem=(0,),
        args=range(5, 14),
        results=range(13),
    )
    return (layer_out, input_grad, clip_norm[0, 0], *outs[:9], *(t.T for t in outs[9:]))


def solution(mesh):
    grid = Mesh(mesh.devices.reshape(4, 4, 4, 2), ("x", "z", "y", "c"))
    row, mat, vec = P(ALL, None), P(None, ALL, None), P(None, ALL)
    return jax.shard_map(
        body,
        mesh=grid,
        in_specs=(row, row, row, mat, row, row, vec, mat, row, row, vec, vec),
        out_specs=(row, row, P(), mat, row, row, mat, row, row, mat, row, row, vec, vec, vec, vec),
        check_vma=False,
    )
```

```python
import math

import jax
import jax.numpy as jnp
from jax import lax
from jax.experimental import pallas as pl
from jax.experimental.pallas import tpu as pltpu
from jax.sharding import Mesh, PartitionSpec as P

D = 512
FF = 2048
H = 8
HD = 64
ROW = 128
STEP = 10
NS_ITERS = 5
HALF = 256

MASKED_SCORE = -1e30
NORM_EPSILON = 1e-05
CLIP_LIMIT = 1.0
MOMENTUM_DECAY = 0.95
RATE_MATRIX = 0.5
DECAY_MATRIX = 0.01
BETA_FIRST = 0.9
BETA_SECOND = 0.999
RATE_VECTOR = 0.2
ADAM_EPSILON = 1e-08
NEWTON_FIRST = 3.4445
NEWTON_SECOND = -4.775
NEWTON_THIRD = 2.0315

CHIPS = ("x", "z", "y")
ALL = ("x", "z", "y", "c")
BF = jnp.bfloat16
F32 = jnp.float32
VMEM_LIMIT = 12 * 1024 * 1024


def call(kernel, outs, ins, scratch=(), smem=(), args=(), far=(), results=(), away=(), flops=0, limit=VMEM_LIMIT):
    spec = [
        pl.BlockSpec(memory_space=pltpu.SMEM if i in smem else pl.ANY if i in far else pltpu.VMEM)
        for i in range(len(ins))
    ]
    placed = [
        x if i in smem or i in args
        else pltpu.with_memory_space_constraint(x, pltpu.HBM if i in far else pltpu.VMEM)
        for i, x in enumerate(ins)
    ]
    shapes = [
        jax.ShapeDtypeStruct(s, t) if i in results else pltpu.HBM(s, t) if i in away else pltpu.VMEM(s, t)
        for i, (s, t) in enumerate(outs)
    ]
    moved = sum(math.prod(a.shape) * a.dtype.itemsize for a in ins)
    return pl.pallas_call(
        kernel,
        out_shape=shapes,
        in_specs=spec,
        out_specs=[
            pl.BlockSpec(memory_space=pl.ANY if i in away else pltpu.VMEM) for i in range(len(shapes))
        ],
        scratch_shapes=list(scratch),
        compiler_params=pltpu.CompilerParams(vmem_limit_bytes=limit),
        cost_estimate=pl.CostEstimate(flops=flops, bytes_accessed=moved, transcendentals=0),
    )(*placed)


def dot(a, b):
    return jnp.dot(a, b, preferred_element_type=F32)


def dot_t(a, b):
    return lax.dot_general(a, b, (((1,), (1,)), ((), ())), preferred_element_type=F32)


def dot_in(a, b):
    return lax.dot_general(a, b, (((0,), (0,)), ((), ())), preferred_element_type=F32)


O_LANE, UP_LANE, DOWN_LANE, VEC_LANE, BLOCK = 768, 1024, 2048, 3072, 3200
X0, A0, H0, Z0, ACTS = 0, 512, 1024, 1536, 3328
Y0, DU0, DF0, GRADS = 0, 1024, 2048, 2560


def half_lanes(half, size):
    return pl.ds(pl.multiple_of(half * size, size), size)


def regroup():
    source = lax.broadcasted_iota(jnp.int32, (D, D), 0)
    target = lax.broadcasted_iota(jnp.int32, (D, D), 1)
    return jnp.where(target == (source & 3) * 128 + (source >> 2), 1.0, 0.0).astype(BF)


def pack_kernel(
    core, attn, up, down, vec, attn_m, up_m, down_m, keep, send,
    attn_v, up_v, down_v, vec_v, attn_mv, up_mv, down_mv, full, block, sems,
):
    c = core[0]
    copies = [
        pltpu.make_async_copy(source, target, sems.at[i])
        for i, (source, target) in enumerate(
            [(attn, attn_v), (up, up_v), (down, down_v), (vec, vec_v), (attn_m, attn_mv), (up_m, up_mv), (down_m, down_mv)]
        )
    ]
    for copy in copies:
        copy.start()
    move = regroup()
    for copy in copies:
        copy.wait()
    for first, attn_one, up_one, down_one in ((0, attn_v, up_v, down_v), (4, attn_mv, up_mv, down_mv)):
        rows = slice(first, first + 4)
        for m in range(4):
            full[rows, D * m : D * (m + 1)] = attn_one[m]
        for part in range(4):
            moved = dot(up_one[:, D * part : D * (part + 1)].astype(BF), move)
            for q in range(4):
                lane = FF + D * q + 128 * part
                full[rows, lane : lane + 128] = moved[:, 128 * q : 128 * (q + 1)]
        for i in range(4):
            for q in range(4):
                lane = 2 * FF + D * q
                full[first + i : first + i + 1, lane : lane + D] = down_one[4 * i + q : 4 * i + q + 1, :]
    for target, half in ((keep, c), (send, 1 - c)):
        for m in range(4):
            lanes = pl.ds(pl.multiple_of(D * m + HALF * half, HALF), HALF)
            block[0:4, HALF * m : HALF * (m + 1)] = full[0:4, lanes]
        for m in range(2):
            lanes = pl.ds(pl.multiple_of(2 * D * m + D * half, D), D)
            block[4:8, D * m : D * (m + 1)] = full[4:8, lanes]
        block[:, UP_LANE:DOWN_LANE] = full[:, pl.ds(pl.multiple_of(FF + 1024 * half, 1024), 1024)]
        for q in range(4):
            lanes = pl.ds(pl.multiple_of(2 * FF + D * q + HALF * half, HALF), HALF)
            lane = DOWN_LANE + HALF * q
            block[0:4, lane : lane + HALF] = full[0:4, lanes]
        lanes = pl.ds(pl.multiple_of(2 * FF + 1024 * half, 1024), 1024)
        block[4:8, DOWN_LANE:VEC_LANE] = full[4:8, lanes]
        block[:, VEC_LANE:BLOCK] = jnp.zeros((8, 128), F32)
        block[0:4, VEC_LANE : VEC_LANE + 12] = vec_v[...]
        target[...] = block[...].astype(BF)


def role_lanes(block, note):
    gap = jnp.zeros((8, 512), block.dtype)
    tail = [] if note is None else [note]
    return [
        jnp.concatenate([block[:, 0:512], gap] + tail, axis=1),
        jnp.concatenate([block[:, 512:1024], gap] + tail, axis=1),
        jnp.concatenate([block[:, UP_LANE:DOWN_LANE]] + tail, axis=1),
        jnp.concatenate([block[:, DOWN_LANE:VEC_LANE]] + tail, axis=1),
    ]


def spread_kernel(core, keep, got, message, message_mom):
    mine, other = keep[...].astype(F32), got[...].astype(F32)
    is_left = core[0] == 0
    left, right = jnp.where(is_left, mine, other), jnp.where(is_left, other, mine)
    block = jnp.concatenate([left[0:4], right[0:4]], axis=0).astype(BF)
    moms = role_lanes(jnp.concatenate([left[4:8], right[4:8]], axis=0).astype(BF), None)
    for i in range(64):
        message[i] = block
        message_mom[i] = moms[i % 4]


def low_lanes():
    return lax.broadcasted_iota(jnp.int32, (ROW, ROW), 1) < HD


def norm_parts(values):
    centred = values - jnp.mean(values, axis=-1, keepdims=True)
    scale = lax.rsqrt(jnp.mean(centred * centred, axis=-1, keepdims=True) + NORM_EPSILON)
    return centred * scale, scale


def norm_back(grad, gain, normed, scale):
    grad = grad * gain
    return scale * (
        grad
        - jnp.mean(grad, axis=-1, keepdims=True)
        - normed * jnp.mean(grad * normed, axis=-1, keepdims=True)
    )


def forward_kernel(
    core, x, w_own, w_far, seg, q_out, k_out, v_out, p_out, vec_out, keep, send, first_out, norm_out, scale_out,
    slope, w_other, wide, pair_scr, acts, sems,
):
    c = core[0]
    copies = []
    for i in range(3):
        lanes = pl.ds(1024 * i, 1024)
        copies.append(pltpu.make_async_copy(w_far.at[:, lanes], w_other.at[:, lanes], sems.at[i]))
        copies[i].start()
    sides = ((c, w_own), (1 - c, w_other))
    vec = w_own[:, VEC_LANE:BLOCK].astype(F32).T[:16]
    vec_out[...] = vec
    moved = dot(vec[8:16].astype(BF), regroup())
    for part in range(4):
        for q in range(4):
            vec_out[8 + q : 9 + q, 128 * part : 128 * (part + 1)] = moved[part : part + 1, 128 * q : 128 * (q + 1)]
    tokens = x[...]
    pair_scr[0] = tokens
    names = jnp.broadcast_to(seg[...].astype(F32), (ROW, ROW))
    same = names == names.T
    low = low_lanes()
    parts = (low.astype(F32).astype(BF), (1.0 - low.astype(F32)).astype(BF))
    for half, w in sides:
        if w is w_other:
            copies[0].wait()
        product = dot(tokens, w[:, 0:O_LANE])
        q = (product[:, 0:HALF] + vec_out[0:1, half_lanes(half, HALF)]).astype(BF)
        k = product[:, HALF : 2 * HALF].astype(BF)
        v = (product[:, 2 * HALF : O_LANE] + vec_out[1:2, half_lanes(half, HALF)]).astype(BF)
        for target, value in ((q_out, q), (k_out, k), (v_out, v)):
            target[:, half_lanes(half, HALF)] = value
        for pair in range(2):
            cols = slice(128 * pair, 128 * pair + 128)
            heads = []
            for h in range(2):
                scores = dot_t(q[:, cols] * parts[h], k[:, cols]) * (HD ** (-0.5))
                scores = jnp.where(same, scores, MASKED_SCORE)
                expo = jnp.exp(scores - jnp.max(scores, axis=-1, keepdims=True))
                soft = expo / jnp.sum(expo, axis=-1, keepdims=True)
                p_out[4 * half + 2 * pair + h] = soft
                heads.append(dot(soft.astype(BF), v[:, cols]))
            lanes = pl.ds(pl.multiple_of(HALF * half + 128 * pair, 128), 128)
            pair_scr[1, :, lanes] = jnp.where(low, heads[0], heads[1]).astype(BF)
    for half, w in sides:
        wide[:, half_lanes(half, HALF)] = dot(pair_scr[1], w[:, O_LANE:UP_LANE])
    normed, scale = norm_parts(tokens.astype(F32) + wide[...] + vec[2:3])
    norm_out[...] = normed
    scale_out[...] = scale
    first = normed * vec[4:5] + vec[5:6]
    first_out[...] = first
    first_low = first.astype(BF)
    root = math.sqrt(2.0 / math.pi)
    copies[1].wait()
    for half, w in sides:
        for k in range(2):
            bias = vec_out[pl.ds(8 + 2 * half + k, 1), :]
            u = dot(first_low, w[:, UP_LANE + D * k : UP_LANE + D * (k + 1)]) + bias
            square = u * u
            tanh = jnp.tanh(root * (u + 0.044715 * (square * u)))
            gate = 0.5 * (1.0 + tanh)
            cols = pl.ds(pl.multiple_of(1024 * half + D * k, D), D)
            slope[:, cols] = gate + 0.5 * u * (1.0 - tanh * tanh) * (root * (1.0 + 3 * 0.044715 * square))
            acts[:, cols] = (u * gate).astype(BF)
    for target, half in ((keep, c), (send, 1 - c)):
        target[:, X0:A0] = tokens
        target[:, A0:H0] = pair_scr[half]
        target[:, H0:Z0] = first_low
        target[:, Z0 : Z0 + 1024] = acts[:, half_lanes(half, 1024)]
        target[:, Z0 + 1024 : ACTS] = jnp.zeros((ROW, ACTS - Z0 - 1024), BF)
    copies[2].wait()


def backward_kernel(
    core, x, acts_own, acts_sent, first, vec_in, w_own, w_other, cot, slope, normed_in, scale_in, q_in, k_in, v_in, p_in,
    out, grad_out, keep, send, vg, wide, du_scr, df_scr, do_scr, y_scr,
):
    c = core[0]
    sides = ((c, w_own), (1 - c, w_other))
    vec = vec_in[...]
    dq_scr, dk_scr, dv_scr, da_scr = (y_scr.at[i] for i in range(4))
    for half, w in sides:
        feed = jnp.zeros((ROW, HALF), F32)
        for group, acts in ((c, acts_own), (1 - c, acts_sent)):
            for k in range(2):
                lanes = pl.ds(pl.multiple_of(DOWN_LANE + 2 * HALF * group + HALF * k, HALF), HALF)
                feed = feed + dot(acts[:, Z0 + D * k : Z0 + D * (k + 1)], w[:, lanes])
        wide[:, half_lanes(half, HALF)] = feed
    residual = wide[...] + vec[3:4] + first[...] + x[...].astype(F32)
    normed, scale = norm_parts(residual)
    out[...] = (normed * vec[6:7] + vec[7:8]).astype(BF)
    grad = cot[...].astype(F32)
    vg[...] = jnp.zeros((16, D), F32)
    vg[6:7, :] = jnp.sum(grad * normed, axis=0, keepdims=True)
    vg[7:8, :] = jnp.sum(grad, axis=0, keepdims=True)
    grad2 = norm_back(grad, vec[6:7], normed, scale)
    df_scr[...] = grad2.astype(BF)
    vg[3:4, :] = jnp.sum(df_scr[...].astype(F32), axis=0, keepdims=True)
    for q in range(4):
        lane = DOWN_LANE + HALF * q
        dz = dot_t(df_scr[:, half_lanes(c, HALF)], w_own[:, lane : lane + HALF])
        dz = dz + dot_t(df_scr[:, half_lanes(1 - c, HALF)], w_other[:, lane : lane + HALF])
        du = (dz * slope[:, D * q : D * (q + 1)]).astype(BF)
        du_scr[:, D * q : D * (q + 1)] = du
        vg[8 + q : 9 + q, :] = jnp.sum(du.astype(F32), axis=0, keepdims=True)
    dfirst = grad2
    for half, w in sides:
        dfirst = dfirst + dot_t(du_scr[:, half_lanes(half, 1024)], w[:, UP_LANE:DOWN_LANE])
    normed1 = normed_in[...]
    vg[4:5, :] = jnp.sum(dfirst * normed1, axis=0, keepdims=True)
    vg[5:6, :] = jnp.sum(dfirst, axis=0, keepdims=True)
    dres = norm_back(dfirst, vec[4:5], normed1, scale_in[...])
    da_scr[...] = dres.astype(BF)
    vg[2:3, :] = jnp.sum(da_scr[...].astype(F32), axis=0, keepdims=True)
    dattended = jnp.zeros((ROW, D), F32)
    for half, w in sides:
        dattended = dattended + dot_t(da_scr[:, half_lanes(half, HALF)], w[:, O_LANE:UP_LANE])
    do_scr[...] = dattended.astype(BF)
    low = low_lanes()
    parts = (low.astype(F32).astype(BF), (1.0 - low.astype(F32)).astype(BF))
    share = HD ** (-0.5)
    for pair in range(H // 2):
        cols = slice(128 * pair, 128 * pair + 128)
        q, k, v, do = q_in[:, cols], k_in[:, cols], v_in[:, cols], do_scr[:, cols]
        dqs, dks, dvs = [], [], []
        for h in range(2):
            soft = p_in[2 * pair + h]
            dsoft = dot_t(do * parts[h], v)
            ds = (soft * (dsoft - jnp.sum(soft * dsoft, axis=-1, keepdims=True))).astype(BF)
            dqs.append(dot(ds, k) * share)
            dks.append(dot_in(ds, q) * share)
            dvs.append(dot_in(soft.astype(BF), do))
        dq_scr[:, cols] = jnp.where(low, dqs[0], dqs[1]).astype(BF)
        dk_scr[:, cols] = jnp.where(low, dks[0], dks[1]).astype(BF)
        dv_scr[:, cols] = jnp.where(low, dvs[0], dvs[1]).astype(BF)
    vg[0:1, :] = jnp.sum(dq_scr[...].astype(F32), axis=0, keepdims=True)
    vg[1:2, :] = jnp.sum(dv_scr[...].astype(F32), axis=0, keepdims=True)
    for target, half in ((keep, c), (send, 1 - c)):
        target[:, 0:D] = y_scr[half]
        target[:, D : 2 * D] = y_scr[2 + half]
        target[:, DU0:DF0] = du_scr[:, half_lanes(half, 1024)]
        target[:, DF0:GRADS] = df_scr[...]
    total = grad2 + dres
    for half, w in sides:
        for i, ref in enumerate((dq_scr, dk_scr, dv_scr)):
            total = total + dot_t(ref[:, half_lanes(half, HALF)], w[:, HALF * i : HALF * (i + 1)])
    grad_out[...] = total.astype(BF)


def weights_kernel(acts, acts_other, keep, got, vg, vg_other, out, block, vec, sems):
    def both(one, two, first, last):
        return jnp.concatenate([one[:, first:last], two[:, first:last]], axis=0)

    copies = []

    def leave(first, last):
        lanes = pl.ds(first, last - first)
        copies.append(pltpu.make_async_copy(block.at[:, lanes], out.at[:, lanes], sems.at[len(copies)]))
        copies[-1].start()

    block[:, UP_LANE:DOWN_LANE] = dot_in(both(acts, acts_other, H0, Z0), both(keep, got, DU0, DF0)).astype(BF)
    leave(UP_LANE, DOWN_LANE)
    down = both(keep, got, DF0, GRADS)
    for k in range(2):
        lane = DOWN_LANE + D * k
        units = both(acts, acts_other, Z0 + D * k, Z0 + D * (k + 1))
        block[:, lane : lane + D] = dot_in(units, down).astype(BF)
    leave(DOWN_LANE, VEC_LANE)
    for k in range(2):
        left = both(acts, acts_other, D * k, D * (k + 1))
        block[:, D * k : D * (k + 1)] = dot_in(left, both(keep, got, D * k, D * (k + 1))).astype(BF)
    leave(0, UP_LANE)
    total = vg[...] + vg_other[...]
    vec[...] = jnp.zeros((128, D), F32)
    vec[0:8, :] = total[0:8]
    for part in range(4):
        for q in range(4):
            vec[8 + part : 9 + part, 128 * q : 128 * (q + 1)] = total[8 + q : 9 + q, 128 * part : 128 * (part + 1)]
    vec[8:16, :] = dot_t(vec[8:16, :].astype(BF), regroup())
    block[:, VEC_LANE:BLOCK] = vec[...].T.astype(BF)
    leave(VEC_LANE, BLOCK)
    for copy in copies:
        copy.wait()


def add_up(ref):
    total = ref[0].astype(F32)
    for i in range(1, 64):
        total = total + ref[i].astype(F32)
    return total


def split3(value):
    one = value.astype(BF)
    rest = value - one.astype(F32)
    two = rest.astype(BF)
    three = (rest - two.astype(F32)).astype(BF)
    return one, two, three


def reduce_kernel(got, grads):
    grads[...] = add_up(got)


def pay_kernel(grads, grads_other, pay):
    vec = grads[:, VEC_LANE:BLOCK]
    own, other = grads[:, 0:VEC_LANE], grads_other[:, 0:VEC_LANE]
    square = (jnp.sum(own * own) + jnp.sum(other * other)) + jnp.sum(vec * vec)
    row = lax.broadcasted_iota(jnp.int32, (8, 128), 0)
    lane = lax.broadcasted_iota(jnp.int32, (8, 128), 1)
    full = jnp.full((8, 128), square, F32)
    one, two, three = split3(full)
    note = jnp.where(lane == 0, one.astype(F32), jnp.where(lane == 1, two.astype(F32), three.astype(F32)))
    note = jnp.where((row == 0) & (lane < 3), note, 0.0).astype(BF)
    rows = role_lanes(grads[:, 0:VEC_LANE].astype(BF), note)
    for i in range(64):
        pay[i] = rows[i % 4]


def halves(value):
    high = value.astype(BF)
    return high, (value - high.astype(F32)).astype(BF)


def fine(a, b):
    ah, al = a
    bh, bl = b
    return dot(jnp.concatenate([ah, ah, al], axis=1), jnp.concatenate([bh, bl, bh], axis=0))


TALL = D + 8


def near_kernel(far, near, sem):
    copy = pltpu.make_async_copy(far, near, sem)
    copy.start()
    copy.wait()


def gram_kernel(role_ref, got, mom, matrix, gram, clip_out, factor_out):
    role = role_ref[0]
    clip = jnp.sqrt(jnp.full((8, 128), jnp.sum(got[:, 1024:1152].astype(F32)), F32))
    factors = CLIP_LIMIT / jnp.maximum(clip, CLIP_LIMIT)
    clip_out[...] = clip[0:1, 0:1]
    factor_out[...] = factors
    factor = factors[0:1, 0:1]

    def make(k):
        cols = slice(D * k, D * (k + 1))
        value = MOMENTUM_DECAY * mom[:, cols].astype(F32) + factor * got[:, cols].astype(F32)
        value = value.astype(BF)
        matrix[k] = value
        value = value.astype(F32)
        return jnp.sum(value * value)

    def finish(total, square):
        gram[0:D, :] = total
        gram[D:TALL, :] = jnp.full((8, D), square, F32)

    @pl.when(role < 2)
    def _():
        square = make(0)
        finish(dot_in(matrix[0], matrix[0]), square)

    @pl.when(role == 2)
    def _():
        square = make(0) + make(1)
        finish(dot_t(matrix[0], matrix[0]) + dot_t(matrix[1], matrix[1]), square)

    @pl.when(role == 3)
    def _():
        square = make(0) + make(1)
        finish(dot_in(matrix[0], matrix[0]) + dot_in(matrix[1], matrix[1]), square)


def newton_kernel(role_ref, plane_ref, matrix, gram_own, gram_other, out, gram, rows_scr):
    role, plane = role_ref[0], plane_ref[0]
    chips = pl.ds(pl.multiple_of(plane * 32, 32), 32)

    def scaled(total):
        size = jnp.sqrt(total[D : D + 1, 0:1]) + 1e-07
        inverse = 1.0 / size
        gram[...] = total[0:D] * (inverse * inverse)
        return inverse

    def rows_of(k):
        return matrix[k, chips, :].astype(F32)

    @pl.when(role < 2)
    def _():
        inverse = scaled(gram_own[...])
        rows_scr[0:32, :] = rows_of(0) * inverse
        rows_scr[32:64, :] = jnp.zeros((32, D), F32)

    @pl.when(role == 2)
    def _():
        inverse = scaled(gram_own[...] + gram_other[...])
        here = lax.broadcasted_iota(jnp.int32, (32, D), 0) + 32 * plane
        there = lax.broadcasted_iota(jnp.int32, (32, D), 1)
        rows_scr[0:32, :] = jnp.where(here == there, 1.0, 0.0) * inverse
        rows_scr[32:64, :] = jnp.zeros((32, D), F32)

    @pl.when(role == 3)
    def _():
        inverse = scaled(gram_own[...] + gram_other[...])
        for k in range(2):
            rows_scr[32 * k : 32 * (k + 1), :] = rows_of(k) * inverse

    diagonal = (
        lax.broadcasted_iota(jnp.int32, (D, D), 0) == lax.broadcasted_iota(jnp.int32, (D, D), 1)
    )

    def turn(_, carry):
        own = halves(gram[...])
        poly = NEWTON_SECOND * gram[...] + NEWTON_THIRD * fine(own, own)
        poly = halves(jnp.where(diagonal, poly + NEWTON_FIRST, poly))
        pairs = zip(halves(fine(poly, own)), halves(rows_scr[...]))
        both = fine(tuple(jnp.concatenate(pair, axis=0) for pair in pairs), poly)
        gram[...] = both[0:D]
        rows_scr[...] = both[D:]
        return carry

    lax.fori_loop(0, NS_ITERS - 1, turn, 0)
    own = halves(gram[...])
    rows = rows_scr[...]
    once = fine(halves(rows), own)
    twice = fine(halves(once), own)
    rows_scr[...] = NEWTON_FIRST * rows + NEWTON_SECOND * once + NEWTON_THIRD * twice

    def send(k, value):
        value = value.astype(BF).reshape(4, 8, D)
        out[:, 0, :, D * k : D * (k + 1)] = value
        out[:, 1, :, D * k : D * (k + 1)] = value

    @pl.when(role == 2)
    def _():
        high, low = halves(rows_scr[0:32, :])
        for k in range(2):
            send(k, dot(high, matrix[k]) + dot(low, matrix[k]))

    @pl.when(role != 2)
    def _():
        for k in range(2):
            send(k, rows_scr[32 * k : 32 * (k + 1), :])


def update_kernel(
    core, got, grads, grads_other, factors, attn, up, down, vec, attn_m, up_m, down_m, vec_m, vec_s,
    attn_mom, up_mom, down_mom, attn_new, up_new, down_new, attn_copy, up_copy, down_copy,
    vec_mom, vec_sec, vec_new, vec_copy, ups, downs,
):
    c = core[0]
    is_left = c == 0
    factor = factors[0:1, 0:1]
    keep_share = 1.0 - RATE_MATRIX * DECAY_MATRIX

    def rows4(value):
        return jnp.where(is_left, value[0:4], value[4:8])

    def both(first, last):
        mine, other = grads[:, first:last], grads_other[:, first:last]
        left = jnp.where(is_left, mine, other)
        right = jnp.where(is_left, other, mine)
        return left, right

    pairs = [both(D * k, D * (k + 1)) for k in range(2)]
    for m in range(4):
        grad = rows4(pairs[m // 2][m % 2])
        attn_mom[m] = MOMENTUM_DECAY * attn_m[m] + factor * grad
        new = attn[m] * keep_share - RATE_MATRIX * rows4(got[m, :, 0:512].astype(F32))
        attn_new[m] = new
        attn_copy[m] = new.astype(BF)
    move = regroup()
    left, right = both(UP_LANE, DOWN_LANE)
    high, low = halves(rows4(jnp.concatenate([left, right], axis=1)))
    ups[0:4, :] = high.astype(F32)
    ups[4:8, :] = low.astype(F32)
    ups[8:12, :] = rows4(jnp.concatenate([got[4].astype(F32), got[5].astype(F32)], axis=1))
    ups[12:16, :] = jnp.zeros((4, FF), F32)
    rate = RATE_MATRIX * math.sqrt(max(1.0, FF / D))
    for part in range(4):
        pieces = [ups[:, D * q + 128 * part : D * q + 128 * (part + 1)] for q in range(4)]
        moved = dot_t(jnp.concatenate(pieces, axis=1).astype(BF), move)
        cols = slice(D * part, D * (part + 1))
        up_mom[:, cols] = MOMENTUM_DECAY * up_m[:, cols] + factor * (moved[0:4] + moved[4:8])
        up_new[:, cols] = up[:, cols] * keep_share - rate * moved[8:12]
    up_copy[...] = up_new[...].astype(BF)
    sides = both(DOWN_LANE, VEC_LANE)
    for q in range(4):
        cols = slice(D * (q % 2), D * (q % 2 + 1))
        grad = rows4(sides[q // 2][:, cols])
        step = rows4(got[6 + q // 2, :, cols].astype(F32))
        for i in range(4):
            downs[0, 4 * i + q : 4 * i + q + 1, :] = grad[i : i + 1]
            downs[1, 4 * i + q : 4 * i + q + 1, :] = step[i : i + 1]
    down_mom[...] = MOMENTUM_DECAY * down_m[...] + factor * downs[0]
    rate = RATE_MATRIX * math.sqrt(max(1.0, D / FF))
    down_new[...] = down[...] * keep_share - rate * downs[1]
    down_copy[...] = down_new[...].astype(BF)
    grad = rows4(grads[:, VEC_LANE:BLOCK])[:, 0:12]
    clipped = factor * grad
    first = BETA_FIRST * vec_m[...] + (1.0 - BETA_FIRST) * clipped
    second = BETA_SECOND * vec_s[...] + (1.0 - BETA_SECOND) * clipped * clipped
    vec_mom[...] = first
    vec_sec[...] = second
    first_hat = first / (1.0 - BETA_FIRST**STEP)
    second_hat = second / (1.0 - BETA_SECOND**STEP)
    new = vec[...] - RATE_VECTOR * first_hat / (jnp.sqrt(second_hat) + ADAM_EPSILON)
    vec_new[...] = new
    vec_copy[...] = new.astype(BF)


def swap(value):
    return lax.ppermute(value, "c", [(0, 1), (1, 0)])


def to_chips(value):
    return lax.all_to_all(value, CHIPS, 0, 0, tiled=True)


def body(
    block_input, cotangent, segment_ids, attn_master, up_master, down_master, vec_master,
    attn_moment, up_moment, down_moment, vec_moment, vec_second,
):
    c = lax.axis_index("c")
    core = c.reshape(1).astype(jnp.int32)
    role = lax.axis_index("y").reshape(1).astype(jnp.int32)
    plane = (lax.axis_index("x") * 4 + lax.axis_index("z")).reshape(1).astype(jnp.int32)
    core, role, plane = lax.optimization_barrier((core, role, plane))

    keep, send = call(
        pack_kernel,
        [((8, BLOCK), BF)] * 2,
        [core, attn_master, up_master, down_master, vec_master.T, attn_moment, up_moment, down_moment],
        scratch=[
            pltpu.VMEM((4, 4, D), F32), pltpu.VMEM((4, FF), F32), pltpu.VMEM((16, D), F32), pltpu.VMEM((4, 12), F32),
            pltpu.VMEM((4, 4, D), F32), pltpu.VMEM((4, FF), F32), pltpu.VMEM((16, D), F32),
            pltpu.VMEM((8, 3 * FF), F32), pltpu.VMEM((8, BLOCK), F32), pltpu.SemaphoreType.DMA((7,)),
        ],
        smem=(0,),
        far=range(1, 8),
    )
    message, message_mom = call(
        spread_kernel, [((64, 8, BLOCK), BF), ((64, 8, 1024), BF)], [core, keep, swap(send)], smem=(0,)
    )
    own = to_chips(message)
    own, message_mom = lax.optimization_barrier((own, message_mom))
    other = swap(own)
    mom = to_chips(message_mom).reshape(D, 1024)
    own, other = own.reshape(D, BLOCK), other.reshape(D, BLOCK)
    q, k, v, soft, vec, acts_own, acts_sent, first, normed, scale, slope, other = call(
        forward_kernel,
        [((ROW, D), BF)] * 3
        + [((H, ROW, ROW), F32), ((16, D), F32), ((ROW, ACTS), BF), ((ROW, ACTS), BF)]
        + [((ROW, D), F32), ((ROW, D), F32), ((ROW, 1), F32), ((ROW, FF), F32), ((D, 3072), BF)],
        [core, block_input, own, other, segment_ids],
        scratch=[
            pltpu.VMEM((ROW, D), F32), pltpu.VMEM((2, ROW, D), BF), pltpu.VMEM((ROW, FF), BF),
            pltpu.SemaphoreType.DMA((3,)),
        ],
        smem=(0,),
        args=(1, 4),
        far=(3,),
        flops=8 * 2 * ROW * D * D,
    )
    acts_other = swap(acts_sent)
    layer_out, input_grad, keep, send, vg = call(
        backward_kernel,
        [((ROW, D), BF), ((ROW, D), BF), ((ROW, GRADS), BF), ((ROW, GRADS), BF), ((16, D), F32)],
        [
            core, block_input, acts_own, acts_sent, first, vec, own, other, cotangent, slope, normed, scale,
            q, k, v, soft,
        ],
        scratch=[
            pltpu.VMEM((ROW, D), F32), pltpu.VMEM((ROW, FF), BF), pltpu.VMEM((ROW, D), BF), pltpu.VMEM((ROW, D), BF),
            pltpu.VMEM((4, ROW, D), BF),
        ],
        smem=(0,),
        args=(1, 8),
        results=(0, 1),
        flops=18 * 2 * ROW * D * D,
    )
    (weights,) = call(
        weights_kernel,
        [((D, BLOCK), BF)],
        [acts_own, acts_other, keep, swap(send), vg, swap(vg)],
        scratch=[pltpu.VMEM((D, BLOCK), BF), pltpu.VMEM((128, D), F32), pltpu.SemaphoreType.DMA((4,))],
        away=(0,),
        flops=2 * 256 * 512 * 3072,
    )
    weights, mom = lax.optimization_barrier((weights, mom))
    weights = to_chips(weights.reshape(64, 8, BLOCK))
    (grads,) = call(reduce_kernel, [((8, BLOCK), F32)], [weights])
    grads, mom = lax.optimization_barrier((grads, mom))
    grads_other = swap(grads)
    (mom,) = call(near_kernel, [((D, 1024), BF)], [mom], scratch=[pltpu.SemaphoreType.DMA], far=(0,))
    (pay,) = call(pay_kernel, [((64, 8, 1152), BF)], [grads, grads_other])
    pay, mom = lax.optimization_barrier((pay, mom))
    pay = to_chips(pay)
    matrix, gram, clip_norm, factors = call(
        gram_kernel,
        [((2, D, D), BF), ((TALL, D), F32), ((1, 1), F32), ((8, 128), F32)],
        [role, pay.reshape(D, 1152), mom],
        smem=(0,),
        results=(2,),
        flops=2 * 2 * D * D * D,
    )
    (orth,) = call(
        newton_kernel,
        [((4, 2, 8, 1024), BF)],
        [role, plane, matrix, gram, swap(gram)],
        scratch=[pltpu.VMEM((D, D), F32), pltpu.VMEM((64, D), F32)],
        smem=(0, 1),
        flops=14 * 3 * 2 * D * D * D,
    )
    orth = orth.reshape(8, 8, 1024)
    orth = lax.all_to_all(orth, ("y", "c"), 0, 0, tiled=True)
    outs = call(
        update_kernel,
        [((4, 4, D), F32), ((4, FF), F32), ((16, D), F32)] * 2
        + [((4, 4, D), BF), ((4, FF), BF), ((16, D), BF)]
        + [((4, 12), F32)] * 3
        + [((4, 12), BF)],
        [
            core, orth, grads, grads_other, factors, attn_master, up_master, down_master, vec_master.T,
            attn_moment, up_moment, down_moment, vec_moment.T, vec_second.T,
        ],
        scratch=[pltpu.VMEM((16, FF), F32), pltpu.VMEM((2, 16, D), F32)],
        smem=(0,),
        args=range(5, 14),
        results=range(13),
    )
    return (layer_out, input_grad, clip_norm[0, 0], *outs[:9], *(t.T for t in outs[9:]))


def solution(mesh):
    grid = Mesh(mesh.devices.reshape(4, 4, 4, 2), ("x", "z", "y", "c"))
    row, mat, vec = P(ALL, None), P(None, ALL, None), P(None, ALL)
    return jax.shard_map(
        body,
        mesh=grid,
        in_specs=(row, row, row, mat, row, row, vec, mat, row, row, vec, vec),
        out_specs=(row, row, P(), mat, row, row, mat, row, row, mat, row, row, vec, vec, vec, vec),
        check_vma=False,
    )
```

```python
import math

import jax
import jax.numpy as jnp
from jax import lax
from jax.experimental import pallas as pl
from jax.experimental.pallas import tpu as pltpu
from jax.sharding import Mesh, PartitionSpec as P

D = 512
FF = 2048
H = 8
HD = 64
ROW = 128
STEP = 10
NS_ITERS = 5
HALF = 256

MASKED_SCORE = -1e30
NORM_EPSILON = 1e-05
CLIP_LIMIT = 1.0
MOMENTUM_DECAY = 0.95
RATE_MATRIX = 0.5
DECAY_MATRIX = 0.01
BETA_FIRST = 0.9
BETA_SECOND = 0.999
RATE_VECTOR = 0.2
ADAM_EPSILON = 1e-08
NEWTON_FIRST = 3.4445
NEWTON_SECOND = -4.775
NEWTON_THIRD = 2.0315

CHIPS = ("x", "z", "y")
ALL = ("x", "z", "y", "c")
BF = jnp.bfloat16
F32 = jnp.float32
VMEM_LIMIT = 12 * 1024 * 1024


def call(kernel, outs, ins, scratch=(), smem=(), args=(), far=(), results=(), away=(), flops=0, limit=VMEM_LIMIT):
    spec = [
        pl.BlockSpec(memory_space=pltpu.SMEM if i in smem else pl.ANY if i in far else pltpu.VMEM)
        for i in range(len(ins))
    ]
    placed = [
        x if i in smem or i in args
        else pltpu.with_memory_space_constraint(x, pltpu.HBM if i in far else pltpu.VMEM)
        for i, x in enumerate(ins)
    ]
    shapes = [
        jax.ShapeDtypeStruct(s, t) if i in results else pltpu.HBM(s, t) if i in away else pltpu.VMEM(s, t)
        for i, (s, t) in enumerate(outs)
    ]
    moved = sum(math.prod(a.shape) * a.dtype.itemsize for a in ins)
    return pl.pallas_call(
        kernel,
        out_shape=shapes,
        in_specs=spec,
        out_specs=[
            pl.BlockSpec(memory_space=pl.ANY if i in away else pltpu.VMEM) for i in range(len(shapes))
        ],
        scratch_shapes=list(scratch),
        compiler_params=pltpu.CompilerParams(vmem_limit_bytes=limit),
        cost_estimate=pl.CostEstimate(flops=flops, bytes_accessed=moved, transcendentals=0),
    )(*placed)


def dot(a, b):
    return jnp.dot(a, b, preferred_element_type=F32)


def dot_t(a, b):
    return lax.dot_general(a, b, (((1,), (1,)), ((), ())), preferred_element_type=F32)


def dot_in(a, b):
    return lax.dot_general(a, b, (((0,), (0,)), ((), ())), preferred_element_type=F32)


O_LANE, UP_LANE, DOWN_LANE, VEC_LANE, BLOCK = 768, 1024, 2048, 3072, 3200
X0, A0, H0, Z0, ACTS = 0, 512, 1024, 1536, 3328
Y0, DU0, DF0, GRADS = 0, 1024, 2048, 2560


def half_lanes(half, size):
    return pl.ds(pl.multiple_of(half * size, size), size)


def regroup():
    source = lax.broadcasted_iota(jnp.int32, (D, D), 0)
    target = lax.broadcasted_iota(jnp.int32, (D, D), 1)
    return jnp.where(target == (source & 3) * 128 + (source >> 2), 1.0, 0.0).astype(BF)


def pack_kernel(
    core, attn, up, down, vec, attn_m, up_m, down_m, keep, send,
    attn_v, up_v, down_v, vec_v, attn_mv, up_mv, down_mv, full, block, sems,
):
    c = core[0]
    copies = [
        pltpu.make_async_copy(source, target, sems.at[i])
        for i, (source, target) in enumerate(
            [(attn, attn_v), (up, up_v), (down, down_v), (vec, vec_v), (attn_m, attn_mv), (up_m, up_mv), (down_m, down_mv)]
        )
    ]
    for copy in copies:
        copy.start()
    move = regroup()
    for copy in copies:
        copy.wait()
    for first, attn_one, up_one, down_one in ((0, attn_v, up_v, down_v), (4, attn_mv, up_mv, down_mv)):
        rows = slice(first, first + 4)
        for m in range(4):
            full[rows, D * m : D * (m + 1)] = attn_one[m]
        for part in range(4):
            moved = dot(up_one[:, D * part : D * (part + 1)].astype(BF), move)
            for q in range(4):
                lane = FF + D * q + 128 * part
                full[rows, lane : lane + 128] = moved[:, 128 * q : 128 * (q + 1)]
        for i in range(4):
            for q in range(4):
                lane = 2 * FF + D * q
                full[first + i : first + i + 1, lane : lane + D] = down_one[4 * i + q : 4 * i + q + 1, :]
    for target, half in ((keep, c), (send, 1 - c)):
        for m in range(4):
            lanes = pl.ds(pl.multiple_of(D * m + HALF * half, HALF), HALF)
            block[0:4, HALF * m : HALF * (m + 1)] = full[0:4, lanes]
        for m in range(2):
            lanes = pl.ds(pl.multiple_of(2 * D * m + D * half, D), D)
            block[4:8, D * m : D * (m + 1)] = full[4:8, lanes]
        block[:, UP_LANE:DOWN_LANE] = full[:, pl.ds(pl.multiple_of(FF + 1024 * half, 1024), 1024)]
        for q in range(4):
            lanes = pl.ds(pl.multiple_of(2 * FF + D * q + HALF * half, HALF), HALF)
            lane = DOWN_LANE + HALF * q
            block[0:4, lane : lane + HALF] = full[0:4, lanes]
        lanes = pl.ds(pl.multiple_of(2 * FF + 1024 * half, 1024), 1024)
        block[4:8, DOWN_LANE:VEC_LANE] = full[4:8, lanes]
        block[:, VEC_LANE:BLOCK] = jnp.zeros((8, 128), F32)
        block[0:4, VEC_LANE : VEC_LANE + 12] = vec_v[...]
        target[...] = block[...].astype(BF)


def role_lanes(block, note):
    gap = jnp.zeros((8, 512), block.dtype)
    tail = [] if note is None else [note]
    return [
        jnp.concatenate([block[:, 0:512], gap] + tail, axis=1),
        jnp.concatenate([block[:, 512:1024], gap] + tail, axis=1),
        jnp.concatenate([block[:, UP_LANE:DOWN_LANE]] + tail, axis=1),
        jnp.concatenate([block[:, DOWN_LANE:VEC_LANE]] + tail, axis=1),
    ]


def spread_kernel(core, keep, got, message, message_mom):
    mine, other = keep[...].astype(F32), got[...].astype(F32)
    is_left = core[0] == 0
    left, right = jnp.where(is_left, mine, other), jnp.where(is_left, other, mine)
    block = jnp.concatenate([left[0:4], right[0:4]], axis=0).astype(BF)
    moms = role_lanes(jnp.concatenate([left[4:8], right[4:8]], axis=0).astype(BF), None)
    for i in range(64):
        message[i] = block
        message_mom[i] = moms[i % 4]


def low_lanes():
    return lax.broadcasted_iota(jnp.int32, (ROW, ROW), 1) < HD


def norm_parts(values):
    centred = values - jnp.mean(values, axis=-1, keepdims=True)
    scale = lax.rsqrt(jnp.mean(centred * centred, axis=-1, keepdims=True) + NORM_EPSILON)
    return centred * scale, scale


def norm_back(grad, gain, normed, scale):
    grad = grad * gain
    return scale * (
        grad
        - jnp.mean(grad, axis=-1, keepdims=True)
        - normed * jnp.mean(grad * normed, axis=-1, keepdims=True)
    )


def forward_kernel(
    core, x, w_own, w_far, seg, q_out, k_out, v_out, p_out, vec_out, keep, send, first_out, norm_out, scale_out,
    slope, w_other, wide, pair_scr, acts, sems,
):
    c = core[0]
    copies = []
    for i in range(3):
        lanes = pl.ds(1024 * i, 1024)
        copies.append(pltpu.make_async_copy(w_far.at[:, lanes], w_other.at[:, lanes], sems.at[i]))
        copies[i].start()
    sides = ((c, w_own), (1 - c, w_other))
    vec = w_own[:, VEC_LANE:BLOCK].astype(F32).T[:16]
    vec_out[...] = vec
    moved = dot(vec[8:16].astype(BF), regroup())
    for part in range(4):
        for q in range(4):
            vec_out[8 + q : 9 + q, 128 * part : 128 * (part + 1)] = moved[part : part + 1, 128 * q : 128 * (q + 1)]
    tokens = x[...]
    pair_scr[0] = tokens
    names = jnp.broadcast_to(seg[...].astype(F32), (ROW, ROW))
    same = names == names.T
    low = low_lanes()
    parts = (low.astype(F32).astype(BF), (1.0 - low.astype(F32)).astype(BF))
    for half, w in sides:
        if w is w_other:
            copies[0].wait()
        product = dot(tokens, w[:, 0:O_LANE])
        q = (product[:, 0:HALF] + vec_out[0:1, half_lanes(half, HALF)]).astype(BF)
        k = product[:, HALF : 2 * HALF].astype(BF)
        v = (product[:, 2 * HALF : O_LANE] + vec_out[1:2, half_lanes(half, HALF)]).astype(BF)
        for target, value in ((q_out, q), (k_out, k), (v_out, v)):
            target[:, half_lanes(half, HALF)] = value
        for pair in range(2):
            cols = slice(128 * pair, 128 * pair + 128)
            heads = []
            for h in range(2):
                scores = dot_t(q[:, cols] * parts[h], k[:, cols]) * (HD ** (-0.5))
                scores = jnp.where(same, scores, MASKED_SCORE)
                expo = jnp.exp(scores - jnp.max(scores, axis=-1, keepdims=True))
                soft = expo / jnp.sum(expo, axis=-1, keepdims=True)
                p_out[4 * half + 2 * pair + h] = soft
                heads.append(dot(soft.astype(BF), v[:, cols]))
            lanes = pl.ds(pl.multiple_of(HALF * half + 128 * pair, 128), 128)
            pair_scr[1, :, lanes] = jnp.where(low, heads[0], heads[1]).astype(BF)
    for half, w in sides:
        wide[:, half_lanes(half, HALF)] = dot(pair_scr[1], w[:, O_LANE:UP_LANE])
    normed, scale = norm_parts(tokens.astype(F32) + wide[...] + vec[2:3])
    norm_out[...] = normed
    scale_out[...] = scale
    first = normed * vec[4:5] + vec[5:6]
    first_out[...] = first
    first_low = first.astype(BF)
    root = math.sqrt(2.0 / math.pi)
    copies[1].wait()
    for half, w in sides:
        for k in range(2):
            bias = vec_out[pl.ds(8 + 2 * half + k, 1), :]
            u = dot(first_low, w[:, UP_LANE + D * k : UP_LANE + D * (k + 1)]) + bias
            square = u * u
            tanh = jnp.tanh(root * (u + 0.044715 * (square * u)))
            gate = 0.5 * (1.0 + tanh)
            cols = pl.ds(pl.multiple_of(1024 * half + D * k, D), D)
            slope[:, cols] = gate + 0.5 * u * (1.0 - tanh * tanh) * (root * (1.0 + 3 * 0.044715 * square))
            acts[:, cols] = (u * gate).astype(BF)
    for target, half in ((keep, c), (send, 1 - c)):
        target[:, X0:A0] = tokens
        target[:, A0:H0] = pair_scr[half]
        target[:, H0:Z0] = first_low
        target[:, Z0 : Z0 + 1024] = acts[:, half_lanes(half, 1024)]
        target[:, Z0 + 1024 : ACTS] = jnp.zeros((ROW, ACTS - Z0 - 1024), BF)
    copies[2].wait()


def backward_kernel(
    core, x, acts_own, acts_sent, first, vec_in, w_own, w_other, cot, slope, normed_in, scale_in, q_in, k_in, v_in, p_in,
    out, grad_out, keep, send, vg, wide, du_scr, df_scr, do_scr, y_scr,
):
    c = core[0]
    sides = ((c, w_own), (1 - c, w_other))
    vec = vec_in[...]
    dq_scr, dk_scr, dv_scr, da_scr = (y_scr.at[i] for i in range(4))
    for half, w in sides:
        feed = jnp.zeros((ROW, HALF), F32)
        for group, acts in ((c, acts_own), (1 - c, acts_sent)):
            for k in range(2):
                lanes = pl.ds(pl.multiple_of(DOWN_LANE + 2 * HALF * group + HALF * k, HALF), HALF)
                feed = feed + dot(acts[:, Z0 + D * k : Z0 + D * (k + 1)], w[:, lanes])
        wide[:, half_lanes(half, HALF)] = feed
    residual = wide[...] + vec[3:4] + first[...] + x[...].astype(F32)
    normed, scale = norm_parts(residual)
    out[...] = (normed * vec[6:7] + vec[7:8]).astype(BF)
    grad = cot[...].astype(F32)
    vg[...] = jnp.zeros((16, D), F32)
    vg[6:7, :] = jnp.sum(grad * normed, axis=0, keepdims=True)
    vg[7:8, :] = jnp.sum(grad, axis=0, keepdims=True)
    grad2 = norm_back(grad, vec[6:7], normed, scale)
    df_scr[...] = grad2.astype(BF)
    vg[3:4, :] = jnp.sum(df_scr[...].astype(F32), axis=0, keepdims=True)
    for q in range(4):
        lane = DOWN_LANE + HALF * q
        dz = dot_t(df_scr[:, half_lanes(c, HALF)], w_own[:, lane : lane + HALF])
        dz = dz + dot_t(df_scr[:, half_lanes(1 - c, HALF)], w_other[:, lane : lane + HALF])
        du = (dz * slope[:, D * q : D * (q + 1)]).astype(BF)
        du_scr[:, D * q : D * (q + 1)] = du
        vg[8 + q : 9 + q, :] = jnp.sum(du.astype(F32), axis=0, keepdims=True)
    dfirst = grad2
    for half, w in sides:
        dfirst = dfirst + dot_t(du_scr[:, half_lanes(half, 1024)], w[:, UP_LANE:DOWN_LANE])
    normed1 = normed_in[...]
    vg[4:5, :] = jnp.sum(dfirst * normed1, axis=0, keepdims=True)
    vg[5:6, :] = jnp.sum(dfirst, axis=0, keepdims=True)
    dres = norm_back(dfirst, vec[4:5], normed1, scale_in[...])
    da_scr[...] = dres.astype(BF)
    vg[2:3, :] = jnp.sum(da_scr[...].astype(F32), axis=0, keepdims=True)
    dattended = jnp.zeros((ROW, D), F32)
    for half, w in sides:
        dattended = dattended + dot_t(da_scr[:, half_lanes(half, HALF)], w[:, O_LANE:UP_LANE])
    do_scr[...] = dattended.astype(BF)
    low = low_lanes()
    parts = (low.astype(F32).astype(BF), (1.0 - low.astype(F32)).astype(BF))
    share = HD ** (-0.5)
    for pair in range(H // 2):
        cols = slice(128 * pair, 128 * pair + 128)
        q, k, v, do = q_in[:, cols], k_in[:, cols], v_in[:, cols], do_scr[:, cols]
        dqs, dks, dvs = [], [], []
        for h in range(2):
            soft = p_in[2 * pair + h]
            dsoft = dot_t(do * parts[h], v)
            ds = (soft * (dsoft - jnp.sum(soft * dsoft, axis=-1, keepdims=True))).astype(BF)
            dqs.append(dot(ds, k) * share)
            dks.append(dot_in(ds, q) * share)
            dvs.append(dot_in(soft.astype(BF), do))
        dq_scr[:, cols] = jnp.where(low, dqs[0], dqs[1]).astype(BF)
        dk_scr[:, cols] = jnp.where(low, dks[0], dks[1]).astype(BF)
        dv_scr[:, cols] = jnp.where(low, dvs[0], dvs[1]).astype(BF)
    vg[0:1, :] = jnp.sum(dq_scr[...].astype(F32), axis=0, keepdims=True)
    vg[1:2, :] = jnp.sum(dv_scr[...].astype(F32), axis=0, keepdims=True)
    for target, half in ((keep, c), (send, 1 - c)):
        target[:, 0:D] = y_scr[half]
        target[:, D : 2 * D] = y_scr[2 + half]
        target[:, DU0:DF0] = du_scr[:, half_lanes(half, 1024)]
        target[:, DF0:GRADS] = df_scr[...]
    total = grad2 + dres
    for half, w in sides:
        for i, ref in enumerate((dq_scr, dk_scr, dv_scr)):
            total = total + dot_t(ref[:, half_lanes(half, HALF)], w[:, HALF * i : HALF * (i + 1)])
    grad_out[...] = total.astype(BF)


def weights_kernel(acts, acts_other, keep, got, vg, vg_other, out, vec):
    def both(one, two, first, last):
        return jnp.concatenate([one[:, first:last], two[:, first:last]], axis=0)

    out[:, UP_LANE:DOWN_LANE] = dot_in(both(acts, acts_other, H0, Z0), both(keep, got, DU0, DF0)).astype(BF)
    down = both(keep, got, DF0, GRADS)
    for k in range(2):
        lane = DOWN_LANE + D * k
        units = both(acts, acts_other, Z0 + D * k, Z0 + D * (k + 1))
        out[:, lane : lane + D] = dot_in(units, down).astype(BF)
    for k in range(2):
        left = both(acts, acts_other, D * k, D * (k + 1))
        out[:, D * k : D * (k + 1)] = dot_in(left, both(keep, got, D * k, D * (k + 1))).astype(BF)
    total = vg[...] + vg_other[...]
    vec[...] = jnp.zeros((128, D), F32)
    vec[0:8, :] = total[0:8]
    for part in range(4):
        for q in range(4):
            vec[8 + part : 9 + part, 128 * q : 128 * (q + 1)] = total[8 + q : 9 + q, 128 * part : 128 * (part + 1)]
    vec[8:16, :] = dot_t(vec[8:16, :].astype(BF), regroup())
    out[:, VEC_LANE:BLOCK] = vec[...].T.astype(BF)


def add_up(ref):
    total = ref[0].astype(F32)
    for i in range(1, 64):
        total = total + ref[i].astype(F32)
    return total


def split3(value):
    one = value.astype(BF)
    rest = value - one.astype(F32)
    two = rest.astype(BF)
    three = (rest - two.astype(F32)).astype(BF)
    return one, two, three


def reduce_kernel(got, grads):
    grads[...] = add_up(got)


def pay_kernel(grads, grads_other, pay):
    vec = grads[:, VEC_LANE:BLOCK]
    own, other = grads[:, 0:VEC_LANE], grads_other[:, 0:VEC_LANE]
    square = (jnp.sum(own * own) + jnp.sum(other * other)) + jnp.sum(vec * vec)
    row = lax.broadcasted_iota(jnp.int32, (8, 128), 0)
    lane = lax.broadcasted_iota(jnp.int32, (8, 128), 1)
    full = jnp.full((8, 128), square, F32)
    one, two, three = split3(full)
    note = jnp.where(lane == 0, one.astype(F32), jnp.where(lane == 1, two.astype(F32), three.astype(F32)))
    note = jnp.where((row == 0) & (lane < 3), note, 0.0).astype(BF)
    rows = role_lanes(grads[:, 0:VEC_LANE].astype(BF), note)
    for i in range(64):
        pay[i] = rows[i % 4]


def halves(value):
    high = value.astype(BF)
    return high, (value - high.astype(F32)).astype(BF)


def fine(a, b):
    ah, al = a
    bh, bl = b
    return dot(jnp.concatenate([ah, ah, al], axis=1), jnp.concatenate([bh, bl, bh], axis=0))


TALL = 3 * HALF + 8


def near_kernel(far, near, sem):
    copy = pltpu.make_async_copy(far, near, sem)
    copy.start()
    copy.wait()


def gram_kernel(role_ref, got, mom, matrix, gram, clip_out, factor_out):
    role = role_ref[0]
    clip = jnp.sqrt(jnp.full((8, 128), jnp.sum(got[:, 1024:1152].astype(F32)), F32))
    factors = CLIP_LIMIT / jnp.maximum(clip, CLIP_LIMIT)
    clip_out[...] = clip[0:1, 0:1]
    factor_out[...] = factors
    factor = factors[0:1, 0:1]

    def make(k):
        cols = slice(D * k, D * (k + 1))
        value = MOMENTUM_DECAY * mom[:, cols].astype(F32) + factor * got[:, cols].astype(F32)
        value = value.astype(BF)
        matrix[k] = value
        value = value.astype(F32)
        return jnp.sum(value * value)

    def finish(product, parts, square):
        for i, (a, b) in enumerate(((0, 0), (0, 1), (1, 1))):
            total = product(a, b, 0)
            for k in range(1, parts):
                total = total + product(a, b, k)
            gram[HALF * i : HALF * (i + 1), :] = total
        gram[3 * HALF : TALL, :] = jnp.full((8, HALF), square, F32)

    def inner(a, b, k):
        return dot_in(matrix[k, :, HALF * a : HALF * (a + 1)], matrix[k, :, HALF * b : HALF * (b + 1)])

    def outer(a, b, k):
        return dot_t(matrix[k, HALF * a : HALF * (a + 1), :], matrix[k, HALF * b : HALF * (b + 1), :])

    @pl.when(role < 2)
    def _():
        square = make(0)
        finish(inner, 1, square)

    @pl.when(role == 2)
    def _():
        square = make(0) + make(1)
        finish(outer, 2, square)

    @pl.when(role == 3)
    def _():
        square = make(0) + make(1)
        finish(inner, 2, square)


def newton_kernel(role_ref, plane_ref, matrix, gram_own, gram_other, out, gram, rows_scr):
    role, plane = role_ref[0], plane_ref[0]
    chips = pl.ds(pl.multiple_of(plane * 32, 32), 32)

    def scaled(total):
        size = jnp.sqrt(total[3 * HALF : 3 * HALF + 1, 0:1]) + 1e-07
        inverse = 1.0 / size
        total = total[0 : 3 * HALF] * (inverse * inverse)
        gram[0:HALF, 0:HALF] = total[0:HALF]
        gram[0:HALF, HALF:D] = total[HALF:D]
        gram[HALF:D, 0:HALF] = total[HALF:D].T
        gram[HALF:D, HALF:D] = total[D : 3 * HALF]
        return inverse

    def rows_of(k):
        return matrix[k, chips, :].astype(F32)

    @pl.when(role < 2)
    def _():
        inverse = scaled(gram_own[...])
        rows_scr[0:32, :] = rows_of(0) * inverse
        rows_scr[32:64, :] = jnp.zeros((32, D), F32)

    @pl.when(role == 2)
    def _():
        inverse = scaled(gram_own[...] + gram_other[...])
        here = lax.broadcasted_iota(jnp.int32, (32, D), 0) + 32 * plane
        there = lax.broadcasted_iota(jnp.int32, (32, D), 1)
        rows_scr[0:32, :] = jnp.where(here == there, 1.0, 0.0) * inverse
        rows_scr[32:64, :] = jnp.zeros((32, D), F32)

    @pl.when(role == 3)
    def _():
        inverse = scaled(gram_own[...] + gram_other[...])
        for k in range(2):
            rows_scr[32 * k : 32 * (k + 1), :] = rows_of(k) * inverse

    diagonal = (
        lax.broadcasted_iota(jnp.int32, (D, D), 0) == lax.broadcasted_iota(jnp.int32, (D, D), 1)
    )

    def turn(_, carry):
        own = halves(gram[...])
        poly = NEWTON_SECOND * gram[...] + NEWTON_THIRD * fine(own, own)
        poly = halves(jnp.where(diagonal, poly + NEWTON_FIRST, poly))
        pairs = zip(halves(fine(poly, own)), halves(rows_scr[...]))
        both = fine(tuple(jnp.concatenate(pair, axis=0) for pair in pairs), poly)
        gram[...] = both[0:D]
        rows_scr[...] = both[D:]
        return carry

    lax.fori_loop(0, NS_ITERS - 1, turn, 0)
    own = halves(gram[...])
    rows = rows_scr[...]
    once = fine(halves(rows), own)
    twice = fine(halves(once), own)
    rows_scr[...] = NEWTON_FIRST * rows + NEWTON_SECOND * once + NEWTON_THIRD * twice

    def send(k, value):
        value = value.astype(BF).reshape(4, 8, D)
        out[:, 0, :, D * k : D * (k + 1)] = value
        out[:, 1, :, D * k : D * (k + 1)] = value

    @pl.when(role == 2)
    def _():
        high, low = halves(rows_scr[0:32, :])
        for k in range(2):
            send(k, dot(high, matrix[k]) + dot(low, matrix[k]))

    @pl.when(role != 2)
    def _():
        for k in range(2):
            send(k, rows_scr[32 * k : 32 * (k + 1), :])


def rows4(is_left, value):
    return jnp.where(is_left, value[0:4], value[4:8])


def natural(ups, move, part):
    pieces = [ups[:, D * q + 128 * part : D * q + 128 * (part + 1)] for q in range(4)]
    return dot_t(jnp.concatenate(pieces, axis=1).astype(BF), move)


def momenta_kernel(
    core, grads, grads_other, factors, vec, attn_m, up_m, down_m, vec_m, vec_s,
    attn_mom, up_mom, down_mom, vec_mom, vec_sec, vec_new, vec_copy, ups, downs,
):
    is_left = core[0] == 0
    factor = factors[0:1, 0:1]

    def both(first, last):
        mine, other = grads[:, first:last], grads_other[:, first:last]
        left = jnp.where(is_left, mine, other)
        right = jnp.where(is_left, other, mine)
        return rows4(is_left, left), rows4(is_left, right)

    pairs = [both(D * k, D * (k + 1)) for k in range(2)]
    for m in range(4):
        attn_mom[m] = MOMENTUM_DECAY * attn_m[m] + factor * pairs[m // 2][m % 2]
    move = regroup()
    high, low = halves(jnp.concatenate(both(UP_LANE, DOWN_LANE), axis=1))
    ups[0:4, :] = high.astype(F32)
    ups[4:8, :] = low.astype(F32)
    for part in range(4):
        moved = natural(ups, move, part)
        cols = slice(D * part, D * (part + 1))
        up_mom[:, cols] = MOMENTUM_DECAY * up_m[:, cols] + factor * (moved[0:4] + moved[4:8])
    sides = both(DOWN_LANE, VEC_LANE)
    for q in range(4):
        grad = sides[q // 2][:, D * (q % 2) : D * (q % 2 + 1)]
        for i in range(4):
            downs[4 * i + q : 4 * i + q + 1, :] = grad[i : i + 1]
    down_mom[...] = MOMENTUM_DECAY * down_m[...] + factor * downs[...]
    clipped = factor * rows4(is_left, grads[:, VEC_LANE:BLOCK])[:, 0:12]
    first = BETA_FIRST * vec_m[...] + (1.0 - BETA_FIRST) * clipped
    second = BETA_SECOND * vec_s[...] + (1.0 - BETA_SECOND) * clipped * clipped
    vec_mom[...] = first
    vec_sec[...] = second
    first_hat = first / (1.0 - BETA_FIRST**STEP)
    second_hat = second / (1.0 - BETA_SECOND**STEP)
    new = vec[...] - RATE_VECTOR * first_hat / (jnp.sqrt(second_hat) + ADAM_EPSILON)
    vec_new[...] = new
    vec_copy[...] = new.astype(BF)


def update_kernel(
    core, got, attn, up, down, attn_new, up_new, down_new, attn_copy, up_copy, down_copy, ups, downs
):
    is_left = core[0] == 0
    keep_share = 1.0 - RATE_MATRIX * DECAY_MATRIX
    for m in range(4):
        new = attn[m] * keep_share - RATE_MATRIX * rows4(is_left, got[m, :, 0:512].astype(F32))
        attn_new[m] = new
        attn_copy[m] = new.astype(BF)
    move = regroup()
    ups[0:4, :] = rows4(is_left, jnp.concatenate([got[4].astype(F32), got[5].astype(F32)], axis=1))
    ups[4:8, :] = jnp.zeros((4, FF), F32)
    rate = RATE_MATRIX * math.sqrt(max(1.0, FF / D))
    for part in range(4):
        cols = slice(D * part, D * (part + 1))
        up_new[:, cols] = up[:, cols] * keep_share - rate * natural(ups, move, part)[0:4]
    up_copy[...] = up_new[...].astype(BF)
    rate = RATE_MATRIX * math.sqrt(max(1.0, D / FF))
    for q in range(4):
        step = rows4(is_left, got[6 + q // 2, :, D * (q % 2) : D * (q % 2 + 1)].astype(F32))
        for i in range(4):
            downs[4 * i + q : 4 * i + q + 1, :] = step[i : i + 1]
    down_new[...] = down[...] * keep_share - rate * downs[...]
    down_copy[...] = down_new[...].astype(BF)


def swap(value):
    return lax.ppermute(value, "c", [(0, 1), (1, 0)])


def to_chips(value):
    return lax.all_to_all(value, CHIPS, 0, 0, tiled=True)


def body(
    block_input, cotangent, segment_ids, attn_master, up_master, down_master, vec_master,
    attn_moment, up_moment, down_moment, vec_moment, vec_second,
):
    c = lax.axis_index("c")
    core = c.reshape(1).astype(jnp.int32)
    role = lax.axis_index("y").reshape(1).astype(jnp.int32)
    plane = (lax.axis_index("x") * 4 + lax.axis_index("z")).reshape(1).astype(jnp.int32)
    core, role, plane = lax.optimization_barrier((core, role, plane))

    keep, send = call(
        pack_kernel,
        [((8, BLOCK), BF)] * 2,
        [core, attn_master, up_master, down_master, vec_master.T, attn_moment, up_moment, down_moment],
        scratch=[
            pltpu.VMEM((4, 4, D), F32), pltpu.VMEM((4, FF), F32), pltpu.VMEM((16, D), F32), pltpu.VMEM((4, 12), F32),
            pltpu.VMEM((4, 4, D), F32), pltpu.VMEM((4, FF), F32), pltpu.VMEM((16, D), F32),
            pltpu.VMEM((8, 3 * FF), F32), pltpu.VMEM((8, BLOCK), F32), pltpu.SemaphoreType.DMA((7,)),
        ],
        smem=(0,),
        far=range(1, 8),
    )
    message, message_mom = call(
        spread_kernel, [((64, 8, BLOCK), BF), ((64, 8, 1024), BF)], [core, keep, swap(send)], smem=(0,)
    )
    own = to_chips(message)
    own, message_mom = lax.optimization_barrier((own, message_mom))
    other = swap(own)
    mom = to_chips(message_mom).reshape(D, 1024)
    own, other = own.reshape(D, BLOCK), other.reshape(D, BLOCK)
    q, k, v, soft, vec, acts_own, acts_sent, first, normed, scale, slope, other = call(
        forward_kernel,
        [((ROW, D), BF)] * 3
        + [((H, ROW, ROW), F32), ((16, D), F32), ((ROW, ACTS), BF), ((ROW, ACTS), BF)]
        + [((ROW, D), F32), ((ROW, D), F32), ((ROW, 1), F32), ((ROW, FF), F32), ((D, 3072), BF)],
        [core, block_input, own, other, segment_ids],
        scratch=[
            pltpu.VMEM((ROW, D), F32), pltpu.VMEM((2, ROW, D), BF), pltpu.VMEM((ROW, FF), BF),
            pltpu.SemaphoreType.DMA((3,)),
        ],
        smem=(0,),
        args=(1, 4),
        far=(3,),
        flops=8 * 2 * ROW * D * D,
    )
    acts_other = swap(acts_sent)
    layer_out, input_grad, keep, send, vg = call(
        backward_kernel,
        [((ROW, D), BF), ((ROW, D), BF), ((ROW, GRADS), BF), ((ROW, GRADS), BF), ((16, D), F32)],
        [
            core, block_input, acts_own, acts_sent, first, vec, own, other, cotangent, slope, normed, scale,
            q, k, v, soft,
        ],
        scratch=[
            pltpu.VMEM((ROW, D), F32), pltpu.VMEM((ROW, FF), BF), pltpu.VMEM((ROW, D), BF), pltpu.VMEM((ROW, D), BF),
            pltpu.VMEM((4, ROW, D), BF),
        ],
        smem=(0,),
        args=(1, 8),
        results=(0, 1),
        flops=18 * 2 * ROW * D * D,
    )
    (weights,) = call(
        weights_kernel,
        [((D, BLOCK), BF)],
        [acts_own, acts_other, keep, swap(send), vg, swap(vg)],
        scratch=[pltpu.VMEM((128, D), F32)],
        flops=2 * 256 * 512 * 3072,
    )
    weights, mom = lax.optimization_barrier((weights, mom))
    weights = to_chips(weights.reshape(64, 8, BLOCK))
    (grads,) = call(reduce_kernel, [((8, BLOCK), F32)], [weights])
    grads, mom = lax.optimization_barrier((grads, mom))
    grads_other = swap(grads)
    (mom,) = call(near_kernel, [((D, 1024), BF)], [mom], scratch=[pltpu.SemaphoreType.DMA], far=(0,))
    (pay,) = call(pay_kernel, [((64, 8, 1152), BF)], [grads, grads_other])
    pay, mom = lax.optimization_barrier((pay, mom))
    pay = to_chips(pay)
    matrix, gram, clip_norm, factors = call(
        gram_kernel,
        [((2, D, D), BF), ((TALL, HALF), F32), ((1, 1), F32), ((8, 128), F32)],
        [role, pay.reshape(D, 1152), mom],
        smem=(0,),
        results=(2,),
        flops=2 * 2 * D * D * D,
    )
    gram_other = swap(gram)
    *moms, vec_mom, vec_sec, vec_new, vec_copy = call(
        momenta_kernel,
        [((4, 4, D), F32), ((4, FF), F32), ((16, D), F32)] + [((4, 12), F32)] * 3 + [((4, 12), BF)],
        [
            core, grads, grads_other, factors, vec_master.T, attn_moment, up_moment, down_moment,
            vec_moment.T, vec_second.T,
        ],
        scratch=[pltpu.VMEM((8, FF), F32), pltpu.VMEM((16, D), F32)],
        smem=(0,),
        args=range(4, 10),
        results=range(7),
    )
    gram_other, *moms = lax.optimization_barrier((gram_other, *moms))
    vecs = [t.T for t in (vec_mom, vec_sec, vec_new, vec_copy)]
    (orth,) = call(
        newton_kernel,
        [((4, 2, 8, 1024), BF)],
        [role, plane, matrix, gram, gram_other],
        scratch=[pltpu.VMEM((D, D), F32), pltpu.VMEM((64, D), F32)],
        smem=(0, 1),
        flops=14 * 3 * 2 * D * D * D,
    )
    orth = orth.reshape(8, 8, 1024)
    orth = lax.all_to_all(orth, ("y", "c"), 0, 0, tiled=True)
    news = call(
        update_kernel,
        [((4, 4, D), F32), ((4, FF), F32), ((16, D), F32), ((4, 4, D), BF), ((4, FF), BF), ((16, D), BF)],
        [core, orth, attn_master, up_master, down_master],
        scratch=[pltpu.VMEM((8, FF), F32), pltpu.VMEM((16, D), F32)],
        smem=(0,),
        args=range(2, 5),
        results=range(6),
    )
    return (layer_out, input_grad, clip_norm[0, 0], *moms, *news, *vecs)


def solution(mesh):
    grid = Mesh(mesh.devices.reshape(4, 4, 4, 2), ("x", "z", "y", "c"))
    row, mat, vec = P(ALL, None), P(None, ALL, None), P(None, ALL)
    return jax.shard_map(
        body,
        mesh=grid,
        in_specs=(row, row, row, mat, row, row, vec, mat, row, row, vec, vec),
        out_specs=(row, row, P(), mat, row, row, mat, row, row, mat, row, row, vec, vec, vec, vec),
        check_vma=False,
    )
```

```python
import math

import jax
import jax.numpy as jnp
from jax import lax
from jax.experimental import pallas as pl
from jax.experimental.pallas import tpu as pltpu
from jax.sharding import Mesh, PartitionSpec as P

D = 512
FF = 2048
H = 8
HD = 64
ROW = 128
STEP = 10
NS_ITERS = 5
HALF = 256

MASKED_SCORE = -1e30
NORM_EPSILON = 1e-05
CLIP_LIMIT = 1.0
MOMENTUM_DECAY = 0.95
RATE_MATRIX = 0.5
DECAY_MATRIX = 0.01
BETA_FIRST = 0.9
BETA_SECOND = 0.999
RATE_VECTOR = 0.2
ADAM_EPSILON = 1e-08
NEWTON_FIRST = 3.4445
NEWTON_SECOND = -4.775
NEWTON_THIRD = 2.0315

CHIPS = ("x", "z", "y")
ALL = ("x", "z", "y", "c")
BF = jnp.bfloat16
F32 = jnp.float32
VMEM_LIMIT = 12 * 1024 * 1024


def call(kernel, outs, ins, scratch=(), smem=(), args=(), far=(), results=(), away=(), flops=0, limit=VMEM_LIMIT):
    spec = [
        pl.BlockSpec(memory_space=pltpu.SMEM if i in smem else pl.ANY if i in far else pltpu.VMEM)
        for i in range(len(ins))
    ]
    placed = [
        x if i in smem or i in args
        else pltpu.with_memory_space_constraint(x, pltpu.HBM if i in far else pltpu.VMEM)
        for i, x in enumerate(ins)
    ]
    shapes = [
        jax.ShapeDtypeStruct(s, t) if i in results else pltpu.HBM(s, t) if i in away else pltpu.VMEM(s, t)
        for i, (s, t) in enumerate(outs)
    ]
    moved = sum(math.prod(a.shape) * a.dtype.itemsize for a in ins)
    return pl.pallas_call(
        kernel,
        out_shape=shapes,
        in_specs=spec,
        out_specs=[
            pl.BlockSpec(memory_space=pl.ANY if i in away else pltpu.VMEM) for i in range(len(shapes))
        ],
        scratch_shapes=list(scratch),
        compiler_params=pltpu.CompilerParams(vmem_limit_bytes=limit),
        cost_estimate=pl.CostEstimate(flops=flops, bytes_accessed=moved, transcendentals=0),
    )(*placed)


def dot(a, b):
    return jnp.dot(a, b, preferred_element_type=F32)


def dot_t(a, b):
    return lax.dot_general(a, b, (((1,), (1,)), ((), ())), preferred_element_type=F32)


def dot_in(a, b):
    return lax.dot_general(a, b, (((0,), (0,)), ((), ())), preferred_element_type=F32)


O_LANE, UP_LANE, DOWN_LANE, VEC_LANE, BLOCK = 768, 1024, 2048, 3072, 3200
X0, A0, H0, Z0, ACTS = 0, 512, 1024, 1536, 3328
Y0, DU0, DF0, GRADS = 0, 1024, 2048, 2560


def half_lanes(half, size):
    return pl.ds(pl.multiple_of(half * size, size), size)


def regroup():
    source = lax.broadcasted_iota(jnp.int32, (D, D), 0)
    target = lax.broadcasted_iota(jnp.int32, (D, D), 1)
    return jnp.where(target == (source & 3) * 128 + (source >> 2), 1.0, 0.0).astype(BF)


def pack_kernel(
    core, attn, up, down, vec, attn_m, up_m, down_m, keep, send,
    attn_v, up_v, down_v, vec_v, attn_mv, up_mv, down_mv, full, block, sems,
):
    c = core[0]
    copies = [
        pltpu.make_async_copy(source, target, sems.at[i])
        for i, (source, target) in enumerate(
            [(attn, attn_v), (up, up_v), (down, down_v), (vec, vec_v), (attn_m, attn_mv), (up_m, up_mv), (down_m, down_mv)]
        )
    ]
    for copy in copies:
        copy.start()
    move = regroup()
    for copy in copies:
        copy.wait()
    for first, attn_one, up_one, down_one in ((0, attn_v, up_v, down_v), (4, attn_mv, up_mv, down_mv)):
        rows = slice(first, first + 4)
        for m in range(4):
            full[rows, D * m : D * (m + 1)] = attn_one[m]
        for part in range(4):
            moved = dot(up_one[:, D * part : D * (part + 1)].astype(BF), move)
            for q in range(4):
                lane = FF + D * q + 128 * part
                full[rows, lane : lane + 128] = moved[:, 128 * q : 128 * (q + 1)]
        for i in range(4):
            for q in range(4):
                lane = 2 * FF + D * q
                full[first + i : first + i + 1, lane : lane + D] = down_one[4 * i + q : 4 * i + q + 1, :]
    for target, half in ((keep, c), (send, 1 - c)):
        for m in range(4):
            lanes = pl.ds(pl.multiple_of(D * m + HALF * half, HALF), HALF)
            block[0:4, HALF * m : HALF * (m + 1)] = full[0:4, lanes]
        for m in range(2):
            lanes = pl.ds(pl.multiple_of(2 * D * m + D * half, D), D)
            block[4:8, D * m : D * (m + 1)] = full[4:8, lanes]
        block[:, UP_LANE:DOWN_LANE] = full[:, pl.ds(pl.multiple_of(FF + 1024 * half, 1024), 1024)]
        for q in range(4):
            lanes = pl.ds(pl.multiple_of(2 * FF + D * q + HALF * half, HALF), HALF)
            lane = DOWN_LANE + HALF * q
            block[0:4, lane : lane + HALF] = full[0:4, lanes]
        lanes = pl.ds(pl.multiple_of(2 * FF + 1024 * half, 1024), 1024)
        block[4:8, DOWN_LANE:VEC_LANE] = full[4:8, lanes]
        block[:, VEC_LANE:BLOCK] = jnp.zeros((8, 128), F32)
        block[0:4, VEC_LANE : VEC_LANE + 12] = vec_v[...]
        target[...] = block[...].astype(BF)


def role_lanes(block, note):
    gap = jnp.zeros((8, 512), block.dtype)
    tail = [] if note is None else [note]
    return [
        jnp.concatenate([block[:, 0:512], gap] + tail, axis=1),
        jnp.concatenate([block[:, 512:1024], gap] + tail, axis=1),
        jnp.concatenate([block[:, UP_LANE:DOWN_LANE]] + tail, axis=1),
        jnp.concatenate([block[:, DOWN_LANE:VEC_LANE]] + tail, axis=1),
    ]


def spread_kernel(core, keep, got, message, message_mom):
    mine, other = keep[...].astype(F32), got[...].astype(F32)
    is_left = core[0] == 0
    left, right = jnp.where(is_left, mine, other), jnp.where(is_left, other, mine)
    block = jnp.concatenate([left[0:4], right[0:4]], axis=0).astype(BF)
    moms = role_lanes(jnp.concatenate([left[4:8], right[4:8]], axis=0).astype(BF), None)
    for i in range(64):
        message[i] = block
        message_mom[i] = moms[i % 4]


def low_lanes():
    return lax.broadcasted_iota(jnp.int32, (ROW, ROW), 1) < HD


def norm_parts(values):
    centred = values - jnp.mean(values, axis=-1, keepdims=True)
    scale = lax.rsqrt(jnp.mean(centred * centred, axis=-1, keepdims=True) + NORM_EPSILON)
    return centred * scale, scale


def norm_back(grad, gain, normed, scale):
    grad = grad * gain
    return scale * (
        grad
        - jnp.mean(grad, axis=-1, keepdims=True)
        - normed * jnp.mean(grad * normed, axis=-1, keepdims=True)
    )


def forward_kernel(
    core, x, w_own, w_far, seg, q_out, k_out, v_out, p_out, vec_out, keep, send, first_out, norm_out, scale_out,
    slope, w_other, wide, pair_scr, acts, sems,
):
    c = core[0]
    copies = []
    for i in range(3):
        lanes = pl.ds(1024 * i, 1024)
        copies.append(pltpu.make_async_copy(w_far.at[:, lanes], w_other.at[:, lanes], sems.at[i]))
        copies[i].start()
    sides = ((c, w_own), (1 - c, w_other))
    vec = w_own[:, VEC_LANE:BLOCK].astype(F32).T[:16]
    vec_out[...] = vec
    moved = dot(vec[8:16].astype(BF), regroup())
    for part in range(4):
        for q in range(4):
            vec_out[8 + q : 9 + q, 128 * part : 128 * (part + 1)] = moved[part : part + 1, 128 * q : 128 * (q + 1)]
    tokens = x[...]
    pair_scr[0] = tokens
    names = jnp.broadcast_to(seg[...].astype(F32), (ROW, ROW))
    same = names == names.T
    low = low_lanes()
    parts = (low.astype(F32).astype(BF), (1.0 - low.astype(F32)).astype(BF))
    for half, w in sides:
        if w is w_other:
            copies[0].wait()
        product = dot(tokens, w[:, 0:O_LANE])
        q = (product[:, 0:HALF] + vec_out[0:1, half_lanes(half, HALF)]).astype(BF)
        k = product[:, HALF : 2 * HALF].astype(BF)
        v = (product[:, 2 * HALF : O_LANE] + vec_out[1:2, half_lanes(half, HALF)]).astype(BF)
        for target, value in ((q_out, q), (k_out, k), (v_out, v)):
            target[:, half_lanes(half, HALF)] = value
        for pair in range(2):
            cols = slice(128 * pair, 128 * pair + 128)
            heads = []
            for h in range(2):
                scores = dot_t(q[:, cols] * parts[h], k[:, cols]) * (HD ** (-0.5))
                scores = jnp.where(same, scores, MASKED_SCORE)
                expo = jnp.exp(scores - jnp.max(scores, axis=-1, keepdims=True))
                soft = expo / jnp.sum(expo, axis=-1, keepdims=True)
                p_out[4 * half + 2 * pair + h] = soft
                heads.append(dot(soft.astype(BF), v[:, cols]))
            lanes = pl.ds(pl.multiple_of(HALF * half + 128 * pair, 128), 128)
            pair_scr[1, :, lanes] = jnp.where(low, heads[0], heads[1]).astype(BF)
    for half, w in sides:
        wide[:, half_lanes(half, HALF)] = dot(pair_scr[1], w[:, O_LANE:UP_LANE])
    normed, scale = norm_parts(tokens.astype(F32) + wide[...] + vec[2:3])
    norm_out[...] = normed
    scale_out[...] = scale
    first = normed * vec[4:5] + vec[5:6]
    first_out[...] = first
    first_low = first.astype(BF)
    root = math.sqrt(2.0 / math.pi)
    copies[1].wait()
    for half, w in sides:
        for k in range(2):
            bias = vec_out[pl.ds(8 + 2 * half + k, 1), :]
            u = dot(first_low, w[:, UP_LANE + D * k : UP_LANE + D * (k + 1)]) + bias
            square = u * u
            tanh = jnp.tanh(root * (u + 0.044715 * (square * u)))
            gate = 0.5 * (1.0 + tanh)
            cols = pl.ds(pl.multiple_of(1024 * half + D * k, D), D)
            slope[:, cols] = gate + 0.5 * u * (1.0 - tanh * tanh) * (root * (1.0 + 3 * 0.044715 * square))
            acts[:, cols] = (u * gate).astype(BF)
    for target, half in ((keep, c), (send, 1 - c)):
        target[:, X0:A0] = tokens
        target[:, A0:H0] = pair_scr[half]
        target[:, H0:Z0] = first_low
        target[:, Z0 : Z0 + 1024] = acts[:, half_lanes(half, 1024)]
        target[:, Z0 + 1024 : ACTS] = jnp.zeros((ROW, ACTS - Z0 - 1024), BF)
    copies[2].wait()


def backward_kernel(
    core, x, acts_own, acts_sent, first, vec_in, w_own, w_other, cot, slope, normed_in, scale_in, q_in, k_in, v_in, p_in,
    out, grad_out, keep, send, vg, wide, du_scr, df_scr, do_scr, y_scr,
):
    c = core[0]
    sides = ((c, w_own), (1 - c, w_other))
    vec = vec_in[...]
    dq_scr, dk_scr, dv_scr, da_scr = (y_scr.at[i] for i in range(4))
    for half, w in sides:
        feed = jnp.zeros((ROW, HALF), F32)
        for group, acts in ((c, acts_own), (1 - c, acts_sent)):
            for k in range(2):
                lanes = pl.ds(pl.multiple_of(DOWN_LANE + 2 * HALF * group + HALF * k, HALF), HALF)
                feed = feed + dot(acts[:, Z0 + D * k : Z0 + D * (k + 1)], w[:, lanes])
        wide[:, half_lanes(half, HALF)] = feed
    residual = wide[...] + vec[3:4] + first[...] + x[...].astype(F32)
    normed, scale = norm_parts(residual)
    out[...] = (normed * vec[6:7] + vec[7:8]).astype(BF)
    grad = cot[...].astype(F32)
    vg[...] = jnp.zeros((16, D), F32)
    vg[6:7, :] = jnp.sum(grad * normed, axis=0, keepdims=True)
    vg[7:8, :] = jnp.sum(grad, axis=0, keepdims=True)
    grad2 = norm_back(grad, vec[6:7], normed, scale)
    df_scr[...] = grad2.astype(BF)
    vg[3:4, :] = jnp.sum(df_scr[...].astype(F32), axis=0, keepdims=True)
    for q in range(4):
        lane = DOWN_LANE + HALF * q
        dz = dot_t(df_scr[:, half_lanes(c, HALF)], w_own[:, lane : lane + HALF])
        dz = dz + dot_t(df_scr[:, half_lanes(1 - c, HALF)], w_other[:, lane : lane + HALF])
        du = (dz * slope[:, D * q : D * (q + 1)]).astype(BF)
        du_scr[:, D * q : D * (q + 1)] = du
        vg[8 + q : 9 + q, :] = jnp.sum(du.astype(F32), axis=0, keepdims=True)
    dfirst = grad2
    for half, w in sides:
        dfirst = dfirst + dot_t(du_scr[:, half_lanes(half, 1024)], w[:, UP_LANE:DOWN_LANE])
    normed1 = normed_in[...]
    vg[4:5, :] = jnp.sum(dfirst * normed1, axis=0, keepdims=True)
    vg[5:6, :] = jnp.sum(dfirst, axis=0, keepdims=True)
    dres = norm_back(dfirst, vec[4:5], normed1, scale_in[...])
    da_scr[...] = dres.astype(BF)
    vg[2:3, :] = jnp.sum(da_scr[...].astype(F32), axis=0, keepdims=True)
    dattended = jnp.zeros((ROW, D), F32)
    for half, w in sides:
        dattended = dattended + dot_t(da_scr[:, half_lanes(half, HALF)], w[:, O_LANE:UP_LANE])
    do_scr[...] = dattended.astype(BF)
    low = low_lanes()
    parts = (low.astype(F32).astype(BF), (1.0 - low.astype(F32)).astype(BF))
    share = HD ** (-0.5)
    for pair in range(H // 2):
        cols = slice(128 * pair, 128 * pair + 128)
        q, k, v, do = q_in[:, cols], k_in[:, cols], v_in[:, cols], do_scr[:, cols]
        dqs, dks, dvs = [], [], []
        for h in range(2):
            soft = p_in[2 * pair + h]
            dsoft = dot_t(do * parts[h], v)
            ds = (soft * (dsoft - jnp.sum(soft * dsoft, axis=-1, keepdims=True))).astype(BF)
            dqs.append(dot(ds, k) * share)
            dks.append(dot_in(ds, q) * share)
            dvs.append(dot_in(soft.astype(BF), do))
        dq_scr[:, cols] = jnp.where(low, dqs[0], dqs[1]).astype(BF)
        dk_scr[:, cols] = jnp.where(low, dks[0], dks[1]).astype(BF)
        dv_scr[:, cols] = jnp.where(low, dvs[0], dvs[1]).astype(BF)
    vg[0:1, :] = jnp.sum(dq_scr[...].astype(F32), axis=0, keepdims=True)
    vg[1:2, :] = jnp.sum(dv_scr[...].astype(F32), axis=0, keepdims=True)
    for target, half in ((keep, c), (send, 1 - c)):
        target[:, 0:D] = y_scr[half]
        target[:, D : 2 * D] = y_scr[2 + half]
        target[:, DU0:DF0] = du_scr[:, half_lanes(half, 1024)]
        target[:, DF0:GRADS] = df_scr[...]
    total = grad2 + dres
    for half, w in sides:
        for i, ref in enumerate((dq_scr, dk_scr, dv_scr)):
            total = total + dot_t(ref[:, half_lanes(half, HALF)], w[:, HALF * i : HALF * (i + 1)])
    grad_out[...] = total.astype(BF)


def weights_kernel(acts, acts_other, keep, got, vg, vg_other, out, vec):
    def both(one, two, first, last):
        return jnp.concatenate([one[:, first:last], two[:, first:last]], axis=0)

    out[:, UP_LANE:DOWN_LANE] = dot_in(both(acts, acts_other, H0, Z0), both(keep, got, DU0, DF0)).astype(BF)
    down = both(keep, got, DF0, GRADS)
    for k in range(2):
        lane = DOWN_LANE + D * k
        units = both(acts, acts_other, Z0 + D * k, Z0 + D * (k + 1))
        out[:, lane : lane + D] = dot_in(units, down).astype(BF)
    for k in range(2):
        left = both(acts, acts_other, D * k, D * (k + 1))
        out[:, D * k : D * (k + 1)] = dot_in(left, both(keep, got, D * k, D * (k + 1))).astype(BF)
    total = vg[...] + vg_other[...]
    vec[...] = jnp.zeros((128, D), F32)
    vec[0:8, :] = total[0:8]
    for part in range(4):
        for q in range(4):
            vec[8 + part : 9 + part, 128 * q : 128 * (q + 1)] = total[8 + q : 9 + q, 128 * part : 128 * (part + 1)]
    vec[8:16, :] = dot_t(vec[8:16, :].astype(BF), regroup())
    out[:, VEC_LANE:BLOCK] = vec[...].T.astype(BF)


def add_up(ref):
    total = ref[0].astype(F32)
    for i in range(1, 64):
        total = total + ref[i].astype(F32)
    return total


def split3(value):
    one = value.astype(BF)
    rest = value - one.astype(F32)
    two = rest.astype(BF)
    three = (rest - two.astype(F32)).astype(BF)
    return one, two, three


def reduce_kernel(got, grads):
    grads[...] = add_up(got)


def pay_kernel(grads, grads_other, pay):
    vec = grads[:, VEC_LANE:BLOCK]
    own, other = grads[:, 0:VEC_LANE], grads_other[:, 0:VEC_LANE]
    square = (jnp.sum(own * own) + jnp.sum(other * other)) + jnp.sum(vec * vec)
    row = lax.broadcasted_iota(jnp.int32, (8, 128), 0)
    lane = lax.broadcasted_iota(jnp.int32, (8, 128), 1)
    full = jnp.full((8, 128), square, F32)
    one, two, three = split3(full)
    note = jnp.where(lane == 0, one.astype(F32), jnp.where(lane == 1, two.astype(F32), three.astype(F32)))
    note = jnp.where((row == 0) & (lane < 3), note, 0.0).astype(BF)
    rows = role_lanes(grads[:, 0:VEC_LANE].astype(BF), note)
    for i in range(64):
        pay[i] = rows[i % 4]


def halves(value):
    high = value.astype(BF)
    return high, (value - high.astype(F32)).astype(BF)


def fine(a, b):
    ah, al = a
    bh, bl = b
    return dot(jnp.concatenate([ah, ah, al], axis=1), jnp.concatenate([bh, bl, bh], axis=0))


TALL = 3 * HALF + 8


def near_kernel(far, near, sem):
    copy = pltpu.make_async_copy(far, near, sem)
    copy.start()
    copy.wait()


def gram_kernel(role_ref, got, mom, matrix, gram, clip_out, factor_out):
    role = role_ref[0]
    clip = jnp.sqrt(jnp.full((8, 128), jnp.sum(got[:, 1024:1152].astype(F32)), F32))
    factors = CLIP_LIMIT / jnp.maximum(clip, CLIP_LIMIT)
    clip_out[...] = clip[0:1, 0:1]
    factor_out[...] = factors
    factor = factors[0:1, 0:1]

    def make(k):
        cols = slice(D * k, D * (k + 1))
        value = MOMENTUM_DECAY * mom[:, cols].astype(F32) + factor * got[:, cols].astype(F32)
        value = value.astype(BF)
        matrix[k] = value
        value = value.astype(F32)
        return jnp.sum(value * value)

    def finish(product, parts, square):
        for i, (a, b) in enumerate(((0, 0), (0, 1), (1, 1))):
            total = product(a, b, 0)
            for k in range(1, parts):
                total = total + product(a, b, k)
            gram[HALF * i : HALF * (i + 1), :] = total
        gram[3 * HALF : TALL, :] = jnp.full((8, HALF), square, F32)

    def inner(a, b, k):
        return dot_in(matrix[k, :, HALF * a : HALF * (a + 1)], matrix[k, :, HALF * b : HALF * (b + 1)])

    def outer(a, b, k):
        return dot_t(matrix[k, HALF * a : HALF * (a + 1), :], matrix[k, HALF * b : HALF * (b + 1), :])

    @pl.when(role < 2)
    def _():
        square = make(0)
        finish(inner, 1, square)

    @pl.when(role == 2)
    def _():
        square = make(0) + make(1)
        finish(outer, 2, square)

    @pl.when(role == 3)
    def _():
        square = make(0) + make(1)
        finish(inner, 2, square)


def newton_kernel(role_ref, plane_ref, matrix, gram_own, gram_other, out, gram, rows_scr):
    role, plane = role_ref[0], plane_ref[0]
    chips = pl.ds(pl.multiple_of(plane * 32, 32), 32)

    def scaled(total):
        size = jnp.sqrt(total[3 * HALF : 3 * HALF + 1, 0:1]) + 1e-07
        inverse = 1.0 / size
        total = total[0 : 3 * HALF] * (inverse * inverse)
        gram[0:HALF, 0:HALF] = total[0:HALF]
        gram[0:HALF, HALF:D] = total[HALF:D]
        gram[HALF:D, 0:HALF] = total[HALF:D].T
        gram[HALF:D, HALF:D] = total[D : 3 * HALF]
        return inverse

    def rows_of(k):
        return matrix[k, chips, :].astype(F32)

    @pl.when(role < 2)
    def _():
        inverse = scaled(gram_own[...])
        rows_scr[0:32, :] = rows_of(0) * inverse
        rows_scr[32:64, :] = jnp.zeros((32, D), F32)

    @pl.when(role == 2)
    def _():
        inverse = scaled(gram_own[...] + gram_other[...])
        here = lax.broadcasted_iota(jnp.int32, (32, D), 0) + 32 * plane
        there = lax.broadcasted_iota(jnp.int32, (32, D), 1)
        rows_scr[0:32, :] = jnp.where(here == there, 1.0, 0.0) * inverse
        rows_scr[32:64, :] = jnp.zeros((32, D), F32)

    @pl.when(role == 3)
    def _():
        inverse = scaled(gram_own[...] + gram_other[...])
        for k in range(2):
            rows_scr[32 * k : 32 * (k + 1), :] = rows_of(k) * inverse

    diagonal = (
        lax.broadcasted_iota(jnp.int32, (D, D), 0) == lax.broadcasted_iota(jnp.int32, (D, D), 1)
    )

    def turn(exact):
        own = halves(gram[...])
        square = fine(own, own) if exact else dot(own[0], own[0])
        poly = NEWTON_SECOND * gram[...] + NEWTON_THIRD * square
        poly = halves(jnp.where(diagonal, poly + NEWTON_FIRST, poly))
        pairs = zip(halves(fine(poly, own)), halves(rows_scr[...]))
        both = fine(tuple(jnp.concatenate(pair, axis=0) for pair in pairs), poly)
        gram[...] = both[0:D]
        rows_scr[...] = both[D:]

    pl.loop(0, NS_ITERS - 2)(lambda _: turn(False))
    turn(True)
    own = halves(gram[...])
    rows = rows_scr[...]
    once = fine(halves(rows), own)
    twice = fine(halves(once), own)
    rows_scr[...] = NEWTON_FIRST * rows + NEWTON_SECOND * once + NEWTON_THIRD * twice

    def send(k, value):
        value = value.astype(BF).reshape(4, 8, D)
        out[:, 0, :, D * k : D * (k + 1)] = value
        out[:, 1, :, D * k : D * (k + 1)] = value

    @pl.when(role == 2)
    def _():
        high, low = halves(rows_scr[0:32, :])
        for k in range(2):
            send(k, dot(high, matrix[k]) + dot(low, matrix[k]))

    @pl.when(role != 2)
    def _():
        for k in range(2):
            send(k, rows_scr[32 * k : 32 * (k + 1), :])


def rows4(is_left, value):
    return jnp.where(is_left, value[0:4], value[4:8])


def natural(ups, move, part):
    pieces = [ups[:, D * q + 128 * part : D * q + 128 * (part + 1)] for q in range(4)]
    return dot_t(jnp.concatenate(pieces, axis=1).astype(BF), move)


def momenta_kernel(
    core, grads, grads_other, factors, vec, attn_m, up_m, down_m, vec_m, vec_s,
    attn_mom, up_mom, down_mom, vec_mom, vec_sec, vec_new, vec_copy, ups, downs,
):
    is_left = core[0] == 0
    factor = factors[0:1, 0:1]

    def both(first, last):
        mine, other = grads[:, first:last], grads_other[:, first:last]
        left = jnp.where(is_left, mine, other)
        right = jnp.where(is_left, other, mine)
        return rows4(is_left, left), rows4(is_left, right)

    pairs = [both(D * k, D * (k + 1)) for k in range(2)]
    for m in range(4):
        attn_mom[m] = MOMENTUM_DECAY * attn_m[m] + factor * pairs[m // 2][m % 2]
    move = regroup()
    high, low = halves(jnp.concatenate(both(UP_LANE, DOWN_LANE), axis=1))
    ups[0:4, :] = high.astype(F32)
    ups[4:8, :] = low.astype(F32)
    for part in range(4):
        moved = natural(ups, move, part)
        cols = slice(D * part, D * (part + 1))
        up_mom[:, cols] = MOMENTUM_DECAY * up_m[:, cols] + factor * (moved[0:4] + moved[4:8])
    sides = both(DOWN_LANE, VEC_LANE)
    for q in range(4):
        grad = sides[q // 2][:, D * (q % 2) : D * (q % 2 + 1)]
        for i in range(4):
            downs[4 * i + q : 4 * i + q + 1, :] = grad[i : i + 1]
    down_mom[...] = MOMENTUM_DECAY * down_m[...] + factor * downs[...]
    clipped = factor * rows4(is_left, grads[:, VEC_LANE:BLOCK])[:, 0:12]
    first = BETA_FIRST * vec_m[...] + (1.0 - BETA_FIRST) * clipped
    second = BETA_SECOND * vec_s[...] + (1.0 - BETA_SECOND) * clipped * clipped
    vec_mom[...] = first
    vec_sec[...] = second
    first_hat = first / (1.0 - BETA_FIRST**STEP)
    second_hat = second / (1.0 - BETA_SECOND**STEP)
    new = vec[...] - RATE_VECTOR * first_hat / (jnp.sqrt(second_hat) + ADAM_EPSILON)
    vec_new[...] = new
    vec_copy[...] = new.astype(BF)


def update_kernel(
    core, got, attn, up, down, attn_new, up_new, down_new, attn_copy, up_copy, down_copy, ups, downs
):
    is_left = core[0] == 0
    keep_share = 1.0 - RATE_MATRIX * DECAY_MATRIX
    for m in range(4):
        new = attn[m] * keep_share - RATE_MATRIX * rows4(is_left, got[m, :, 0:512].astype(F32))
        attn_new[m] = new
        attn_copy[m] = new.astype(BF)
    move = regroup()
    ups[0:4, :] = rows4(is_left, jnp.concatenate([got[4].astype(F32), got[5].astype(F32)], axis=1))
    ups[4:8, :] = jnp.zeros((4, FF), F32)
    rate = RATE_MATRIX * math.sqrt(max(1.0, FF / D))
    for part in range(4):
        cols = slice(D * part, D * (part + 1))
        up_new[:, cols] = up[:, cols] * keep_share - rate * natural(ups, move, part)[0:4]
    up_copy[...] = up_new[...].astype(BF)
    rate = RATE_MATRIX * math.sqrt(max(1.0, D / FF))
    for q in range(4):
        step = rows4(is_left, got[6 + q // 2, :, D * (q % 2) : D * (q % 2 + 1)].astype(F32))
        for i in range(4):
            downs[4 * i + q : 4 * i + q + 1, :] = step[i : i + 1]
    down_new[...] = down[...] * keep_share - rate * downs[...]
    down_copy[...] = down_new[...].astype(BF)


def swap(value):
    return lax.ppermute(value, "c", [(0, 1), (1, 0)])


def to_chips(value):
    return lax.all_to_all(value, CHIPS, 0, 0, tiled=True)


def body(
    block_input, cotangent, segment_ids, attn_master, up_master, down_master, vec_master,
    attn_moment, up_moment, down_moment, vec_moment, vec_second,
):
    c = lax.axis_index("c")
    core = c.reshape(1).astype(jnp.int32)
    role = lax.axis_index("y").reshape(1).astype(jnp.int32)
    plane = (lax.axis_index("x") * 4 + lax.axis_index("z")).reshape(1).astype(jnp.int32)
    core, role, plane = lax.optimization_barrier((core, role, plane))

    keep, send = call(
        pack_kernel,
        [((8, BLOCK), BF)] * 2,
        [core, attn_master, up_master, down_master, vec_master.T, attn_moment, up_moment, down_moment],
        scratch=[
            pltpu.VMEM((4, 4, D), F32), pltpu.VMEM((4, FF), F32), pltpu.VMEM((16, D), F32), pltpu.VMEM((4, 12), F32),
            pltpu.VMEM((4, 4, D), F32), pltpu.VMEM((4, FF), F32), pltpu.VMEM((16, D), F32),
            pltpu.VMEM((8, 3 * FF), F32), pltpu.VMEM((8, BLOCK), F32), pltpu.SemaphoreType.DMA((7,)),
        ],
        smem=(0,),
        far=range(1, 8),
    )
    message, message_mom = call(
        spread_kernel, [((64, 8, BLOCK), BF), ((64, 8, 1024), BF)], [core, keep, swap(send)], smem=(0,)
    )
    own = to_chips(message)
    own, message_mom = lax.optimization_barrier((own, message_mom))
    other = swap(own)
    mom = to_chips(message_mom).reshape(D, 1024)
    own, other = own.reshape(D, BLOCK), other.reshape(D, BLOCK)
    q, k, v, soft, vec, acts_own, acts_sent, first, normed, scale, slope, other = call(
        forward_kernel,
        [((ROW, D), BF)] * 3
        + [((H, ROW, ROW), F32), ((16, D), F32), ((ROW, ACTS), BF), ((ROW, ACTS), BF)]
        + [((ROW, D), F32), ((ROW, D), F32), ((ROW, 1), F32), ((ROW, FF), F32), ((D, 3072), BF)],
        [core, block_input, own, other, segment_ids],
        scratch=[
            pltpu.VMEM((ROW, D), F32), pltpu.VMEM((2, ROW, D), BF), pltpu.VMEM((ROW, FF), BF),
            pltpu.SemaphoreType.DMA((3,)),
        ],
        smem=(0,),
        args=(1, 4),
        far=(3,),
        flops=8 * 2 * ROW * D * D,
    )
    acts_other = swap(acts_sent)
    layer_out, input_grad, keep, send, vg = call(
        backward_kernel,
        [((ROW, D), BF), ((ROW, D), BF), ((ROW, GRADS), BF), ((ROW, GRADS), BF), ((16, D), F32)],
        [
            core, block_input, acts_own, acts_sent, first, vec, own, other, cotangent, slope, normed, scale,
            q, k, v, soft,
        ],
        scratch=[
            pltpu.VMEM((ROW, D), F32), pltpu.VMEM((ROW, FF), BF), pltpu.VMEM((ROW, D), BF), pltpu.VMEM((ROW, D), BF),
            pltpu.VMEM((4, ROW, D), BF),
        ],
        smem=(0,),
        args=(1, 8),
        results=(0, 1),
        flops=18 * 2 * ROW * D * D,
    )
    (weights,) = call(
        weights_kernel,
        [((D, BLOCK), BF)],
        [acts_own, acts_other, keep, swap(send), vg, swap(vg)],
        scratch=[pltpu.VMEM((128, D), F32)],
        flops=2 * 256 * 512 * 3072,
    )
    weights, mom = lax.optimization_barrier((weights, mom))
    weights = to_chips(weights.reshape(64, 8, BLOCK))
    (grads,) = call(reduce_kernel, [((8, BLOCK), F32)], [weights])
    grads, mom = lax.optimization_barrier((grads, mom))
    grads_other = swap(grads)
    (mom,) = call(near_kernel, [((D, 1024), BF)], [mom], scratch=[pltpu.SemaphoreType.DMA], far=(0,))
    (pay,) = call(pay_kernel, [((64, 8, 1152), BF)], [grads, grads_other])
    pay, mom = lax.optimization_barrier((pay, mom))
    pay = to_chips(pay)
    matrix, gram, clip_norm, factors = call(
        gram_kernel,
        [((2, D, D), BF), ((TALL, HALF), F32), ((1, 1), F32), ((8, 128), F32)],
        [role, pay.reshape(D, 1152), mom],
        smem=(0,),
        results=(2,),
        flops=2 * 2 * D * D * D,
    )
    gram_other = swap(gram)
    *moms, vec_mom, vec_sec, vec_new, vec_copy = call(
        momenta_kernel,
        [((4, 4, D), F32), ((4, FF), F32), ((16, D), F32)] + [((4, 12), F32)] * 3 + [((4, 12), BF)],
        [
            core, grads, grads_other, factors, vec_master.T, attn_moment, up_moment, down_moment,
            vec_moment.T, vec_second.T,
        ],
        scratch=[pltpu.VMEM((8, FF), F32), pltpu.VMEM((16, D), F32)],
        smem=(0,),
        args=range(4, 10),
        results=range(7),
    )
    gram_other, *moms = lax.optimization_barrier((gram_other, *moms))
    vecs = [t.T for t in (vec_mom, vec_sec, vec_new, vec_copy)]
    (orth,) = call(
        newton_kernel,
        [((4, 2, 8, 1024), BF)],
        [role, plane, matrix, gram, gram_other],
        scratch=[pltpu.VMEM((D, D), F32), pltpu.VMEM((64, D), F32)],
        smem=(0, 1),
        flops=14 * 3 * 2 * D * D * D,
    )
    orth = orth.reshape(8, 8, 1024)
    orth = lax.all_to_all(orth, ("y", "c"), 0, 0, tiled=True)
    news = call(
        update_kernel,
        [((4, 4, D), F32), ((4, FF), F32), ((16, D), F32), ((4, 4, D), BF), ((4, FF), BF), ((16, D), BF)],
        [core, orth, attn_master, up_master, down_master],
        scratch=[pltpu.VMEM((8, FF), F32), pltpu.VMEM((16, D), F32)],
        smem=(0,),
        args=range(2, 5),
        results=range(6),
    )
    return (layer_out, input_grad, clip_norm[0, 0], *moms, *news, *vecs)


def solution(mesh):
    grid = Mesh(mesh.devices.reshape(4, 4, 4, 2), ("x", "z", "y", "c"))
    row, mat, vec = P(ALL, None), P(None, ALL, None), P(None, ALL)
    return jax.shard_map(
        body,
        mesh=grid,
        in_specs=(row, row, row, mat, row, row, vec, mat, row, row, vec, vec),
        out_specs=(row, row, P(), mat, row, row, mat, row, row, mat, row, row, vec, vec, vec, vec),
        check_vma=False,
    )
```

```python
import math

import jax
import jax.numpy as jnp
from jax import lax
from jax.experimental import pallas as pl
from jax.experimental.pallas import tpu as pltpu
from jax.sharding import Mesh, PartitionSpec as P

D = 512
FF = 2048
H = 8
HD = 64
ROW = 128
STEP = 10
NS_ITERS = 5
HALF = 256

MASKED_SCORE = -1e30
NORM_EPSILON = 1e-05
CLIP_LIMIT = 1.0
MOMENTUM_DECAY = 0.95
RATE_MATRIX = 0.5
DECAY_MATRIX = 0.01
BETA_FIRST = 0.9
BETA_SECOND = 0.999
RATE_VECTOR = 0.2
ADAM_EPSILON = 1e-08
NEWTON_FIRST = 3.4445
NEWTON_SECOND = -4.775
NEWTON_THIRD = 2.0315

CHIPS = ("x", "z", "y")
ALL = ("x", "z", "y", "c")
BF = jnp.bfloat16
F32 = jnp.float32
VMEM_LIMIT = 12 * 1024 * 1024


def call(kernel, outs, ins, scratch=(), smem=(), args=(), far=(), results=(), away=(), flops=0, limit=VMEM_LIMIT):
    spec = [
        pl.BlockSpec(memory_space=pltpu.SMEM if i in smem else pl.ANY if i in far else pltpu.VMEM)
        for i in range(len(ins))
    ]
    placed = [
        x if i in smem or i in args
        else pltpu.with_memory_space_constraint(x, pltpu.HBM if i in far else pltpu.VMEM)
        for i, x in enumerate(ins)
    ]
    shapes = [
        jax.ShapeDtypeStruct(s, t) if i in results else pltpu.HBM(s, t) if i in away else pltpu.VMEM(s, t)
        for i, (s, t) in enumerate(outs)
    ]
    moved = sum(math.prod(a.shape) * a.dtype.itemsize for a in ins)
    return pl.pallas_call(
        kernel,
        out_shape=shapes,
        in_specs=spec,
        out_specs=[
            pl.BlockSpec(memory_space=pl.ANY if i in away else pltpu.VMEM) for i in range(len(shapes))
        ],
        scratch_shapes=list(scratch),
        compiler_params=pltpu.CompilerParams(vmem_limit_bytes=limit),
        cost_estimate=pl.CostEstimate(flops=flops, bytes_accessed=moved, transcendentals=0),
    )(*placed)


def dot(a, b):
    return jnp.dot(a, b, preferred_element_type=F32)


def dot_t(a, b):
    return lax.dot_general(a, b, (((1,), (1,)), ((), ())), preferred_element_type=F32)


def dot_in(a, b):
    return lax.dot_general(a, b, (((0,), (0,)), ((), ())), preferred_element_type=F32)


O_LANE, UP_LANE, DOWN_LANE, VEC_LANE, BLOCK = 768, 1024, 2048, 3072, 3200
X0, A0, H0, Z0, ACTS = 0, 512, 1024, 1536, 3328
Y0, DU0, DF0, GRADS = 0, 1024, 2048, 2560


def half_lanes(half, size):
    return pl.ds(pl.multiple_of(half * size, size), size)


def regroup():
    source = lax.broadcasted_iota(jnp.int32, (D, D), 0)
    target = lax.broadcasted_iota(jnp.int32, (D, D), 1)
    return jnp.where(target == (source & 3) * 128 + (source >> 2), 1.0, 0.0).astype(BF)


def pack_kernel(
    core, attn, up, down, vec, attn_m, up_m, down_m, keep, send,
    attn_v, up_v, down_v, vec_v, attn_mv, up_mv, down_mv, full, block, sems,
):
    c = core[0]
    copies = [
        pltpu.make_async_copy(source, target, sems.at[i])
        for i, (source, target) in enumerate(
            [(attn, attn_v), (up, up_v), (down, down_v), (vec, vec_v), (attn_m, attn_mv), (up_m, up_mv), (down_m, down_mv)]
        )
    ]
    for copy in copies:
        copy.start()
    move = regroup()
    for copy in copies:
        copy.wait()
    for first, attn_one, up_one, down_one in ((0, attn_v, up_v, down_v), (4, attn_mv, up_mv, down_mv)):
        rows = slice(first, first + 4)
        for m in range(4):
            full[rows, D * m : D * (m + 1)] = attn_one[m]
        for part in range(4):
            moved = dot(up_one[:, D * part : D * (part + 1)].astype(BF), move)
            for q in range(4):
                lane = FF + D * q + 128 * part
                full[rows, lane : lane + 128] = moved[:, 128 * q : 128 * (q + 1)]
        for i in range(4):
            for q in range(4):
                lane = 2 * FF + D * q
                full[first + i : first + i + 1, lane : lane + D] = down_one[4 * i + q : 4 * i + q + 1, :]
    for target, half in ((keep, c), (send, 1 - c)):
        for m in range(4):
            lanes = pl.ds(pl.multiple_of(D * m + HALF * half, HALF), HALF)
            block[0:4, HALF * m : HALF * (m + 1)] = full[0:4, lanes]
        for m in range(2):
            lanes = pl.ds(pl.multiple_of(2 * D * m + D * half, D), D)
            block[4:8, D * m : D * (m + 1)] = full[4:8, lanes]
        block[:, UP_LANE:DOWN_LANE] = full[:, pl.ds(pl.multiple_of(FF + 1024 * half, 1024), 1024)]
        for q in range(4):
            lanes = pl.ds(pl.multiple_of(2 * FF + D * q + HALF * half, HALF), HALF)
            lane = DOWN_LANE + HALF * q
            block[0:4, lane : lane + HALF] = full[0:4, lanes]
        lanes = pl.ds(pl.multiple_of(2 * FF + 1024 * half, 1024), 1024)
        block[4:8, DOWN_LANE:VEC_LANE] = full[4:8, lanes]
        block[:, VEC_LANE:BLOCK] = jnp.zeros((8, 128), F32)
        block[0:4, VEC_LANE : VEC_LANE + 12] = vec_v[...]
        target[...] = block[...].astype(BF)


def role_lanes(block, note):
    gap = jnp.zeros((8, 512), block.dtype)
    tail = [] if note is None else [note]
    return [
        jnp.concatenate([block[:, 0:512], gap] + tail, axis=1),
        jnp.concatenate([block[:, 512:1024], gap] + tail, axis=1),
        jnp.concatenate([block[:, UP_LANE:DOWN_LANE]] + tail, axis=1),
        jnp.concatenate([block[:, DOWN_LANE:VEC_LANE]] + tail, axis=1),
    ]


def spread_kernel(core, keep, got, message, message_mom):
    mine, other = keep[...].astype(F32), got[...].astype(F32)
    is_left = core[0] == 0
    left, right = jnp.where(is_left, mine, other), jnp.where(is_left, other, mine)
    block = jnp.concatenate([left[0:4], right[0:4]], axis=0).astype(BF)
    moms = role_lanes(jnp.concatenate([left[4:8], right[4:8]], axis=0).astype(BF), None)
    for i in range(64):
        message[i] = block
        message_mom[i] = moms[i % 4]


def by_head(pair):
    low = (lax.broadcasted_iota(jnp.int32, (ROW, ROW), 1) < HD).astype(F32)
    return jnp.concatenate([pair * low.astype(BF), pair * (1.0 - low).astype(BF)], axis=0)


def abreast(stacked):
    return jnp.concatenate([stacked[0:ROW], stacked[ROW:]], axis=1)


def norm_parts(values):
    centred = values - jnp.mean(values, axis=-1, keepdims=True)
    scale = lax.rsqrt(jnp.mean(centred * centred, axis=-1, keepdims=True) + NORM_EPSILON)
    return centred * scale, scale


def norm_back(grad, gain, normed, scale):
    grad = grad * gain
    return scale * (
        grad
        - jnp.mean(grad, axis=-1, keepdims=True)
        - normed * jnp.mean(grad * normed, axis=-1, keepdims=True)
    )


def forward_kernel(
    core, x, w_own, w_far, seg, q_out, k_out, v_out, p_out, vec_out, keep, send, first_out, norm_out, scale_out,
    slope, w_other, wide, pair_scr, acts, sems,
):
    c = core[0]
    copies = []
    for i in range(3):
        lanes = pl.ds(1024 * i, 1024)
        copies.append(pltpu.make_async_copy(w_far.at[:, lanes], w_other.at[:, lanes], sems.at[i]))
        copies[i].start()
    sides = ((c, w_own), (1 - c, w_other))
    vec = w_own[:, VEC_LANE:BLOCK].astype(F32).T[:16]
    vec_out[...] = vec
    moved = dot(vec[8:16].astype(BF), regroup())
    for part in range(4):
        for q in range(4):
            vec_out[8 + q : 9 + q, 128 * part : 128 * (part + 1)] = moved[part : part + 1, 128 * q : 128 * (q + 1)]
    tokens = x[...]
    pair_scr[0] = tokens
    names = jnp.broadcast_to(seg[...].astype(F32), (ROW, ROW))
    gap = names - names.T
    same = jnp.concatenate([gap, gap], axis=0) == 0.0
    for half, w in sides:
        if w is w_other:
            copies[0].wait()
        product = dot(tokens, w[:, 0:O_LANE])
        q = (product[:, 0:HALF] + vec_out[0:1, half_lanes(half, HALF)]).astype(BF)
        k = product[:, HALF : 2 * HALF].astype(BF)
        v = (product[:, 2 * HALF : O_LANE] + vec_out[1:2, half_lanes(half, HALF)]).astype(BF)
        for target, value in ((q_out, q), (k_out, k), (v_out, v)):
            target[:, half_lanes(half, HALF)] = value
        for pair in range(2):
            cols = slice(128 * pair, 128 * pair + 128)
            scores = dot_t(by_head(q[:, cols]), k[:, cols]) * (HD ** (-0.5))
            scores = jnp.where(same, scores, MASKED_SCORE)
            expo = jnp.exp(scores - jnp.max(scores, axis=-1, keepdims=True))
            soft = expo / jnp.sum(expo, axis=-1, keepdims=True)
            p_out[2 * half + pair] = soft
            attended = dot(abreast(soft.astype(BF)), by_head(v[:, cols]))
            lanes = pl.ds(pl.multiple_of(HALF * half + 128 * pair, 128), 128)
            pair_scr[1, :, lanes] = attended.astype(BF)
    for half, w in sides:
        wide[:, half_lanes(half, HALF)] = dot(pair_scr[1], w[:, O_LANE:UP_LANE])
    normed, scale = norm_parts(tokens.astype(F32) + wide[...] + vec[2:3])
    norm_out[...] = normed
    scale_out[...] = scale
    first = normed * vec[4:5] + vec[5:6]
    first_out[...] = first
    first_low = first.astype(BF)
    root = math.sqrt(2.0 / math.pi)
    copies[1].wait()
    for half, w in sides:
        for k in range(2):
            bias = vec_out[pl.ds(8 + 2 * half + k, 1), :]
            u = dot(first_low, w[:, UP_LANE + D * k : UP_LANE + D * (k + 1)]) + bias
            square = u * u
            tanh = jnp.tanh(root * (u + 0.044715 * (square * u)))
            gate = 0.5 * (1.0 + tanh)
            cols = pl.ds(pl.multiple_of(1024 * half + D * k, D), D)
            slope[:, cols] = gate + 0.5 * u * (1.0 - tanh * tanh) * (root * (1.0 + 3 * 0.044715 * square))
            acts[:, cols] = (u * gate).astype(BF)
    for target, half in ((keep, c), (send, 1 - c)):
        target[:, X0:A0] = tokens
        target[:, A0:H0] = pair_scr[half]
        target[:, H0:Z0] = first_low
        target[:, Z0 : Z0 + 1024] = acts[:, half_lanes(half, 1024)]
        target[:, Z0 + 1024 : ACTS] = jnp.zeros((ROW, ACTS - Z0 - 1024), BF)
    copies[2].wait()


def backward_kernel(
    core, x, acts_own, acts_sent, first, vec_in, w_own, w_other, cot, slope, normed_in, scale_in, q_in, k_in, v_in, p_in,
    out, base, y_scr, keep, send, vg, wide, du_scr, df_scr, do_scr,
):
    c = core[0]
    sides = ((c, w_own), (1 - c, w_other))
    vec = vec_in[...]
    dq_scr, dk_scr, dv_scr, da_scr = (y_scr.at[i] for i in range(4))
    for half, w in sides:
        feed = jnp.zeros((ROW, HALF), F32)
        for group, acts in ((c, acts_own), (1 - c, acts_sent)):
            for k in range(2):
                lanes = pl.ds(pl.multiple_of(DOWN_LANE + 2 * HALF * group + HALF * k, HALF), HALF)
                feed = feed + dot(acts[:, Z0 + D * k : Z0 + D * (k + 1)], w[:, lanes])
        wide[:, half_lanes(half, HALF)] = feed
    residual = wide[...] + vec[3:4] + first[...] + x[...].astype(F32)
    normed, scale = norm_parts(residual)
    out[...] = (normed * vec[6:7] + vec[7:8]).astype(BF)
    grad = cot[...].astype(F32)
    vg[...] = jnp.zeros((16, D), F32)
    vg[6:7, :] = jnp.sum(grad * normed, axis=0, keepdims=True)
    vg[7:8, :] = jnp.sum(grad, axis=0, keepdims=True)
    grad2 = norm_back(grad, vec[6:7], normed, scale)
    df_scr[...] = grad2.astype(BF)
    vg[3:4, :] = jnp.sum(df_scr[...].astype(F32), axis=0, keepdims=True)
    for q in range(4):
        lane = DOWN_LANE + HALF * q
        dz = dot_t(df_scr[:, half_lanes(c, HALF)], w_own[:, lane : lane + HALF])
        dz = dz + dot_t(df_scr[:, half_lanes(1 - c, HALF)], w_other[:, lane : lane + HALF])
        du = (dz * slope[:, D * q : D * (q + 1)]).astype(BF)
        du_scr[:, D * q : D * (q + 1)] = du
        vg[8 + q : 9 + q, :] = jnp.sum(du.astype(F32), axis=0, keepdims=True)
    dfirst = grad2
    for half, w in sides:
        dfirst = dfirst + dot_t(du_scr[:, half_lanes(half, 1024)], w[:, UP_LANE:DOWN_LANE])
    normed1 = normed_in[...]
    vg[4:5, :] = jnp.sum(dfirst * normed1, axis=0, keepdims=True)
    vg[5:6, :] = jnp.sum(dfirst, axis=0, keepdims=True)
    dres = norm_back(dfirst, vec[4:5], normed1, scale_in[...])
    da_scr[...] = dres.astype(BF)
    vg[2:3, :] = jnp.sum(da_scr[...].astype(F32), axis=0, keepdims=True)
    dattended = jnp.zeros((ROW, D), F32)
    for half, w in sides:
        dattended = dattended + dot_t(da_scr[:, half_lanes(half, HALF)], w[:, O_LANE:UP_LANE])
    do_scr[...] = dattended.astype(BF)
    share = HD ** (-0.5)
    pairs = [slice(128 * pair, 128 * pair + 128) for pair in range(H // 2)]
    dos = [by_head(do_scr[:, cols]) for cols in pairs]
    dsofts = [dot_t(do, v_in[:, cols]) for do, cols in zip(dos, pairs)]
    dss = []
    for pair, dsoft in enumerate(dsofts):
        soft = p_in[pair]
        dss.append((soft * (dsoft - jnp.sum(soft * dsoft, axis=-1, keepdims=True))).astype(BF))
    for pair, cols in enumerate(pairs):
        ds = dss[pair]
        dq_scr[:, cols] = (dot(abreast(ds), by_head(k_in[:, cols])) * share).astype(BF)
        dk_scr[:, cols] = (dot_in(ds, by_head(q_in[:, cols])) * share).astype(BF)
        dv_scr[:, cols] = dot_in(p_in[pair].astype(BF), dos[pair]).astype(BF)
    vg[0:1, :] = jnp.sum(dq_scr[...].astype(F32), axis=0, keepdims=True)
    vg[1:2, :] = jnp.sum(dv_scr[...].astype(F32), axis=0, keepdims=True)
    for target, half in ((keep, c), (send, 1 - c)):
        target[:, 0:D] = y_scr[half]
        target[:, D : 2 * D] = y_scr[2 + half]
        target[:, DU0:DF0] = du_scr[:, half_lanes(half, 1024)]
        target[:, DF0:GRADS] = df_scr[...]
    base[...] = grad2 + dres


def input_kernel(core, base, grads, w_own, w_other, out):
    total = base[...]
    for half, w in ((core[0], w_own), (1 - core[0], w_other)):
        for i in range(3):
            total = total + dot_t(grads[i, :, half_lanes(half, HALF)], w[:, HALF * i : HALF * (i + 1)])
    out[...] = total.astype(BF)


def weights_kernel(acts, acts_other, keep, got, vg, vg_other, out, vec):
    def both(one, two, first, last):
        return jnp.concatenate([one[:, first:last], two[:, first:last]], axis=0)

    out[:, UP_LANE:DOWN_LANE] = dot_in(both(acts, acts_other, H0, Z0), both(keep, got, DU0, DF0)).astype(BF)
    down = both(keep, got, DF0, GRADS)
    for k in range(2):
        lane = DOWN_LANE + D * k
        units = both(acts, acts_other, Z0 + D * k, Z0 + D * (k + 1))
        out[:, lane : lane + D] = dot_in(units, down).astype(BF)
    for k in range(2):
        left = both(acts, acts_other, D * k, D * (k + 1))
        out[:, D * k : D * (k + 1)] = dot_in(left, both(keep, got, D * k, D * (k + 1))).astype(BF)
    total = vg[...] + vg_other[...]
    vec[...] = jnp.zeros((128, D), F32)
    vec[0:8, :] = total[0:8]
    for part in range(4):
        for q in range(4):
            vec[8 + part : 9 + part, 128 * q : 128 * (q + 1)] = total[8 + q : 9 + q, 128 * part : 128 * (part + 1)]
    vec[8:16, :] = dot_t(vec[8:16, :].astype(BF), regroup())
    out[:, VEC_LANE:BLOCK] = vec[...].T.astype(BF)


def add_up(ref):
    total = ref[0].astype(F32)
    for i in range(1, 64):
        total = total + ref[i].astype(F32)
    return total


def split3(value):
    one = value.astype(BF)
    rest = value - one.astype(F32)
    two = rest.astype(BF)
    three = (rest - two.astype(F32)).astype(BF)
    return one, two, three


def reduce_kernel(got, grads):
    grads[...] = add_up(got)


def pay_kernel(grads, grads_other, pay):
    vec = grads[:, VEC_LANE:BLOCK]
    own, other = grads[:, 0:VEC_LANE], grads_other[:, 0:VEC_LANE]
    square = (jnp.sum(own * own) + jnp.sum(other * other)) + jnp.sum(vec * vec)
    row = lax.broadcasted_iota(jnp.int32, (8, 128), 0)
    lane = lax.broadcasted_iota(jnp.int32, (8, 128), 1)
    full = jnp.full((8, 128), square, F32)
    one, two, three = split3(full)
    note = jnp.where(lane == 0, one.astype(F32), jnp.where(lane == 1, two.astype(F32), three.astype(F32)))
    note = jnp.where((row == 0) & (lane < 3), note, 0.0).astype(BF)
    rows = role_lanes(grads[:, 0:VEC_LANE].astype(BF), note)
    for i in range(64):
        pay[i] = rows[i % 4]


def halves(value):
    high = value.astype(BF)
    return high, (value - high.astype(F32)).astype(BF)


def fine(a, b):
    ah, al = a
    bh, bl = b
    return dot(jnp.concatenate([ah, ah, al], axis=1), jnp.concatenate([bh, bl, bh], axis=0))


TALL = 3 * HALF + 8


def near_kernel(far, near, sem):
    copy = pltpu.make_async_copy(far, near, sem)
    copy.start()
    copy.wait()


def gram_kernel(role_ref, got, mom, matrix, gram, clip_out, factor_out):
    role = role_ref[0]
    clip = jnp.sqrt(jnp.full((8, 128), jnp.sum(got[:, 1024:1152].astype(F32)), F32))
    factors = CLIP_LIMIT / jnp.maximum(clip, CLIP_LIMIT)
    clip_out[...] = clip[0:1, 0:1]
    factor_out[...] = factors
    factor = factors[0:1, 0:1]

    def make(k):
        cols = slice(D * k, D * (k + 1))
        value = MOMENTUM_DECAY * mom[:, cols].astype(F32) + factor * got[:, cols].astype(F32)
        value = value.astype(BF)
        matrix[k] = value
        value = value.astype(F32)
        return jnp.sum(value * value)

    def finish(product, parts, square):
        for i, (a, b) in enumerate(((0, 0), (0, 1), (1, 1))):
            total = product(a, b, 0)
            for k in range(1, parts):
                total = total + product(a, b, k)
            gram[HALF * i : HALF * (i + 1), :] = total
        gram[3 * HALF : TALL, :] = jnp.full((8, HALF), square, F32)

    def inner(a, b, k):
        return dot_in(matrix[k, :, HALF * a : HALF * (a + 1)], matrix[k, :, HALF * b : HALF * (b + 1)])

    def outer(a, b, k):
        return dot_t(matrix[k, HALF * a : HALF * (a + 1), :], matrix[k, HALF * b : HALF * (b + 1), :])

    @pl.when(role < 2)
    def _():
        square = make(0)
        finish(inner, 1, square)

    @pl.when(role == 2)
    def _():
        square = make(0) + make(1)
        finish(outer, 2, square)

    @pl.when(role == 3)
    def _():
        square = make(0) + make(1)
        finish(inner, 2, square)


def newton_kernel(role_ref, plane_ref, matrix, gram_own, gram_other, out, gram, rows_scr):
    role, plane = role_ref[0], plane_ref[0]
    chips = pl.ds(pl.multiple_of(plane * 32, 32), 32)

    def scaled(total):
        size = jnp.sqrt(total[3 * HALF : 3 * HALF + 1, 0:1]) + 1e-07
        inverse = 1.0 / size
        total = total[0 : 3 * HALF] * (inverse * inverse)
        gram[0:HALF, 0:HALF] = total[0:HALF]
        gram[0:HALF, HALF:D] = total[HALF:D]
        gram[HALF:D, 0:HALF] = total[HALF:D].T
        gram[HALF:D, HALF:D] = total[D : 3 * HALF]
        return inverse

    def rows_of(k):
        return matrix[k, chips, :].astype(F32)

    @pl.when(role < 2)
    def _():
        inverse = scaled(gram_own[...])
        rows_scr[0:32, :] = rows_of(0) * inverse
        rows_scr[32:64, :] = jnp.zeros((32, D), F32)

    @pl.when(role == 2)
    def _():
        inverse = scaled(gram_own[...] + gram_other[...])
        here = lax.broadcasted_iota(jnp.int32, (32, D), 0) + 32 * plane
        there = lax.broadcasted_iota(jnp.int32, (32, D), 1)
        rows_scr[0:32, :] = jnp.where(here == there, 1.0, 0.0) * inverse
        rows_scr[32:64, :] = jnp.zeros((32, D), F32)

    @pl.when(role == 3)
    def _():
        inverse = scaled(gram_own[...] + gram_other[...])
        for k in range(2):
            rows_scr[32 * k : 32 * (k + 1), :] = rows_of(k) * inverse

    diagonal = (
        lax.broadcasted_iota(jnp.int32, (D, D), 0) == lax.broadcasted_iota(jnp.int32, (D, D), 1)
    )

    def turn(exact):
        own = halves(gram[...])
        square = fine(own, own) if exact else dot(own[0], own[0])
        poly = NEWTON_SECOND * gram[...] + NEWTON_THIRD * square
        poly = halves(jnp.where(diagonal, poly + NEWTON_FIRST, poly))
        pairs = zip(halves(fine(poly, own)), halves(rows_scr[...]))
        both = fine(tuple(jnp.concatenate(pair, axis=0) for pair in pairs), poly)
        gram[...] = both[0:D]
        rows_scr[...] = both[D:]

    pl.loop(0, NS_ITERS - 2)(lambda _: turn(False))
    turn(True)
    own = halves(gram[...])
    rows = rows_scr[...]
    once = fine(halves(rows), own)
    twice = fine(halves(once), own)
    rows_scr[...] = NEWTON_FIRST * rows + NEWTON_SECOND * once + NEWTON_THIRD * twice

    def send(k, value):
        value = value.astype(BF).reshape(4, 8, D)
        out[:, 0, :, D * k : D * (k + 1)] = value
        out[:, 1, :, D * k : D * (k + 1)] = value

    @pl.when(role == 2)
    def _():
        high, low = halves(rows_scr[0:32, :])
        for k in range(2):
            send(k, dot(high, matrix[k]) + dot(low, matrix[k]))

    @pl.when(role != 2)
    def _():
        for k in range(2):
            send(k, rows_scr[32 * k : 32 * (k + 1), :])


def rows4(is_left, value):
    return jnp.where(is_left, value[0:4], value[4:8])


def natural(ups, move, part):
    pieces = [ups[:, D * q + 128 * part : D * q + 128 * (part + 1)] for q in range(4)]
    return dot_t(jnp.concatenate(pieces, axis=1).astype(BF), move)


def momenta_kernel(
    core, grads, grads_other, factors, vec, attn_m, up_m, down_m, vec_m, vec_s,
    attn_mom, up_mom, down_mom, vec_mom, vec_sec, vec_new, vec_copy, ups, downs,
):
    is_left = core[0] == 0
    factor = factors[0:1, 0:1]

    def both(first, last):
        mine, other = grads[:, first:last], grads_other[:, first:last]
        left = jnp.where(is_left, mine, other)
        right = jnp.where(is_left, other, mine)
        return rows4(is_left, left), rows4(is_left, right)

    pairs = [both(D * k, D * (k + 1)) for k in range(2)]
    for m in range(4):
        attn_mom[m] = MOMENTUM_DECAY * attn_m[m] + factor * pairs[m // 2][m % 2]
    move = regroup()
    high, low = halves(jnp.concatenate(both(UP_LANE, DOWN_LANE), axis=1))
    ups[0:4, :] = high.astype(F32)
    ups[4:8, :] = low.astype(F32)
    for part in range(4):
        moved = natural(ups, move, part)
        cols = slice(D * part, D * (part + 1))
        up_mom[:, cols] = MOMENTUM_DECAY * up_m[:, cols] + factor * (moved[0:4] + moved[4:8])
    sides = both(DOWN_LANE, VEC_LANE)
    for q in range(4):
        grad = sides[q // 2][:, D * (q % 2) : D * (q % 2 + 1)]
        for i in range(4):
            downs[4 * i + q : 4 * i + q + 1, :] = grad[i : i + 1]
    down_mom[...] = MOMENTUM_DECAY * down_m[...] + factor * downs[...]
    clipped = factor * rows4(is_left, grads[:, VEC_LANE:BLOCK])[:, 0:12]
    first = BETA_FIRST * vec_m[...] + (1.0 - BETA_FIRST) * clipped
    second = BETA_SECOND * vec_s[...] + (1.0 - BETA_SECOND) * clipped * clipped
    vec_mom[...] = first
    vec_sec[...] = second
    first_hat = first / (1.0 - BETA_FIRST**STEP)
    second_hat = second / (1.0 - BETA_SECOND**STEP)
    new = vec[...] - RATE_VECTOR * first_hat / (jnp.sqrt(second_hat) + ADAM_EPSILON)
    vec_new[...] = new
    vec_copy[...] = new.astype(BF)


def update_kernel(
    core, got, attn, up, down, attn_new, up_new, down_new, attn_copy, up_copy, down_copy, ups, downs
):
    is_left = core[0] == 0
    keep_share = 1.0 - RATE_MATRIX * DECAY_MATRIX
    for m in range(4):
        new = attn[m] * keep_share - RATE_MATRIX * rows4(is_left, got[m, :, 0:512].astype(F32))
        attn_new[m] = new
        attn_copy[m] = new.astype(BF)
    move = regroup()
    ups[0:4, :] = rows4(is_left, jnp.concatenate([got[4].astype(F32), got[5].astype(F32)], axis=1))
    ups[4:8, :] = jnp.zeros((4, FF), F32)
    rate = RATE_MATRIX * math.sqrt(max(1.0, FF / D))
    for part in range(4):
        cols = slice(D * part, D * (part + 1))
        up_new[:, cols] = up[:, cols] * keep_share - rate * natural(ups, move, part)[0:4]
    up_copy[...] = up_new[...].astype(BF)
    rate = RATE_MATRIX * math.sqrt(max(1.0, D / FF))
    for q in range(4):
        step = rows4(is_left, got[6 + q // 2, :, D * (q % 2) : D * (q % 2 + 1)].astype(F32))
        for i in range(4):
            downs[4 * i + q : 4 * i + q + 1, :] = step[i : i + 1]
    down_new[...] = down[...] * keep_share - rate * downs[...]
    down_copy[...] = down_new[...].astype(BF)


def swap(value):
    return lax.ppermute(value, "c", [(0, 1), (1, 0)])


def to_chips(value):
    return lax.all_to_all(value, CHIPS, 0, 0, tiled=True)


def body(
    block_input, cotangent, segment_ids, attn_master, up_master, down_master, vec_master,
    attn_moment, up_moment, down_moment, vec_moment, vec_second,
):
    c = lax.axis_index("c")
    core = c.reshape(1).astype(jnp.int32)
    role = lax.axis_index("y").reshape(1).astype(jnp.int32)
    plane = (lax.axis_index("x") * 4 + lax.axis_index("z")).reshape(1).astype(jnp.int32)
    core, role, plane = lax.optimization_barrier((core, role, plane))

    keep, send = call(
        pack_kernel,
        [((8, BLOCK), BF)] * 2,
        [core, attn_master, up_master, down_master, vec_master.T, attn_moment, up_moment, down_moment],
        scratch=[
            pltpu.VMEM((4, 4, D), F32), pltpu.VMEM((4, FF), F32), pltpu.VMEM((16, D), F32), pltpu.VMEM((4, 12), F32),
            pltpu.VMEM((4, 4, D), F32), pltpu.VMEM((4, FF), F32), pltpu.VMEM((16, D), F32),
            pltpu.VMEM((8, 3 * FF), F32), pltpu.VMEM((8, BLOCK), F32), pltpu.SemaphoreType.DMA((7,)),
        ],
        smem=(0,),
        far=range(1, 8),
    )
    message, message_mom = call(
        spread_kernel, [((64, 8, BLOCK), BF), ((64, 8, 1024), BF)], [core, keep, swap(send)], smem=(0,)
    )
    own = to_chips(message)
    own, message_mom = lax.optimization_barrier((own, message_mom))
    other = swap(own)
    mom = to_chips(message_mom).reshape(D, 1024)
    own, other = own.reshape(D, BLOCK), other.reshape(D, BLOCK)
    q, k, v, soft, vec, acts_own, acts_sent, first, normed, scale, slope, other = call(
        forward_kernel,
        [((ROW, D), BF)] * 3
        + [((H // 2, 2 * ROW, ROW), F32), ((16, D), F32), ((ROW, ACTS), BF), ((ROW, ACTS), BF)]
        + [((ROW, D), F32), ((ROW, D), F32), ((ROW, 1), F32), ((ROW, FF), F32), ((D, 3072), BF)],
        [core, block_input, own, other, segment_ids],
        scratch=[
            pltpu.VMEM((ROW, D), F32), pltpu.VMEM((2, ROW, D), BF), pltpu.VMEM((ROW, FF), BF),
            pltpu.SemaphoreType.DMA((3,)),
        ],
        smem=(0,),
        args=(1, 4),
        far=(3,),
        flops=8 * 2 * ROW * D * D,
    )
    acts_other = swap(acts_sent)
    layer_out, base, ygrads, keep, send, vg = call(
        backward_kernel,
        [((ROW, D), BF), ((ROW, D), F32), ((4, ROW, D), BF), ((ROW, GRADS), BF), ((ROW, GRADS), BF), ((16, D), F32)],
        [
            core, block_input, acts_own, acts_sent, first, vec, own, other, cotangent, slope, normed, scale,
            q, k, v, soft,
        ],
        scratch=[
            pltpu.VMEM((ROW, D), F32), pltpu.VMEM((ROW, FF), BF), pltpu.VMEM((ROW, D), BF), pltpu.VMEM((ROW, D), BF),
        ],
        smem=(0,),
        args=(1, 8),
        results=(0,),
        flops=18 * 2 * ROW * D * D,
    )
    got, vg_other = swap(send), swap(vg)
    (input_grad,) = call(
        input_kernel,
        [((ROW, D), BF)],
        [core, base, ygrads, own, other],
        smem=(0,),
        results=(0,),
        flops=3 * 2 * ROW * D * D,
    )
    got, input_grad = lax.optimization_barrier((got, input_grad))
    (weights,) = call(
        weights_kernel,
        [((D, BLOCK), BF)],
        [acts_own, acts_other, keep, got, vg, vg_other],
        scratch=[pltpu.VMEM((128, D), F32)],
        flops=2 * 256 * 512 * 3072,
    )
    weights, mom = lax.optimization_barrier((weights, mom))
    weights = to_chips(weights.reshape(64, 8, BLOCK))
    (grads,) = call(reduce_kernel, [((8, BLOCK), F32)], [weights])
    grads, mom = lax.optimization_barrier((grads, mom))
    grads_other = swap(grads)
    (mom,) = call(near_kernel, [((D, 1024), BF)], [mom], scratch=[pltpu.SemaphoreType.DMA], far=(0,))
    (pay,) = call(pay_kernel, [((64, 8, 1152), BF)], [grads, grads_other])
    pay, mom = lax.optimization_barrier((pay, mom))
    pay = to_chips(pay)
    matrix, gram, clip_norm, factors = call(
        gram_kernel,
        [((2, D, D), BF), ((TALL, HALF), F32), ((1, 1), F32), ((8, 128), F32)],
        [role, pay.reshape(D, 1152), mom],
        smem=(0,),
        results=(2,),
        flops=2 * 2 * D * D * D,
    )
    gram_other = swap(gram)
    *moms, vec_mom, vec_sec, vec_new, vec_copy = call(
        momenta_kernel,
        [((4, 4, D), F32), ((4, FF), F32), ((16, D), F32)] + [((4, 12), F32)] * 3 + [((4, 12), BF)],
        [
            core, grads, grads_other, factors, vec_master.T, attn_moment, up_moment, down_moment,
            vec_moment.T, vec_second.T,
        ],
        scratch=[pltpu.VMEM((8, FF), F32), pltpu.VMEM((16, D), F32)],
        smem=(0,),
        args=range(4, 10),
        results=range(7),
    )
    gram_other, *moms = lax.optimization_barrier((gram_other, *moms))
    vecs = [t.T for t in (vec_mom, vec_sec, vec_new, vec_copy)]
    (orth,) = call(
        newton_kernel,
        [((4, 2, 8, 1024), BF)],
        [role, plane, matrix, gram, gram_other],
        scratch=[pltpu.VMEM((D, D), F32), pltpu.VMEM((64, D), F32)],
        smem=(0, 1),
        flops=14 * 3 * 2 * D * D * D,
    )
    orth = orth.reshape(8, 8, 1024)
    orth = lax.all_to_all(orth, ("y", "c"), 0, 0, tiled=True)
    news = call(
        update_kernel,
        [((4, 4, D), F32), ((4, FF), F32), ((16, D), F32), ((4, 4, D), BF), ((4, FF), BF), ((16, D), BF)],
        [core, orth, attn_master, up_master, down_master],
        scratch=[pltpu.VMEM((8, FF), F32), pltpu.VMEM((16, D), F32)],
        smem=(0,),
        args=range(2, 5),
        results=range(6),
    )
    return (layer_out, input_grad, clip_norm[0, 0], *moms, *news, *vecs)


def solution(mesh):
    grid = Mesh(mesh.devices.reshape(4, 4, 4, 2), ("x", "z", "y", "c"))
    row, mat, vec = P(ALL, None), P(None, ALL, None), P(None, ALL)
    return jax.shard_map(
        body,
        mesh=grid,
        in_specs=(row, row, row, mat, row, row, vec, mat, row, row, vec, vec),
        out_specs=(row, row, P(), mat, row, row, mat, row, row, mat, row, row, vec, vec, vec, vec),
        check_vma=False,
    )
```

```python
import math

import jax
import jax.numpy as jnp
from jax import lax
from jax.experimental import pallas as pl
from jax.experimental.pallas import tpu as pltpu
from jax.sharding import Mesh, PartitionSpec as P

D = 512
FF = 2048
H = 8
HD = 64
ROW = 128
STEP = 10
NS_ITERS = 5
HALF = 256

MASKED_SCORE = -1e30
NORM_EPSILON = 1e-05
CLIP_LIMIT = 1.0
MOMENTUM_DECAY = 0.95
RATE_MATRIX = 0.5
DECAY_MATRIX = 0.01
BETA_FIRST = 0.9
BETA_SECOND = 0.999
RATE_VECTOR = 0.2
ADAM_EPSILON = 1e-08
NEWTON_FIRST = 3.4445
NEWTON_SECOND = -4.775
NEWTON_THIRD = 2.0315

CHIPS = ("x", "z", "y")
ALL = ("x", "z", "y", "c")
BF = jnp.bfloat16
F32 = jnp.float32
VMEM_LIMIT = 12 * 1024 * 1024


def call(kernel, outs, ins, scratch=(), smem=(), args=(), far=(), results=(), away=(), flops=0, limit=VMEM_LIMIT):
    spec = [
        pl.BlockSpec(memory_space=pltpu.SMEM if i in smem else pl.ANY if i in far else pltpu.VMEM)
        for i in range(len(ins))
    ]
    placed = [
        x if i in smem or i in args
        else pltpu.with_memory_space_constraint(x, pltpu.HBM if i in far else pltpu.VMEM)
        for i, x in enumerate(ins)
    ]
    shapes = [
        jax.ShapeDtypeStruct(s, t) if i in results else pltpu.HBM(s, t) if i in away else pltpu.VMEM(s, t)
        for i, (s, t) in enumerate(outs)
    ]
    moved = sum(math.prod(a.shape) * a.dtype.itemsize for a in ins)
    return pl.pallas_call(
        kernel,
        out_shape=shapes,
        in_specs=spec,
        out_specs=[
            pl.BlockSpec(memory_space=pl.ANY if i in away else pltpu.VMEM) for i in range(len(shapes))
        ],
        scratch_shapes=list(scratch),
        compiler_params=pltpu.CompilerParams(vmem_limit_bytes=limit),
        cost_estimate=pl.CostEstimate(flops=flops, bytes_accessed=moved, transcendentals=0),
    )(*placed)


def dot(a, b):
    return jnp.dot(a, b, preferred_element_type=F32)


def dot_t(a, b):
    return lax.dot_general(a, b, (((1,), (1,)), ((), ())), preferred_element_type=F32)


def dot_in(a, b):
    return lax.dot_general(a, b, (((0,), (0,)), ((), ())), preferred_element_type=F32)


O_LANE, UP_LANE, DOWN_LANE, VEC_LANE, BLOCK = 768, 1024, 2048, 3072, 3200
X0, A0, H0, Z0, ACTS = 0, 512, 1024, 1536, 3328
Y0, DU0, DF0, GRADS = 0, 1024, 2048, 2560


def half_lanes(half, size):
    return pl.ds(pl.multiple_of(half * size, size), size)


def regroup():
    source = lax.broadcasted_iota(jnp.int32, (D, D), 0)
    target = lax.broadcasted_iota(jnp.int32, (D, D), 1)
    return jnp.where(target == (source & 3) * 128 + (source >> 2), 1.0, 0.0).astype(BF)


def pack_kernel(
    core, attn, up, down, vec, attn_m, up_m, down_m, keep, send,
    attn_v, up_v, down_v, vec_v, attn_mv, up_mv, down_mv, full, block, stage, sems,
):
    c = core[0]
    copies = [
        pltpu.make_async_copy(source, target, sems.at[i])
        for i, (source, target) in enumerate(
            [(attn, attn_v), (up, up_v), (down, down_v), (vec, vec_v), (attn_m, attn_mv), (up_m, up_mv), (down_m, down_mv)]
        )
    ]
    for copy in copies:
        copy.start()
    move = regroup()
    for copy in copies:
        copy.wait()
    for first, attn_one, up_one, down_one in ((0, attn_v, up_v, down_v), (4, attn_mv, up_mv, down_mv)):
        rows = slice(first, first + 4)
        for m in range(4):
            full[rows, D * m : D * (m + 1)] = attn_one[m]
        for part in range(4):
            row = 8 * part + first
            stage[row : row + 4, :] = up_one[:, D * part : D * (part + 1)]
        for i in range(4):
            for q in range(4):
                lane = 2 * FF + D * q
                full[first + i : first + i + 1, lane : lane + D] = down_one[4 * i + q : 4 * i + q + 1, :]
    moved = dot(stage[...].astype(BF), move)
    for part in range(4):
        for q in range(4):
            lane = FF + D * q + 128 * part
            full[:, lane : lane + 128] = moved[8 * part : 8 * (part + 1), 128 * q : 128 * (q + 1)]
    for target, half in ((keep, c), (send, 1 - c)):
        for m in range(4):
            lanes = pl.ds(pl.multiple_of(D * m + HALF * half, HALF), HALF)
            block[0:4, HALF * m : HALF * (m + 1)] = full[0:4, lanes]
        for m in range(2):
            lanes = pl.ds(pl.multiple_of(2 * D * m + D * half, D), D)
            block[4:8, D * m : D * (m + 1)] = full[4:8, lanes]
        block[:, UP_LANE:DOWN_LANE] = full[:, pl.ds(pl.multiple_of(FF + 1024 * half, 1024), 1024)]
        for q in range(4):
            lanes = pl.ds(pl.multiple_of(2 * FF + D * q + HALF * half, HALF), HALF)
            lane = DOWN_LANE + HALF * q
            block[0:4, lane : lane + HALF] = full[0:4, lanes]
        lanes = pl.ds(pl.multiple_of(2 * FF + 1024 * half, 1024), 1024)
        block[4:8, DOWN_LANE:VEC_LANE] = full[4:8, lanes]
        block[:, VEC_LANE:BLOCK] = jnp.zeros((8, 128), F32)
        block[0:4, VEC_LANE : VEC_LANE + 12] = vec_v[...]
        target[...] = block[...].astype(BF)


def role_lanes(block, note):
    gap = jnp.zeros((8, 512), block.dtype)
    tail = [] if note is None else [note]
    return [
        jnp.concatenate([block[:, 0:512], gap] + tail, axis=1),
        jnp.concatenate([block[:, 512:1024], gap] + tail, axis=1),
        jnp.concatenate([block[:, UP_LANE:DOWN_LANE]] + tail, axis=1),
        jnp.concatenate([block[:, DOWN_LANE:VEC_LANE]] + tail, axis=1),
    ]


def spread_kernel(core, keep, got, message, message_mom):
    mine, other = keep[...].astype(F32), got[...].astype(F32)
    is_left = core[0] == 0
    left, right = jnp.where(is_left, mine, other), jnp.where(is_left, other, mine)
    block = jnp.concatenate([left[0:4], right[0:4]], axis=0).astype(BF)
    moms = role_lanes(jnp.concatenate([left[4:8], right[4:8]], axis=0).astype(BF), None)
    for i in range(64):
        message[i] = block
        message_mom[i] = moms[i % 4]


def by_head(pair):
    low = (lax.broadcasted_iota(jnp.int32, (ROW, ROW), 1) < HD).astype(F32)
    return jnp.concatenate([pair * low.astype(BF), pair * (1.0 - low).astype(BF)], axis=0)


def abreast(stacked):
    return jnp.concatenate([stacked[0:ROW], stacked[ROW:]], axis=1)


def norm_parts(values):
    centred = values - jnp.mean(values, axis=-1, keepdims=True)
    scale = lax.rsqrt(jnp.mean(centred * centred, axis=-1, keepdims=True) + NORM_EPSILON)
    return centred * scale, scale


def norm_back(grad, gain, normed, scale):
    grad = grad * gain
    return scale * (
        grad
        - jnp.mean(grad, axis=-1, keepdims=True)
        - normed * jnp.mean(grad * normed, axis=-1, keepdims=True)
    )


def forward_kernel(
    core, x, w_own, w_far, seg, q_out, k_out, v_out, p_out, vec_out, keep, send, first_out, norm_out, scale_out,
    slope, w_other, wide, pair_scr, acts, sems,
):
    c = core[0]
    copies = []
    for i in range(3):
        lanes = pl.ds(1024 * i, 1024)
        copies.append(pltpu.make_async_copy(w_far.at[:, lanes], w_other.at[:, lanes], sems.at[i]))
        copies[i].start()
    sides = ((c, w_own), (1 - c, w_other))
    vec = w_own[:, VEC_LANE:BLOCK].astype(F32).T[:16]
    vec_out[...] = vec
    moved = dot(vec[8:16].astype(BF), regroup())
    for part in range(4):
        for q in range(4):
            vec_out[8 + q : 9 + q, 128 * part : 128 * (part + 1)] = moved[part : part + 1, 128 * q : 128 * (q + 1)]
    tokens = x[...]
    pair_scr[0] = tokens
    names = jnp.broadcast_to(seg[...].astype(F32), (ROW, ROW))
    gap = names - names.T
    same = jnp.concatenate([gap, gap], axis=0) == 0.0
    for half, w in sides:
        if w is w_other:
            copies[0].wait()
        product = dot(tokens, w[:, 0:O_LANE])
        q = (product[:, 0:HALF] + vec_out[0:1, half_lanes(half, HALF)]).astype(BF)
        k = product[:, HALF : 2 * HALF].astype(BF)
        v = (product[:, 2 * HALF : O_LANE] + vec_out[1:2, half_lanes(half, HALF)]).astype(BF)
        for target, value in ((q_out, q), (k_out, k), (v_out, v)):
            target[:, half_lanes(half, HALF)] = value
        for pair in range(2):
            cols = slice(128 * pair, 128 * pair + 128)
            scores = dot_t(by_head(q[:, cols]), k[:, cols]) * (HD ** (-0.5))
            scores = jnp.where(same, scores, MASKED_SCORE)
            expo = jnp.exp(scores - jnp.max(scores, axis=-1, keepdims=True))
            soft = expo / jnp.sum(expo, axis=-1, keepdims=True)
            p_out[2 * half + pair] = soft
            attended = dot(abreast(soft.astype(BF)), by_head(v[:, cols]))
            lanes = pl.ds(pl.multiple_of(HALF * half + 128 * pair, 128), 128)
            pair_scr[1, :, lanes] = attended.astype(BF)
    for half, w in sides:
        wide[:, half_lanes(half, HALF)] = dot(pair_scr[1], w[:, O_LANE:UP_LANE])
    normed, scale = norm_parts(tokens.astype(F32) + wide[...] + vec[2:3])
    norm_out[...] = normed
    scale_out[...] = scale
    first = normed * vec[4:5] + vec[5:6]
    first_out[...] = first
    first_low = first.astype(BF)
    root = math.sqrt(2.0 / math.pi)
    copies[1].wait()
    for half, w in sides:
        for k in range(2):
            bias = vec_out[pl.ds(8 + 2 * half + k, 1), :]
            u = dot(first_low, w[:, UP_LANE + D * k : UP_LANE + D * (k + 1)]) + bias
            square = u * u
            tanh = jnp.tanh(root * (u + 0.044715 * (square * u)))
            gate = 0.5 * (1.0 + tanh)
            cols = pl.ds(pl.multiple_of(1024 * half + D * k, D), D)
            slope[:, cols] = gate + 0.5 * u * (1.0 - tanh * tanh) * (root * (1.0 + 3 * 0.044715 * square))
            acts[:, cols] = (u * gate).astype(BF)
    for target, half in ((keep, c), (send, 1 - c)):
        target[:, X0:A0] = tokens
        target[:, A0:H0] = pair_scr[half]
        target[:, H0:Z0] = first_low
        target[:, Z0 : Z0 + 1024] = acts[:, half_lanes(half, 1024)]
        target[:, Z0 + 1024 : ACTS] = jnp.zeros((ROW, ACTS - Z0 - 1024), BF)
    copies[2].wait()


def backward_kernel(
    core, x, acts_own, acts_sent, first, vec_in, w_own, w_other, cot, slope, normed_in, scale_in, q_in, k_in, v_in, p_in,
    out, base, y_scr, keep, send, vg, wide, du_scr, df_scr, do_scr,
):
    c = core[0]
    sides = ((c, w_own), (1 - c, w_other))
    vec = vec_in[...]
    dq_scr, dk_scr, dv_scr, da_scr = (y_scr.at[i] for i in range(4))
    for half, w in sides:
        feed = jnp.zeros((ROW, HALF), F32)
        for group, acts in ((c, acts_own), (1 - c, acts_sent)):
            for k in range(2):
                lanes = pl.ds(pl.multiple_of(DOWN_LANE + 2 * HALF * group + HALF * k, HALF), HALF)
                feed = feed + dot(acts[:, Z0 + D * k : Z0 + D * (k + 1)], w[:, lanes])
        wide[:, half_lanes(half, HALF)] = feed
    residual = wide[...] + vec[3:4] + first[...] + x[...].astype(F32)
    normed, scale = norm_parts(residual)
    out[...] = (normed * vec[6:7] + vec[7:8]).astype(BF)
    grad = cot[...].astype(F32)
    vg[...] = jnp.zeros((16, D), F32)
    vg[6:7, :] = jnp.sum(grad * normed, axis=0, keepdims=True)
    vg[7:8, :] = jnp.sum(grad, axis=0, keepdims=True)
    grad2 = norm_back(grad, vec[6:7], normed, scale)
    df_scr[...] = grad2.astype(BF)
    vg[3:4, :] = jnp.sum(df_scr[...].astype(F32), axis=0, keepdims=True)
    for q in range(4):
        lane = DOWN_LANE + HALF * q
        dz = dot_t(df_scr[:, half_lanes(c, HALF)], w_own[:, lane : lane + HALF])
        dz = dz + dot_t(df_scr[:, half_lanes(1 - c, HALF)], w_other[:, lane : lane + HALF])
        du = (dz * slope[:, D * q : D * (q + 1)]).astype(BF)
        du_scr[:, D * q : D * (q + 1)] = du
        vg[8 + q : 9 + q, :] = jnp.sum(du.astype(F32), axis=0, keepdims=True)
    dfirst = grad2
    for half, w in sides:
        dfirst = dfirst + dot_t(du_scr[:, half_lanes(half, 1024)], w[:, UP_LANE:DOWN_LANE])
    normed1 = normed_in[...]
    vg[4:5, :] = jnp.sum(dfirst * normed1, axis=0, keepdims=True)
    vg[5:6, :] = jnp.sum(dfirst, axis=0, keepdims=True)
    dres = norm_back(dfirst, vec[4:5], normed1, scale_in[...])
    da_scr[...] = dres.astype(BF)
    vg[2:3, :] = jnp.sum(da_scr[...].astype(F32), axis=0, keepdims=True)
    dattended = jnp.zeros((ROW, D), F32)
    for half, w in sides:
        dattended = dattended + dot_t(da_scr[:, half_lanes(half, HALF)], w[:, O_LANE:UP_LANE])
    do_scr[...] = dattended.astype(BF)
    share = HD ** (-0.5)
    pairs = [slice(128 * pair, 128 * pair + 128) for pair in range(H // 2)]
    dos = [by_head(do_scr[:, cols]) for cols in pairs]
    dsofts = [dot_t(do, v_in[:, cols]) for do, cols in zip(dos, pairs)]
    dss = []
    for pair, dsoft in enumerate(dsofts):
        soft = p_in[pair]
        dss.append((soft * (dsoft - jnp.sum(soft * dsoft, axis=-1, keepdims=True))).astype(BF))
    for pair, cols in enumerate(pairs):
        ds = dss[pair]
        dq_scr[:, cols] = (dot(abreast(ds), by_head(k_in[:, cols])) * share).astype(BF)
        dk_scr[:, cols] = (dot_in(ds, by_head(q_in[:, cols])) * share).astype(BF)
        dv_scr[:, cols] = dot_in(p_in[pair].astype(BF), dos[pair]).astype(BF)
    vg[0:1, :] = jnp.sum(dq_scr[...].astype(F32), axis=0, keepdims=True)
    vg[1:2, :] = jnp.sum(dv_scr[...].astype(F32), axis=0, keepdims=True)
    for target, half in ((keep, c), (send, 1 - c)):
        target[:, 0:D] = y_scr[half]
        target[:, D : 2 * D] = y_scr[2 + half]
        target[:, DU0:DF0] = du_scr[:, half_lanes(half, 1024)]
        target[:, DF0:GRADS] = df_scr[...]
    base[...] = grad2 + dres


def input_kernel(core, base, grads, w_own, w_other, out):
    total = base[...]
    for half, w in ((core[0], w_own), (1 - core[0], w_other)):
        for i in range(3):
            total = total + dot_t(grads[i, :, half_lanes(half, HALF)], w[:, HALF * i : HALF * (i + 1)])
    out[...] = total.astype(BF)


def weights_kernel(acts, acts_other, keep, got, vg, vg_other, out, vec):
    def both(one, two, first, last):
        return jnp.concatenate([one[:, first:last], two[:, first:last]], axis=0)

    out[:, UP_LANE:DOWN_LANE] = dot_in(both(acts, acts_other, H0, Z0), both(keep, got, DU0, DF0)).astype(BF)
    down = both(keep, got, DF0, GRADS)
    for k in range(2):
        lane = DOWN_LANE + D * k
        units = both(acts, acts_other, Z0 + D * k, Z0 + D * (k + 1))
        out[:, lane : lane + D] = dot_in(units, down).astype(BF)
    for k in range(2):
        left = both(acts, acts_other, D * k, D * (k + 1))
        out[:, D * k : D * (k + 1)] = dot_in(left, both(keep, got, D * k, D * (k + 1))).astype(BF)
    total = vg[...] + vg_other[...]
    vec[...] = jnp.zeros((128, D), F32)
    vec[0:8, :] = total[0:8]
    for part in range(4):
        for q in range(4):
            vec[8 + part : 9 + part, 128 * q : 128 * (q + 1)] = total[8 + q : 9 + q, 128 * part : 128 * (part + 1)]
    vec[8:16, :] = dot_t(vec[8:16, :].astype(BF), regroup())
    out[:, VEC_LANE:BLOCK] = vec[...].T.astype(BF)


def add_up(ref):
    total = ref[0].astype(F32)
    for i in range(1, 64):
        total = total + ref[i].astype(F32)
    return total


def split3(value):
    one = value.astype(BF)
    rest = value - one.astype(F32)
    two = rest.astype(BF)
    three = (rest - two.astype(F32)).astype(BF)
    return one, two, three


def reduce_kernel(got, grads):
    grads[...] = add_up(got)


def pay_kernel(grads, grads_other, pay):
    vec = grads[:, VEC_LANE:BLOCK]
    own, other = grads[:, 0:VEC_LANE], grads_other[:, 0:VEC_LANE]
    square = (jnp.sum(own * own) + jnp.sum(other * other)) + jnp.sum(vec * vec)
    row = lax.broadcasted_iota(jnp.int32, (8, 128), 0)
    lane = lax.broadcasted_iota(jnp.int32, (8, 128), 1)
    full = jnp.full((8, 128), square, F32)
    one, two, three = split3(full)
    note = jnp.where(lane == 0, one.astype(F32), jnp.where(lane == 1, two.astype(F32), three.astype(F32)))
    note = jnp.where((row == 0) & (lane < 3), note, 0.0).astype(BF)
    rows = role_lanes(grads[:, 0:VEC_LANE].astype(BF), note)
    for i in range(64):
        pay[i] = rows[i % 4]


def halves(value):
    high = value.astype(BF)
    return high, (value - high.astype(F32)).astype(BF)


def fine(a, b):
    ah, al = a
    bh, bl = b
    return dot(jnp.concatenate([ah, ah, al], axis=1), jnp.concatenate([bh, bl, bh], axis=0))


TALL = 3 * HALF + 8


def near_kernel(far, near, sem):
    copy = pltpu.make_async_copy(far, near, sem)
    copy.start()
    copy.wait()


def gram_kernel(role_ref, got, mom, matrix, gram, clip_out, factor_out):
    role = role_ref[0]
    clip = jnp.sqrt(jnp.full((8, 128), jnp.sum(got[:, 1024:1152].astype(F32)), F32))
    factors = CLIP_LIMIT / jnp.maximum(clip, CLIP_LIMIT)
    clip_out[...] = clip[0:1, 0:1]
    factor_out[...] = factors
    factor = factors[0:1, 0:1]

    def make(k):
        cols = slice(D * k, D * (k + 1))
        value = MOMENTUM_DECAY * mom[:, cols].astype(F32) + factor * got[:, cols].astype(F32)
        value = value.astype(BF)
        matrix[k] = value
        value = value.astype(F32)
        return jnp.sum(value * value)

    def finish(product, parts, square):
        for i, (a, b) in enumerate(((0, 0), (0, 1), (1, 1))):
            total = product(a, b, 0)
            for k in range(1, parts):
                total = total + product(a, b, k)
            gram[HALF * i : HALF * (i + 1), :] = total
        gram[3 * HALF : TALL, :] = jnp.full((8, HALF), square, F32)

    def inner(a, b, k):
        return dot_in(matrix[k, :, HALF * a : HALF * (a + 1)], matrix[k, :, HALF * b : HALF * (b + 1)])

    def outer(a, b, k):
        return dot_t(matrix[k, HALF * a : HALF * (a + 1), :], matrix[k, HALF * b : HALF * (b + 1), :])

    @pl.when(role < 2)
    def _():
        square = make(0)
        finish(inner, 1, square)

    @pl.when(role == 2)
    def _():
        square = make(0) + make(1)
        finish(outer, 2, square)

    @pl.when(role == 3)
    def _():
        square = make(0) + make(1)
        finish(inner, 2, square)


def newton_kernel(role_ref, plane_ref, matrix, gram_own, gram_other, out, gram, rows_scr):
    role, plane = role_ref[0], plane_ref[0]
    chips = pl.ds(pl.multiple_of(plane * 32, 32), 32)

    def scaled(total):
        size = jnp.sqrt(total[3 * HALF : 3 * HALF + 1, 0:1]) + 1e-07
        inverse = 1.0 / size
        total = total[0 : 3 * HALF] * (inverse * inverse)
        gram[0:HALF, 0:HALF] = total[0:HALF]
        gram[0:HALF, HALF:D] = total[HALF:D]
        gram[HALF:D, 0:HALF] = total[HALF:D].T
        gram[HALF:D, HALF:D] = total[D : 3 * HALF]
        return inverse

    def rows_of(k):
        return matrix[k, chips, :].astype(F32)

    @pl.when(role < 2)
    def _():
        inverse = scaled(gram_own[...])
        rows_scr[0:32, :] = rows_of(0) * inverse
        rows_scr[32:64, :] = jnp.zeros((32, D), F32)

    @pl.when(role == 2)
    def _():
        inverse = scaled(gram_own[...] + gram_other[...])
        here = lax.broadcasted_iota(jnp.int32, (32, D), 0) + 32 * plane
        there = lax.broadcasted_iota(jnp.int32, (32, D), 1)
        rows_scr[0:32, :] = jnp.where(here == there, 1.0, 0.0) * inverse
        rows_scr[32:64, :] = jnp.zeros((32, D), F32)

    @pl.when(role == 3)
    def _():
        inverse = scaled(gram_own[...] + gram_other[...])
        for k in range(2):
            rows_scr[32 * k : 32 * (k + 1), :] = rows_of(k) * inverse

    diagonal = (
        lax.broadcasted_iota(jnp.int32, (D, D), 0) == lax.broadcasted_iota(jnp.int32, (D, D), 1)
    )

    def turn(exact):
        own = halves(gram[...])
        square = fine(own, own) if exact else dot(own[0], own[0])
        poly = NEWTON_SECOND * gram[...] + NEWTON_THIRD * square
        poly = halves(jnp.where(diagonal, poly + NEWTON_FIRST, poly))
        pairs = zip(halves(fine(poly, own)), halves(rows_scr[...]))
        both = fine(tuple(jnp.concatenate(pair, axis=0) for pair in pairs), poly)
        gram[...] = both[0:D]
        rows_scr[...] = both[D:]

    pl.loop(0, NS_ITERS - 2)(lambda _: turn(False))
    turn(True)
    own = halves(gram[...])
    rows = rows_scr[...]
    once = fine(halves(rows), own)
    twice = fine(halves(once), own)
    rows_scr[...] = NEWTON_FIRST * rows + NEWTON_SECOND * once + NEWTON_THIRD * twice

    def send(k, value):
        value = value.astype(BF).reshape(4, 8, D)
        out[:, 0, :, D * k : D * (k + 1)] = value
        out[:, 1, :, D * k : D * (k + 1)] = value

    @pl.when(role == 2)
    def _():
        high, low = halves(rows_scr[0:32, :])
        for k in range(2):
            send(k, dot(high, matrix[k]) + dot(low, matrix[k]))

    @pl.when(role != 2)
    def _():
        for k in range(2):
            send(k, rows_scr[32 * k : 32 * (k + 1), :])


def rows4(is_left, value):
    return jnp.where(is_left, value[0:4], value[4:8])


def natural(ups):
    parts = [
        jnp.concatenate([ups[:, D * q + 128 * part : D * q + 128 * (part + 1)] for q in range(4)], axis=1)
        for part in range(4)
    ]
    return dot_t(jnp.concatenate(parts, axis=0).astype(BF), regroup())


def momenta_kernel(
    core, grads, grads_other, factors, vec, attn_m, up_m, down_m, vec_m, vec_s,
    attn_mom, up_mom, down_mom, vec_mom, vec_sec, vec_new, vec_copy, ups, downs,
):
    is_left = core[0] == 0
    factor = factors[0:1, 0:1]

    def both(first, last):
        mine, other = grads[:, first:last], grads_other[:, first:last]
        left = jnp.where(is_left, mine, other)
        right = jnp.where(is_left, other, mine)
        return rows4(is_left, left), rows4(is_left, right)

    pairs = [both(D * k, D * (k + 1)) for k in range(2)]
    for m in range(4):
        attn_mom[m] = MOMENTUM_DECAY * attn_m[m] + factor * pairs[m // 2][m % 2]
    high, low = halves(jnp.concatenate(both(UP_LANE, DOWN_LANE), axis=1))
    ups[0:4, :] = high.astype(F32)
    ups[4:8, :] = low.astype(F32)
    moved = natural(ups)
    for part in range(4):
        cols = slice(D * part, D * (part + 1))
        grad = moved[8 * part : 8 * part + 4] + moved[8 * part + 4 : 8 * part + 8]
        up_mom[:, cols] = MOMENTUM_DECAY * up_m[:, cols] + factor * grad
    sides = both(DOWN_LANE, VEC_LANE)
    for q in range(4):
        grad = sides[q // 2][:, D * (q % 2) : D * (q % 2 + 1)]
        for i in range(4):
            downs[4 * i + q : 4 * i + q + 1, :] = grad[i : i + 1]
    down_mom[...] = MOMENTUM_DECAY * down_m[...] + factor * downs[...]
    clipped = factor * rows4(is_left, grads[:, VEC_LANE:BLOCK])[:, 0:12]
    first = BETA_FIRST * vec_m[...] + (1.0 - BETA_FIRST) * clipped
    second = BETA_SECOND * vec_s[...] + (1.0 - BETA_SECOND) * clipped * clipped
    vec_mom[...] = first
    vec_sec[...] = second
    first_hat = first / (1.0 - BETA_FIRST**STEP)
    second_hat = second / (1.0 - BETA_SECOND**STEP)
    new = vec[...] - RATE_VECTOR * first_hat / (jnp.sqrt(second_hat) + ADAM_EPSILON)
    vec_new[...] = new
    vec_copy[...] = new.astype(BF)


def update_kernel(
    core, got, attn, up, down, attn_new, up_new, down_new, attn_copy, up_copy, down_copy, ups, downs
):
    is_left = core[0] == 0
    keep_share = 1.0 - RATE_MATRIX * DECAY_MATRIX
    for m in range(4):
        new = attn[m] * keep_share - RATE_MATRIX * rows4(is_left, got[m, :, 0:512].astype(F32))
        attn_new[m] = new
        attn_copy[m] = new.astype(BF)
    ups[0:4, :] = rows4(is_left, jnp.concatenate([got[4].astype(F32), got[5].astype(F32)], axis=1))
    ups[4:8, :] = jnp.zeros((4, FF), F32)
    rate = RATE_MATRIX * math.sqrt(max(1.0, FF / D))
    moved = natural(ups)
    for part in range(4):
        cols = slice(D * part, D * (part + 1))
        up_new[:, cols] = up[:, cols] * keep_share - rate * moved[8 * part : 8 * part + 4]
    up_copy[...] = up_new[...].astype(BF)
    rate = RATE_MATRIX * math.sqrt(max(1.0, D / FF))
    for q in range(4):
        step = rows4(is_left, got[6 + q // 2, :, D * (q % 2) : D * (q % 2 + 1)].astype(F32))
        for i in range(4):
            downs[4 * i + q : 4 * i + q + 1, :] = step[i : i + 1]
    down_new[...] = down[...] * keep_share - rate * downs[...]
    down_copy[...] = down_new[...].astype(BF)


def swap(value):
    return lax.ppermute(value, "c", [(0, 1), (1, 0)])


def to_chips(value):
    return lax.all_to_all(value, CHIPS, 0, 0, tiled=True)


def body(
    block_input, cotangent, segment_ids, attn_master, up_master, down_master, vec_master,
    attn_moment, up_moment, down_moment, vec_moment, vec_second,
):
    c = lax.axis_index("c")
    core = c.reshape(1).astype(jnp.int32)
    role = lax.axis_index("y").reshape(1).astype(jnp.int32)
    plane = (lax.axis_index("x") * 4 + lax.axis_index("z")).reshape(1).astype(jnp.int32)
    core, role, plane = lax.optimization_barrier((core, role, plane))

    keep, send = call(
        pack_kernel,
        [((8, BLOCK), BF)] * 2,
        [core, attn_master, up_master, down_master, vec_master.T, attn_moment, up_moment, down_moment],
        scratch=[
            pltpu.VMEM((4, 4, D), F32), pltpu.VMEM((4, FF), F32), pltpu.VMEM((16, D), F32), pltpu.VMEM((4, 12), F32),
            pltpu.VMEM((4, 4, D), F32), pltpu.VMEM((4, FF), F32), pltpu.VMEM((16, D), F32),
            pltpu.VMEM((8, 3 * FF), F32), pltpu.VMEM((8, BLOCK), F32), pltpu.VMEM((32, D), F32),
            pltpu.SemaphoreType.DMA((7,)),
        ],
        smem=(0,),
        far=range(1, 8),
    )
    message, message_mom = call(
        spread_kernel, [((64, 8, BLOCK), BF), ((64, 8, 1024), BF)], [core, keep, swap(send)], smem=(0,)
    )
    own = to_chips(message)
    own, message_mom = lax.optimization_barrier((own, message_mom))
    other = swap(own)
    mom = to_chips(message_mom).reshape(D, 1024)
    own, other = own.reshape(D, BLOCK), other.reshape(D, BLOCK)
    q, k, v, soft, vec, acts_own, acts_sent, first, normed, scale, slope, other = call(
        forward_kernel,
        [((ROW, D), BF)] * 3
        + [((H // 2, 2 * ROW, ROW), F32), ((16, D), F32), ((ROW, ACTS), BF), ((ROW, ACTS), BF)]
        + [((ROW, D), F32), ((ROW, D), F32), ((ROW, 1), F32), ((ROW, FF), F32), ((D, 3072), BF)],
        [core, block_input, own, other, segment_ids],
        scratch=[
            pltpu.VMEM((ROW, D), F32), pltpu.VMEM((2, ROW, D), BF), pltpu.VMEM((ROW, FF), BF),
            pltpu.SemaphoreType.DMA((3,)),
        ],
        smem=(0,),
        args=(1, 4),
        far=(3,),
        flops=8 * 2 * ROW * D * D,
    )
    acts_other = swap(acts_sent)
    layer_out, base, ygrads, keep, send, vg = call(
        backward_kernel,
        [((ROW, D), BF), ((ROW, D), F32), ((4, ROW, D), BF), ((ROW, GRADS), BF), ((ROW, GRADS), BF), ((16, D), F32)],
        [
            core, block_input, acts_own, acts_sent, first, vec, own, other, cotangent, slope, normed, scale,
            q, k, v, soft,
        ],
        scratch=[
            pltpu.VMEM((ROW, D), F32), pltpu.VMEM((ROW, FF), BF), pltpu.VMEM((ROW, D), BF), pltpu.VMEM((ROW, D), BF),
        ],
        smem=(0,),
        args=(1, 8),
        results=(0,),
        flops=18 * 2 * ROW * D * D,
    )
    got, vg_other = swap(send), swap(vg)
    (input_grad,) = call(
        input_kernel,
        [((ROW, D), BF)],
        [core, base, ygrads, own, other],
        smem=(0,),
        results=(0,),
        flops=3 * 2 * ROW * D * D,
    )
    got, input_grad = lax.optimization_barrier((got, input_grad))
    (weights,) = call(
        weights_kernel,
        [((D, BLOCK), BF)],
        [acts_own, acts_other, keep, got, vg, vg_other],
        scratch=[pltpu.VMEM((128, D), F32)],
        flops=2 * 256 * 512 * 3072,
    )
    weights, mom = lax.optimization_barrier((weights, mom))
    weights = to_chips(weights.reshape(64, 8, BLOCK))
    (grads,) = call(reduce_kernel, [((8, BLOCK), F32)], [weights])
    grads, mom = lax.optimization_barrier((grads, mom))
    grads_other = swap(grads)
    (mom,) = call(near_kernel, [((D, 1024), BF)], [mom], scratch=[pltpu.SemaphoreType.DMA], far=(0,))
    (pay,) = call(pay_kernel, [((64, 8, 1152), BF)], [grads, grads_other])
    pay, mom = lax.optimization_barrier((pay, mom))
    pay = to_chips(pay)
    matrix, gram, clip_norm, factors = call(
        gram_kernel,
        [((2, D, D), BF), ((TALL, HALF), F32), ((1, 1), F32), ((8, 128), F32)],
        [role, pay.reshape(D, 1152), mom],
        smem=(0,),
        results=(2,),
        flops=2 * 2 * D * D * D,
    )
    gram_other = swap(gram)
    *moms, vec_mom, vec_sec, vec_new, vec_copy = call(
        momenta_kernel,
        [((4, 4, D), F32), ((4, FF), F32), ((16, D), F32)] + [((4, 12), F32)] * 3 + [((4, 12), BF)],
        [
            core, grads, grads_other, factors, vec_master.T, attn_moment, up_moment, down_moment,
            vec_moment.T, vec_second.T,
        ],
        scratch=[pltpu.VMEM((8, FF), F32), pltpu.VMEM((16, D), F32)],
        smem=(0,),
        args=range(4, 10),
        results=range(7),
    )
    gram_other, *moms = lax.optimization_barrier((gram_other, *moms))
    vecs = [t.T for t in (vec_mom, vec_sec, vec_new, vec_copy)]
    (orth,) = call(
        newton_kernel,
        [((4, 2, 8, 1024), BF)],
        [role, plane, matrix, gram, gram_other],
        scratch=[pltpu.VMEM((D, D), F32), pltpu.VMEM((64, D), F32)],
        smem=(0, 1),
        flops=14 * 3 * 2 * D * D * D,
    )
    orth = orth.reshape(8, 8, 1024)
    orth = lax.all_to_all(orth, ("y", "c"), 0, 0, tiled=True)
    news = call(
        update_kernel,
        [((4, 4, D), F32), ((4, FF), F32), ((16, D), F32), ((4, 4, D), BF), ((4, FF), BF), ((16, D), BF)],
        [core, orth, attn_master, up_master, down_master],
        scratch=[pltpu.VMEM((8, FF), F32), pltpu.VMEM((16, D), F32)],
        smem=(0,),
        args=range(2, 5),
        results=range(6),
    )
    return (layer_out, input_grad, clip_norm[0, 0], *moms, *news, *vecs)


def solution(mesh):
    grid = Mesh(mesh.devices.reshape(4, 4, 4, 2), ("x", "z", "y", "c"))
    row, mat, vec = P(ALL, None), P(None, ALL, None), P(None, ALL)
    return jax.shard_map(
        body,
        mesh=grid,
        in_specs=(row, row, row, mat, row, row, vec, mat, row, row, vec, vec),
        out_specs=(row, row, P(), mat, row, row, mat, row, row, mat, row, row, vec, vec, vec, vec),
        check_vma=False,
    )
```

```python
import math

import jax
import jax.numpy as jnp
from jax import lax
from jax.experimental import pallas as pl
from jax.experimental.pallas import tpu as pltpu
from jax.sharding import Mesh, PartitionSpec as P

D = 512
FF = 2048
H = 8
HD = 64
ROW = 128
STEP = 10
NS_ITERS = 5
HALF = 256

MASKED_SCORE = -1e30
NORM_EPSILON = 1e-05
CLIP_LIMIT = 1.0
MOMENTUM_DECAY = 0.95
RATE_MATRIX = 0.5
DECAY_MATRIX = 0.01
BETA_FIRST = 0.9
BETA_SECOND = 0.999
RATE_VECTOR = 0.2
ADAM_EPSILON = 1e-08
NEWTON_FIRST = 3.4445
NEWTON_SECOND = -4.775
NEWTON_THIRD = 2.0315

CHIPS = ("x", "z", "y")
ALL = ("x", "z", "y", "c")
BF = jnp.bfloat16
F32 = jnp.float32
VMEM_LIMIT = 12 * 1024 * 1024


def call(kernel, outs, ins, scratch=(), smem=(), args=(), far=(), results=(), away=(), flops=0, limit=VMEM_LIMIT):
    spec = [
        pl.BlockSpec(memory_space=pltpu.SMEM if i in smem else pl.ANY if i in far else pltpu.VMEM)
        for i in range(len(ins))
    ]
    placed = [
        x if i in smem or i in args
        else pltpu.with_memory_space_constraint(x, pltpu.HBM if i in far else pltpu.VMEM)
        for i, x in enumerate(ins)
    ]
    shapes = [
        jax.ShapeDtypeStruct(s, t) if i in results else pltpu.HBM(s, t) if i in away else pltpu.VMEM(s, t)
        for i, (s, t) in enumerate(outs)
    ]
    moved = sum(math.prod(a.shape) * a.dtype.itemsize for a in ins)
    return pl.pallas_call(
        kernel,
        out_shape=shapes,
        in_specs=spec,
        out_specs=[
            pl.BlockSpec(memory_space=pl.ANY if i in away else pltpu.VMEM) for i in range(len(shapes))
        ],
        scratch_shapes=list(scratch),
        compiler_params=pltpu.CompilerParams(vmem_limit_bytes=limit),
        cost_estimate=pl.CostEstimate(flops=flops, bytes_accessed=moved, transcendentals=0),
    )(*placed)


def dot(a, b):
    return jnp.dot(a, b, preferred_element_type=F32)


def dot_t(a, b):
    return lax.dot_general(a, b, (((1,), (1,)), ((), ())), preferred_element_type=F32)


def dot_in(a, b):
    return lax.dot_general(a, b, (((0,), (0,)), ((), ())), preferred_element_type=F32)


O_LANE, UP_LANE, DOWN_LANE, VEC_LANE, BLOCK = 768, 1024, 2048, 3072, 3200
X0, A0, H0, Z0, ACTS = 0, 512, 1024, 1536, 3328
Y0, DU0, DF0, GRADS = 0, 1024, 2048, 2560


def half_lanes(half, size):
    return pl.ds(pl.multiple_of(half * size, size), size)


def regroup():
    source = lax.broadcasted_iota(jnp.int32, (D, D), 0)
    target = lax.broadcasted_iota(jnp.int32, (D, D), 1)
    return jnp.where(target == (source & 3) * 128 + (source >> 2), 1.0, 0.0).astype(BF)


def pack_kernel(
    core, attn, up, down, vec, attn_m, up_m, down_m, keep, send,
    attn_v, up_v, down_v, vec_v, attn_mv, up_mv, down_mv, full, block, stage, sems,
):
    c = core[0]
    copies = [
        pltpu.make_async_copy(source, target, sems.at[i])
        for i, (source, target) in enumerate(
            [(attn, attn_v), (up, up_v), (down, down_v), (vec, vec_v), (attn_m, attn_mv), (up_m, up_mv), (down_m, down_mv)]
        )
    ]
    for copy in copies:
        copy.start()
    move = regroup()
    for copy in copies:
        copy.wait()
    for first, attn_one, up_one, down_one in ((0, attn_v, up_v, down_v), (4, attn_mv, up_mv, down_mv)):
        rows = slice(first, first + 4)
        for m in range(4):
            full[rows, D * m : D * (m + 1)] = attn_one[m]
        for part in range(4):
            row = 8 * part + first
            stage[row : row + 4, :] = up_one[:, D * part : D * (part + 1)]
        for i in range(4):
            for q in range(4):
                lane = 2 * FF + D * q
                full[first + i : first + i + 1, lane : lane + D] = down_one[4 * i + q : 4 * i + q + 1, :]
    moved = dot(stage[...].astype(BF), move)
    for part in range(4):
        for q in range(4):
            lane = FF + D * q + 128 * part
            full[:, lane : lane + 128] = moved[8 * part : 8 * (part + 1), 128 * q : 128 * (q + 1)]
    for target, half in ((keep, c), (send, 1 - c)):
        for m in range(4):
            lanes = pl.ds(pl.multiple_of(D * m + HALF * half, HALF), HALF)
            block[0:4, HALF * m : HALF * (m + 1)] = full[0:4, lanes]
        for m in range(2):
            lanes = pl.ds(pl.multiple_of(2 * D * m + D * half, D), D)
            block[4:8, D * m : D * (m + 1)] = full[4:8, lanes]
        block[:, UP_LANE:DOWN_LANE] = full[:, pl.ds(pl.multiple_of(FF + 1024 * half, 1024), 1024)]
        for q in range(4):
            lanes = pl.ds(pl.multiple_of(2 * FF + D * q + HALF * half, HALF), HALF)
            lane = DOWN_LANE + HALF * q
            block[0:4, lane : lane + HALF] = full[0:4, lanes]
        lanes = pl.ds(pl.multiple_of(2 * FF + 1024 * half, 1024), 1024)
        block[4:8, DOWN_LANE:VEC_LANE] = full[4:8, lanes]
        block[:, VEC_LANE:BLOCK] = jnp.zeros((8, 128), F32)
        block[0:4, VEC_LANE : VEC_LANE + 12] = vec_v[...]
        target[...] = block[...].astype(BF)


def role_lanes(block, note):
    gap = jnp.zeros((8, 512), block.dtype)
    tail = [] if note is None else [note]
    return [
        jnp.concatenate([block[:, 0:512], gap] + tail, axis=1),
        jnp.concatenate([block[:, 512:1024], gap] + tail, axis=1),
        jnp.concatenate([block[:, UP_LANE:DOWN_LANE]] + tail, axis=1),
        jnp.concatenate([block[:, DOWN_LANE:VEC_LANE]] + tail, axis=1),
    ]


def spread_kernel(core, keep, got, message, message_mom):
    mine, other = keep[...].astype(F32), got[...].astype(F32)
    is_left = core[0] == 0
    left, right = jnp.where(is_left, mine, other), jnp.where(is_left, other, mine)
    block = jnp.concatenate([left[0:4], right[0:4]], axis=0).astype(BF)
    moms = role_lanes(jnp.concatenate([left[4:8], right[4:8]], axis=0).astype(BF), None)
    for i in range(64):
        message[i] = block
        message_mom[i] = moms[i % 4]


def by_head(pair):
    low = (lax.broadcasted_iota(jnp.int32, (ROW, ROW), 1) < HD).astype(F32)
    return jnp.concatenate([pair * low.astype(BF), pair * (1.0 - low).astype(BF)], axis=0)


def abreast(stacked):
    return jnp.concatenate([stacked[0:ROW], stacked[ROW:]], axis=1)


def norm_parts(values):
    centred = values - jnp.mean(values, axis=-1, keepdims=True)
    scale = lax.rsqrt(jnp.mean(centred * centred, axis=-1, keepdims=True) + NORM_EPSILON)
    return centred * scale, scale


def norm_back(grad, gain, normed, scale):
    grad = grad * gain
    return scale * (
        grad
        - jnp.mean(grad, axis=-1, keepdims=True)
        - normed * jnp.mean(grad * normed, axis=-1, keepdims=True)
    )


def forward_kernel(
    core, x, w_own, w_far, seg, q_out, k_out, v_out, p_out, vec_out, keep, send, first_out, norm_out, scale_out,
    slope, w_other, wide, pair_scr, acts, sems,
):
    c = core[0]
    copies = []
    for i in range(3):
        lanes = pl.ds(1024 * i, 1024)
        copies.append(pltpu.make_async_copy(w_far.at[:, lanes], w_other.at[:, lanes], sems.at[i]))
        copies[i].start()
    sides = ((c, w_own), (1 - c, w_other))
    vec = w_own[:, VEC_LANE:BLOCK].astype(F32).T[:16]
    vec_out[...] = vec
    moved = dot(vec[8:16].astype(BF), regroup())
    for part in range(4):
        for q in range(4):
            vec_out[8 + q : 9 + q, 128 * part : 128 * (part + 1)] = moved[part : part + 1, 128 * q : 128 * (q + 1)]
    tokens = x[...]
    pair_scr[0] = tokens
    names = jnp.broadcast_to(seg[...].astype(F32), (ROW, ROW))
    gap = names - names.T
    same = jnp.concatenate([gap, gap], axis=0) == 0.0
    for half, w in sides:
        if w is w_other:
            copies[0].wait()
        product = dot(tokens, w[:, 0:O_LANE])
        q = (product[:, 0:HALF] + vec_out[0:1, half_lanes(half, HALF)]).astype(BF)
        k = product[:, HALF : 2 * HALF].astype(BF)
        v = (product[:, 2 * HALF : O_LANE] + vec_out[1:2, half_lanes(half, HALF)]).astype(BF)
        for target, value in ((q_out, q), (k_out, k), (v_out, v)):
            target[:, half_lanes(half, HALF)] = value
        for pair in range(2):
            cols = slice(128 * pair, 128 * pair + 128)
            scores = dot_t(by_head(q[:, cols]), k[:, cols]) * (HD ** (-0.5))
            scores = jnp.where(same, scores, MASKED_SCORE)
            expo = jnp.exp(scores - jnp.max(scores, axis=-1, keepdims=True))
            soft = expo / jnp.sum(expo, axis=-1, keepdims=True)
            p_out[2 * half + pair] = soft
            attended = dot(abreast(soft.astype(BF)), by_head(v[:, cols]))
            lanes = pl.ds(pl.multiple_of(HALF * half + 128 * pair, 128), 128)
            pair_scr[1, :, lanes] = attended.astype(BF)
    for half, w in sides:
        wide[:, half_lanes(half, HALF)] = dot(pair_scr[1], w[:, O_LANE:UP_LANE])
    normed, scale = norm_parts(tokens.astype(F32) + wide[...] + vec[2:3])
    norm_out[...] = normed
    scale_out[...] = scale
    first = normed * vec[4:5] + vec[5:6]
    first_out[...] = first
    first_low = first.astype(BF)
    root = math.sqrt(2.0 / math.pi)
    copies[1].wait()
    for half, w in sides:
        for k in range(2):
            bias = vec_out[pl.ds(8 + 2 * half + k, 1), :]
            u = dot(first_low, w[:, UP_LANE + D * k : UP_LANE + D * (k + 1)]) + bias
            square = u * u
            tanh = jnp.tanh(root * (u + 0.044715 * (square * u)))
            gate = 0.5 * (1.0 + tanh)
            cols = pl.ds(pl.multiple_of(1024 * half + D * k, D), D)
            slope[:, cols] = gate + 0.5 * u * (1.0 - tanh * tanh) * (root * (1.0 + 3 * 0.044715 * square))
            acts[:, cols] = (u * gate).astype(BF)
    for target, half in ((keep, c), (send, 1 - c)):
        target[:, X0:A0] = tokens
        target[:, A0:H0] = pair_scr[half]
        target[:, H0:Z0] = first_low
        target[:, Z0 : Z0 + 1024] = acts[:, half_lanes(half, 1024)]
        target[:, Z0 + 1024 : ACTS] = jnp.zeros((ROW, ACTS - Z0 - 1024), BF)
    copies[2].wait()


def backward_kernel(
    core, x, acts_own, acts_sent, first, vec_in, w_own, w_other, cot, slope, normed_in, scale_in, q_in, k_in, v_in, p_in,
    out, base, y_scr, keep, send, vg, wide, du_scr, df_scr, do_scr,
):
    c = core[0]
    sides = ((c, w_own), (1 - c, w_other))
    vec = vec_in[...]
    dq_scr, dk_scr, dv_scr, da_scr = (y_scr.at[i] for i in range(4))
    for half, w in sides:
        feed = jnp.zeros((ROW, HALF), F32)
        for group, acts in ((c, acts_own), (1 - c, acts_sent)):
            for k in range(2):
                lanes = pl.ds(pl.multiple_of(DOWN_LANE + 2 * HALF * group + HALF * k, HALF), HALF)
                feed = feed + dot(acts[:, Z0 + D * k : Z0 + D * (k + 1)], w[:, lanes])
        wide[:, half_lanes(half, HALF)] = feed
    residual = wide[...] + vec[3:4] + first[...] + x[...].astype(F32)
    normed, scale = norm_parts(residual)
    out[...] = (normed * vec[6:7] + vec[7:8]).astype(BF)
    grad = cot[...].astype(F32)
    vg[...] = jnp.zeros((16, D), F32)
    vg[6:7, :] = jnp.sum(grad * normed, axis=0, keepdims=True)
    vg[7:8, :] = jnp.sum(grad, axis=0, keepdims=True)
    grad2 = norm_back(grad, vec[6:7], normed, scale)
    df_scr[...] = grad2.astype(BF)
    vg[3:4, :] = jnp.sum(df_scr[...].astype(F32), axis=0, keepdims=True)
    for q in range(4):
        lane = DOWN_LANE + HALF * q
        dz = dot_t(df_scr[:, half_lanes(c, HALF)], w_own[:, lane : lane + HALF])
        dz = dz + dot_t(df_scr[:, half_lanes(1 - c, HALF)], w_other[:, lane : lane + HALF])
        du = (dz * slope[:, D * q : D * (q + 1)]).astype(BF)
        du_scr[:, D * q : D * (q + 1)] = du
        vg[8 + q : 9 + q, :] = jnp.sum(du.astype(F32), axis=0, keepdims=True)
    dfirst = grad2
    for half, w in sides:
        dfirst = dfirst + dot_t(du_scr[:, half_lanes(half, 1024)], w[:, UP_LANE:DOWN_LANE])
    normed1 = normed_in[...]
    vg[4:5, :] = jnp.sum(dfirst * normed1, axis=0, keepdims=True)
    vg[5:6, :] = jnp.sum(dfirst, axis=0, keepdims=True)
    dres = norm_back(dfirst, vec[4:5], normed1, scale_in[...])
    da_scr[...] = dres.astype(BF)
    vg[2:3, :] = jnp.sum(da_scr[...].astype(F32), axis=0, keepdims=True)
    dattended = jnp.zeros((ROW, D), F32)
    for half, w in sides:
        dattended = dattended + dot_t(da_scr[:, half_lanes(half, HALF)], w[:, O_LANE:UP_LANE])
    do_scr[...] = dattended.astype(BF)
    share = HD ** (-0.5)
    pairs = [slice(128 * pair, 128 * pair + 128) for pair in range(H // 2)]
    dos = [by_head(do_scr[:, cols]) for cols in pairs]
    dsofts = [dot_t(do, v_in[:, cols]) for do, cols in zip(dos, pairs)]
    dss = []
    for pair, dsoft in enumerate(dsofts):
        soft = p_in[pair]
        dss.append((soft * (dsoft - jnp.sum(soft * dsoft, axis=-1, keepdims=True))).astype(BF))
    for pair, cols in enumerate(pairs):
        ds = dss[pair]
        dq_scr[:, cols] = (dot(abreast(ds), by_head(k_in[:, cols])) * share).astype(BF)
        dk_scr[:, cols] = (dot_in(ds, by_head(q_in[:, cols])) * share).astype(BF)
        dv_scr[:, cols] = dot_in(p_in[pair].astype(BF), dos[pair]).astype(BF)
    vg[0:1, :] = jnp.sum(dq_scr[...].astype(F32), axis=0, keepdims=True)
    vg[1:2, :] = jnp.sum(dv_scr[...].astype(F32), axis=0, keepdims=True)
    for target, half in ((keep, c), (send, 1 - c)):
        target[:, 0:D] = y_scr[half]
        target[:, D : 2 * D] = y_scr[2 + half]
        target[:, DU0:DF0] = du_scr[:, half_lanes(half, 1024)]
        target[:, DF0:GRADS] = df_scr[...]
    base[...] = grad2 + dres


def input_kernel(core, base, grads, w_own, w_other, out):
    total = base[...]
    for half, w in ((core[0], w_own), (1 - core[0], w_other)):
        for i in range(3):
            total = total + dot_t(grads[i, :, half_lanes(half, HALF)], w[:, HALF * i : HALF * (i + 1)])
    out[...] = total.astype(BF)


def weights_kernel(acts, acts_other, keep, got, vg, vg_other, out, vec):
    def both(one, two, first, last):
        return jnp.concatenate([one[:, first:last], two[:, first:last]], axis=0)

    out[:, UP_LANE:DOWN_LANE] = dot_in(both(acts, acts_other, H0, Z0), both(keep, got, DU0, DF0)).astype(BF)
    down = both(keep, got, DF0, GRADS)
    for k in range(2):
        lane = DOWN_LANE + D * k
        units = both(acts, acts_other, Z0 + D * k, Z0 + D * (k + 1))
        out[:, lane : lane + D] = dot_in(units, down).astype(BF)
    for k in range(2):
        left = both(acts, acts_other, D * k, D * (k + 1))
        out[:, D * k : D * (k + 1)] = dot_in(left, both(keep, got, D * k, D * (k + 1))).astype(BF)
    total = vg[...] + vg_other[...]
    vec[...] = jnp.zeros((128, D), F32)
    vec[0:8, :] = total[0:8]
    for part in range(4):
        for q in range(4):
            vec[8 + part : 9 + part, 128 * q : 128 * (q + 1)] = total[8 + q : 9 + q, 128 * part : 128 * (part + 1)]
    vec[8:16, :] = dot_t(vec[8:16, :].astype(BF), regroup())
    out[:, VEC_LANE:BLOCK] = vec[...].T.astype(BF)


def add_up(ref):
    total = ref[0].astype(F32)
    for i in range(1, 64):
        total = total + ref[i].astype(F32)
    return total


def split3(value):
    one = value.astype(BF)
    rest = value - one.astype(F32)
    two = rest.astype(BF)
    three = (rest - two.astype(F32)).astype(BF)
    return one, two, three


def reduce_kernel(got, grads, pay):
    grads[...] = add_up(got)
    own, vec = grads[:, 0:VEC_LANE], grads[:, VEC_LANE:BLOCK]
    square = jnp.sum(own * own) + 0.5 * jnp.sum(vec * vec)
    row = lax.broadcasted_iota(jnp.int32, (8, 128), 0)
    lane = lax.broadcasted_iota(jnp.int32, (8, 128), 1)
    full = jnp.full((8, 128), square, F32)
    one, two, three = split3(full)
    note = jnp.where(lane == 0, one.astype(F32), jnp.where(lane == 1, two.astype(F32), three.astype(F32)))
    note = jnp.where((row == 0) & (lane < 3), note, 0.0).astype(BF)
    rows = role_lanes(grads[:, 0:VEC_LANE].astype(BF), note)
    for i in range(64):
        pay[i] = rows[i % 4]


def halves(value):
    high = value.astype(BF)
    return high, (value - high.astype(F32)).astype(BF)


def fine(a, b):
    ah, al = a
    bh, bl = b
    return dot(jnp.concatenate([ah, ah, al], axis=1), jnp.concatenate([bh, bl, bh], axis=0))


TALL = 3 * HALF + 8


def near_kernel(far, near, sem):
    copy = pltpu.make_async_copy(far, near, sem)
    copy.start()
    copy.wait()


def note_kernel(got, note):
    note[...] = jnp.full((8, 128), jnp.sum(got[:, 1024:1152].astype(F32)), F32)


def gram_kernel(role_ref, got, mom, note, note_other, matrix, gram, clip_out, factor_out):
    role = role_ref[0]
    clip = jnp.sqrt(note[...] + note_other[...])
    factors = CLIP_LIMIT / jnp.maximum(clip, CLIP_LIMIT)
    clip_out[...] = clip[0:1, 0:1]
    factor_out[...] = factors
    factor = factors[0:1, 0:1]

    def make(k):
        cols = slice(D * k, D * (k + 1))
        value = MOMENTUM_DECAY * mom[:, cols].astype(F32) + factor * got[:, cols].astype(F32)
        value = value.astype(BF)
        matrix[k] = value
        value = value.astype(F32)
        return jnp.sum(value * value)

    def finish(product, parts, square):
        for i, (a, b) in enumerate(((0, 0), (0, 1), (1, 1))):
            total = product(a, b, 0)
            for k in range(1, parts):
                total = total + product(a, b, k)
            gram[HALF * i : HALF * (i + 1), :] = total
        gram[3 * HALF : TALL, :] = jnp.full((8, HALF), square, F32)

    def inner(a, b, k):
        return dot_in(matrix[k, :, HALF * a : HALF * (a + 1)], matrix[k, :, HALF * b : HALF * (b + 1)])

    def outer(a, b, k):
        return dot_t(matrix[k, HALF * a : HALF * (a + 1), :], matrix[k, HALF * b : HALF * (b + 1), :])

    @pl.when(role < 2)
    def _():
        square = make(0)
        finish(inner, 1, square)

    @pl.when(role == 2)
    def _():
        square = make(0) + make(1)
        finish(outer, 2, square)

    @pl.when(role == 3)
    def _():
        square = make(0) + make(1)
        finish(inner, 2, square)


def newton_kernel(role_ref, plane_ref, matrix, gram_own, gram_other, out, gram, rows_scr):
    role, plane = role_ref[0], plane_ref[0]
    chips = pl.ds(pl.multiple_of(plane * 32, 32), 32)

    def scaled(total):
        size = jnp.sqrt(total[3 * HALF : 3 * HALF + 1, 0:1]) + 1e-07
        inverse = 1.0 / size
        total = total[0 : 3 * HALF] * (inverse * inverse)
        gram[0:HALF, 0:HALF] = total[0:HALF]
        gram[0:HALF, HALF:D] = total[HALF:D]
        gram[HALF:D, 0:HALF] = total[HALF:D].T
        gram[HALF:D, HALF:D] = total[D : 3 * HALF]
        return inverse

    def rows_of(k):
        return matrix[k, chips, :].astype(F32)

    @pl.when(role < 2)
    def _():
        inverse = scaled(gram_own[...])
        rows_scr[0:32, :] = rows_of(0) * inverse
        rows_scr[32:64, :] = jnp.zeros((32, D), F32)

    @pl.when(role == 2)
    def _():
        inverse = scaled(gram_own[...] + gram_other[...])
        here = lax.broadcasted_iota(jnp.int32, (32, D), 0) + 32 * plane
        there = lax.broadcasted_iota(jnp.int32, (32, D), 1)
        rows_scr[0:32, :] = jnp.where(here == there, 1.0, 0.0) * inverse
        rows_scr[32:64, :] = jnp.zeros((32, D), F32)

    @pl.when(role == 3)
    def _():
        inverse = scaled(gram_own[...] + gram_other[...])
        for k in range(2):
            rows_scr[32 * k : 32 * (k + 1), :] = rows_of(k) * inverse

    diagonal = (
        lax.broadcasted_iota(jnp.int32, (D, D), 0) == lax.broadcasted_iota(jnp.int32, (D, D), 1)
    )

    def turn(exact):
        own = halves(gram[...])
        square = fine(own, own) if exact else dot(own[0], own[0])
        poly = NEWTON_SECOND * gram[...] + NEWTON_THIRD * square
        poly = halves(jnp.where(diagonal, poly + NEWTON_FIRST, poly))
        pairs = zip(halves(fine(poly, own)), halves(rows_scr[...]))
        both = fine(tuple(jnp.concatenate(pair, axis=0) for pair in pairs), poly)
        gram[...] = both[0:D]
        rows_scr[...] = both[D:]

    pl.loop(0, NS_ITERS - 2)(lambda _: turn(False))
    turn(True)
    own = halves(gram[...])
    rows = rows_scr[...]
    once = fine(halves(rows), own)
    twice = fine(halves(once), own)
    rows_scr[...] = NEWTON_FIRST * rows + NEWTON_SECOND * once + NEWTON_THIRD * twice

    def send(k, value):
        value = value.astype(BF).reshape(4, 8, D)
        out[:, 0, :, D * k : D * (k + 1)] = value
        out[:, 1, :, D * k : D * (k + 1)] = value

    @pl.when(role == 2)
    def _():
        high, low = halves(rows_scr[0:32, :])
        for k in range(2):
            send(k, dot(high, matrix[k]) + dot(low, matrix[k]))

    @pl.when(role != 2)
    def _():
        for k in range(2):
            send(k, rows_scr[32 * k : 32 * (k + 1), :])


def rows4(is_left, value):
    return jnp.where(is_left, value[0:4], value[4:8])


def natural(ups):
    parts = [
        jnp.concatenate([ups[:, D * q + 128 * part : D * q + 128 * (part + 1)] for q in range(4)], axis=1)
        for part in range(4)
    ]
    return dot_t(jnp.concatenate(parts, axis=0).astype(BF), regroup())


def momenta_kernel(
    core, grads, grads_other, factors, vec, attn_m, up_m, down_m, vec_m, vec_s,
    attn_mom, up_mom, down_mom, vec_mom, vec_sec, vec_new, vec_copy, ups, downs,
):
    is_left = core[0] == 0
    factor = factors[0:1, 0:1]

    def both(first, last):
        mine, other = grads[:, first:last], grads_other[:, first:last]
        left = jnp.where(is_left, mine, other)
        right = jnp.where(is_left, other, mine)
        return rows4(is_left, left), rows4(is_left, right)

    pairs = [both(D * k, D * (k + 1)) for k in range(2)]
    for m in range(4):
        attn_mom[m] = MOMENTUM_DECAY * attn_m[m] + factor * pairs[m // 2][m % 2]
    high, low = halves(jnp.concatenate(both(UP_LANE, DOWN_LANE), axis=1))
    ups[0:4, :] = high.astype(F32)
    ups[4:8, :] = low.astype(F32)
    moved = natural(ups)
    for part in range(4):
        cols = slice(D * part, D * (part + 1))
        grad = moved[8 * part : 8 * part + 4] + moved[8 * part + 4 : 8 * part + 8]
        up_mom[:, cols] = MOMENTUM_DECAY * up_m[:, cols] + factor * grad
    sides = both(DOWN_LANE, VEC_LANE)
    for q in range(4):
        grad = sides[q // 2][:, D * (q % 2) : D * (q % 2 + 1)]
        for i in range(4):
            downs[4 * i + q : 4 * i + q + 1, :] = grad[i : i + 1]
    down_mom[...] = MOMENTUM_DECAY * down_m[...] + factor * downs[...]
    clipped = factor * rows4(is_left, grads[:, VEC_LANE:BLOCK])[:, 0:12]
    first = BETA_FIRST * vec_m[...] + (1.0 - BETA_FIRST) * clipped
    second = BETA_SECOND * vec_s[...] + (1.0 - BETA_SECOND) * clipped * clipped
    vec_mom[...] = first
    vec_sec[...] = second
    first_hat = first / (1.0 - BETA_FIRST**STEP)
    second_hat = second / (1.0 - BETA_SECOND**STEP)
    new = vec[...] - RATE_VECTOR * first_hat / (jnp.sqrt(second_hat) + ADAM_EPSILON)
    vec_new[...] = new
    vec_copy[...] = new.astype(BF)


def update_kernel(
    core, got, attn, up, down, attn_new, up_new, down_new, attn_copy, up_copy, down_copy, ups, downs
):
    is_left = core[0] == 0
    keep_share = 1.0 - RATE_MATRIX * DECAY_MATRIX
    for m in range(4):
        new = attn[m] * keep_share - RATE_MATRIX * rows4(is_left, got[m, :, 0:512].astype(F32))
        attn_new[m] = new
        attn_copy[m] = new.astype(BF)
    ups[0:4, :] = rows4(is_left, jnp.concatenate([got[4].astype(F32), got[5].astype(F32)], axis=1))
    ups[4:8, :] = jnp.zeros((4, FF), F32)
    rate = RATE_MATRIX * math.sqrt(max(1.0, FF / D))
    moved = natural(ups)
    for part in range(4):
        cols = slice(D * part, D * (part + 1))
        up_new[:, cols] = up[:, cols] * keep_share - rate * moved[8 * part : 8 * part + 4]
    up_copy[...] = up_new[...].astype(BF)
    rate = RATE_MATRIX * math.sqrt(max(1.0, D / FF))
    for q in range(4):
        step = rows4(is_left, got[6 + q // 2, :, D * (q % 2) : D * (q % 2 + 1)].astype(F32))
        for i in range(4):
            downs[4 * i + q : 4 * i + q + 1, :] = step[i : i + 1]
    down_new[...] = down[...] * keep_share - rate * downs[...]
    down_copy[...] = down_new[...].astype(BF)


def swap(value):
    return lax.ppermute(value, "c", [(0, 1), (1, 0)])


def to_chips(value):
    return lax.all_to_all(value, CHIPS, 0, 0, tiled=True)


def body(
    block_input, cotangent, segment_ids, attn_master, up_master, down_master, vec_master,
    attn_moment, up_moment, down_moment, vec_moment, vec_second,
):
    c = lax.axis_index("c")
    core = c.reshape(1).astype(jnp.int32)
    role = lax.axis_index("y").reshape(1).astype(jnp.int32)
    plane = (lax.axis_index("x") * 4 + lax.axis_index("z")).reshape(1).astype(jnp.int32)
    core, role, plane = lax.optimization_barrier((core, role, plane))

    keep, send = call(
        pack_kernel,
        [((8, BLOCK), BF)] * 2,
        [core, attn_master, up_master, down_master, vec_master.T, attn_moment, up_moment, down_moment],
        scratch=[
            pltpu.VMEM((4, 4, D), F32), pltpu.VMEM((4, FF), F32), pltpu.VMEM((16, D), F32), pltpu.VMEM((4, 12), F32),
            pltpu.VMEM((4, 4, D), F32), pltpu.VMEM((4, FF), F32), pltpu.VMEM((16, D), F32),
            pltpu.VMEM((8, 3 * FF), F32), pltpu.VMEM((8, BLOCK), F32), pltpu.VMEM((32, D), F32),
            pltpu.SemaphoreType.DMA((7,)),
        ],
        smem=(0,),
        far=range(1, 8),
    )
    message, message_mom = call(
        spread_kernel, [((64, 8, BLOCK), BF), ((64, 8, 1024), BF)], [core, keep, swap(send)], smem=(0,)
    )
    own = to_chips(message)
    own, message_mom = lax.optimization_barrier((own, message_mom))
    other = swap(own)
    mom = to_chips(message_mom).reshape(D, 1024)
    own, other = own.reshape(D, BLOCK), other.reshape(D, BLOCK)
    q, k, v, soft, vec, acts_own, acts_sent, first, normed, scale, slope, other = call(
        forward_kernel,
        [((ROW, D), BF)] * 3
        + [((H // 2, 2 * ROW, ROW), F32), ((16, D), F32), ((ROW, ACTS), BF), ((ROW, ACTS), BF)]
        + [((ROW, D), F32), ((ROW, D), F32), ((ROW, 1), F32), ((ROW, FF), F32), ((D, 3072), BF)],
        [core, block_input, own, other, segment_ids],
        scratch=[
            pltpu.VMEM((ROW, D), F32), pltpu.VMEM((2, ROW, D), BF), pltpu.VMEM((ROW, FF), BF),
            pltpu.SemaphoreType.DMA((3,)),
        ],
        smem=(0,),
        args=(1, 4),
        far=(3,),
        flops=8 * 2 * ROW * D * D,
    )
    acts_other = swap(acts_sent)
    layer_out, base, ygrads, keep, send, vg = call(
        backward_kernel,
        [((ROW, D), BF), ((ROW, D), F32), ((4, ROW, D), BF), ((ROW, GRADS), BF), ((ROW, GRADS), BF), ((16, D), F32)],
        [
            core, block_input, acts_own, acts_sent, first, vec, own, other, cotangent, slope, normed, scale,
            q, k, v, soft,
        ],
        scratch=[
            pltpu.VMEM((ROW, D), F32), pltpu.VMEM((ROW, FF), BF), pltpu.VMEM((ROW, D), BF), pltpu.VMEM((ROW, D), BF),
        ],
        smem=(0,),
        args=(1, 8),
        results=(0,),
        flops=18 * 2 * ROW * D * D,
    )
    got, vg_other = swap(send), swap(vg)
    (input_grad,) = call(
        input_kernel,
        [((ROW, D), BF)],
        [core, base, ygrads, own, other],
        smem=(0,),
        results=(0,),
        flops=3 * 2 * ROW * D * D,
    )
    got, input_grad = lax.optimization_barrier((got, input_grad))
    (weights,) = call(
        weights_kernel,
        [((D, BLOCK), BF)],
        [acts_own, acts_other, keep, got, vg, vg_other],
        scratch=[pltpu.VMEM((128, D), F32)],
        flops=2 * 256 * 512 * 3072,
    )
    weights, mom = lax.optimization_barrier((weights, mom))
    weights = to_chips(weights.reshape(64, 8, BLOCK))
    grads, pay = call(reduce_kernel, [((8, BLOCK), F32), ((64, 8, 1152), BF)], [weights])
    pay = to_chips(pay)
    pay, mom, grads = lax.optimization_barrier((pay, mom, grads))
    (note,) = call(note_kernel, [((8, 128), F32)], [pay.reshape(D, 1152)])
    note_other, grads_other = swap(note), swap(grads)
    (mom,) = call(near_kernel, [((D, 1024), BF)], [mom], scratch=[pltpu.SemaphoreType.DMA], far=(0,))
    note_other, grads_other, mom = lax.optimization_barrier((note_other, grads_other, mom))
    matrix, gram, clip_norm, factors = call(
        gram_kernel,
        [((2, D, D), BF), ((TALL, HALF), F32), ((1, 1), F32), ((8, 128), F32)],
        [role, pay.reshape(D, 1152), mom, note, note_other],
        smem=(0,),
        results=(2,),
        flops=2 * 2 * D * D * D,
    )
    gram_other = swap(gram)
    *moms, vec_mom, vec_sec, vec_new, vec_copy = call(
        momenta_kernel,
        [((4, 4, D), F32), ((4, FF), F32), ((16, D), F32)] + [((4, 12), F32)] * 3 + [((4, 12), BF)],
        [
            core, grads, grads_other, factors, vec_master.T, attn_moment, up_moment, down_moment,
            vec_moment.T, vec_second.T,
        ],
        scratch=[pltpu.VMEM((8, FF), F32), pltpu.VMEM((16, D), F32)],
        smem=(0,),
        args=range(4, 10),
        results=range(7),
    )
    gram_other, *moms = lax.optimization_barrier((gram_other, *moms))
    vecs = [t.T for t in (vec_mom, vec_sec, vec_new, vec_copy)]
    (orth,) = call(
        newton_kernel,
        [((4, 2, 8, 1024), BF)],
        [role, plane, matrix, gram, gram_other],
        scratch=[pltpu.VMEM((D, D), F32), pltpu.VMEM((64, D), F32)],
        smem=(0, 1),
        flops=14 * 3 * 2 * D * D * D,
    )
    orth = orth.reshape(8, 8, 1024)
    orth = lax.all_to_all(orth, ("y", "c"), 0, 0, tiled=True)
    news = call(
        update_kernel,
        [((4, 4, D), F32), ((4, FF), F32), ((16, D), F32), ((4, 4, D), BF), ((4, FF), BF), ((16, D), BF)],
        [core, orth, attn_master, up_master, down_master],
        scratch=[pltpu.VMEM((8, FF), F32), pltpu.VMEM((16, D), F32)],
        smem=(0,),
        args=range(2, 5),
        results=range(6),
    )
    return (layer_out, input_grad, clip_norm[0, 0], *moms, *news, *vecs)


def solution(mesh):
    grid = Mesh(mesh.devices.reshape(4, 4, 4, 2), ("x", "z", "y", "c"))
    row, mat, vec = P(ALL, None), P(None, ALL, None), P(None, ALL)
    return jax.shard_map(
        body,
        mesh=grid,
        in_specs=(row, row, row, mat, row, row, vec, mat, row, row, vec, vec),
        out_specs=(row, row, P(), mat, row, row, mat, row, row, mat, row, row, vec, vec, vec, vec),
        check_vma=False,
    )
```

```python
import math

import jax
import jax.numpy as jnp
from jax import lax
from jax.experimental import pallas as pl
from jax.experimental.pallas import tpu as pltpu
from jax.sharding import Mesh, PartitionSpec as P

D = 512
FF = 2048
H = 8
HD = 64
ROW = 128
STEP = 10
NS_ITERS = 5
HALF = 256

MASKED_SCORE = -1e30
NORM_EPSILON = 1e-05
CLIP_LIMIT = 1.0
MOMENTUM_DECAY = 0.95
RATE_MATRIX = 0.5
DECAY_MATRIX = 0.01
BETA_FIRST = 0.9
BETA_SECOND = 0.999
RATE_VECTOR = 0.2
ADAM_EPSILON = 1e-08
NEWTON_FIRST = 3.4445
NEWTON_SECOND = -4.775
NEWTON_THIRD = 2.0315

CHIPS = ("x", "z", "y")
ALL = ("x", "z", "y", "c")
BF = jnp.bfloat16
F32 = jnp.float32
VMEM_LIMIT = 12 * 1024 * 1024


def call(kernel, outs, ins, scratch=(), smem=(), args=(), far=(), results=(), away=(), flops=0, limit=VMEM_LIMIT):
    spec = [
        pl.BlockSpec(memory_space=pltpu.SMEM if i in smem else pl.ANY if i in far else pltpu.VMEM)
        for i in range(len(ins))
    ]
    placed = [
        x if i in smem or i in args
        else pltpu.with_memory_space_constraint(x, pltpu.HBM if i in far else pltpu.VMEM)
        for i, x in enumerate(ins)
    ]
    shapes = [
        jax.ShapeDtypeStruct(s, t) if i in results else pltpu.HBM(s, t) if i in away else pltpu.VMEM(s, t)
        for i, (s, t) in enumerate(outs)
    ]
    moved = sum(math.prod(a.shape) * a.dtype.itemsize for a in ins)
    return pl.pallas_call(
        kernel,
        out_shape=shapes,
        in_specs=spec,
        out_specs=[
            pl.BlockSpec(memory_space=pl.ANY if i in away else pltpu.VMEM) for i in range(len(shapes))
        ],
        scratch_shapes=list(scratch),
        compiler_params=pltpu.CompilerParams(vmem_limit_bytes=limit),
        cost_estimate=pl.CostEstimate(flops=flops, bytes_accessed=moved, transcendentals=0),
    )(*placed)


def dot(a, b):
    return jnp.dot(a, b, preferred_element_type=F32)


def dot_t(a, b):
    return lax.dot_general(a, b, (((1,), (1,)), ((), ())), preferred_element_type=F32)


def dot_in(a, b):
    return lax.dot_general(a, b, (((0,), (0,)), ((), ())), preferred_element_type=F32)


O_LANE, UP_LANE, DOWN_LANE, VEC_LANE, BLOCK = 768, 1024, 2048, 3072, 3200
X0, A0, H0, Z0, ACTS = 0, 512, 1024, 1536, 3328
Y0, DU0, DF0, GRADS = 0, 1024, 2048, 2560


def half_lanes(half, size):
    return pl.ds(pl.multiple_of(half * size, size), size)


def regroup():
    source = lax.broadcasted_iota(jnp.int32, (D, D), 0)
    target = lax.broadcasted_iota(jnp.int32, (D, D), 1)
    return jnp.where(target == (source & 3) * 128 + (source >> 2), 1.0, 0.0).astype(BF)


def pack_kernel(
    core, attn, up, down, vec, attn_m, up_m, down_m, keep, send,
    attn_v, up_v, down_v, vec_v, attn_mv, up_mv, down_mv, full, block, stage, sems,
):
    c = core[0]
    copies = [
        pltpu.make_async_copy(source, target, sems.at[i])
        for i, (source, target) in enumerate(
            [(attn, attn_v), (up, up_v), (down, down_v), (vec, vec_v), (attn_m, attn_mv), (up_m, up_mv), (down_m, down_mv)]
        )
    ]
    for copy in copies:
        copy.start()
    move = regroup()
    for copy in copies:
        copy.wait()
    for first, attn_one, up_one, down_one in ((0, attn_v, up_v, down_v), (4, attn_mv, up_mv, down_mv)):
        rows = slice(first, first + 4)
        for m in range(4):
            full[rows, D * m : D * (m + 1)] = attn_one[m]
        for part in range(4):
            row = 8 * part + first
            stage[row : row + 4, :] = up_one[:, D * part : D * (part + 1)]
        for i in range(4):
            for q in range(4):
                lane = 2 * FF + D * q
                full[first + i : first + i + 1, lane : lane + D] = down_one[4 * i + q : 4 * i + q + 1, :]
    moved = dot(stage[...].astype(BF), move)
    for part in range(4):
        for q in range(4):
            lane = FF + D * q + 128 * part
            full[:, lane : lane + 128] = moved[8 * part : 8 * (part + 1), 128 * q : 128 * (q + 1)]
    for target, half in ((keep, c), (send, 1 - c)):
        for m in range(4):
            lanes = pl.ds(pl.multiple_of(D * m + HALF * half, HALF), HALF)
            block[0:4, HALF * m : HALF * (m + 1)] = full[0:4, lanes]
        for m in range(2):
            lanes = pl.ds(pl.multiple_of(2 * D * m + D * half, D), D)
            block[4:8, D * m : D * (m + 1)] = full[4:8, lanes]
        block[:, UP_LANE:DOWN_LANE] = full[:, pl.ds(pl.multiple_of(FF + 1024 * half, 1024), 1024)]
        for q in range(4):
            lanes = pl.ds(pl.multiple_of(2 * FF + D * q + HALF * half, HALF), HALF)
            lane = DOWN_LANE + HALF * q
            block[0:4, lane : lane + HALF] = full[0:4, lanes]
        lanes = pl.ds(pl.multiple_of(2 * FF + 1024 * half, 1024), 1024)
        block[4:8, DOWN_LANE:VEC_LANE] = full[4:8, lanes]
        block[:, VEC_LANE:BLOCK] = jnp.zeros((8, 128), F32)
        block[0:4, VEC_LANE : VEC_LANE + 12] = vec_v[...]
        target[...] = block[...].astype(BF)


def role_lanes(block, note):
    gap = jnp.zeros((8, 512), block.dtype)
    tail = [] if note is None else [note]
    return [
        jnp.concatenate([block[:, 0:512], gap] + tail, axis=1),
        jnp.concatenate([block[:, 512:1024], gap] + tail, axis=1),
        jnp.concatenate([block[:, UP_LANE:DOWN_LANE]] + tail, axis=1),
        jnp.concatenate([block[:, DOWN_LANE:VEC_LANE]] + tail, axis=1),
    ]


def spread_kernel(core, keep, got, message, message_mom):
    mine, other = keep[...].astype(F32), got[...].astype(F32)
    is_left = core[0] == 0
    left, right = jnp.where(is_left, mine, other), jnp.where(is_left, other, mine)
    block = jnp.concatenate([left[0:4], right[0:4]], axis=0).astype(BF)
    moms = role_lanes(jnp.concatenate([left[4:8], right[4:8]], axis=0).astype(BF), None)
    for i in range(64):
        message[i] = block
        message_mom[i] = moms[i % 4]


def by_head(pair):
    low = (lax.broadcasted_iota(jnp.int32, (ROW, ROW), 1) < HD).astype(F32)
    return jnp.concatenate([pair * low.astype(BF), pair * (1.0 - low).astype(BF)], axis=0)


def abreast(stacked):
    return jnp.concatenate([stacked[0:ROW], stacked[ROW:]], axis=1)


def norm_parts(values):
    centred = values - jnp.mean(values, axis=-1, keepdims=True)
    scale = lax.rsqrt(jnp.mean(centred * centred, axis=-1, keepdims=True) + NORM_EPSILON)
    return centred * scale, scale


def norm_back(grad, gain, normed, scale):
    grad = grad * gain
    return scale * (
        grad
        - jnp.mean(grad, axis=-1, keepdims=True)
        - normed * jnp.mean(grad * normed, axis=-1, keepdims=True)
    )


def forward_kernel(
    core, x, w_own, w_far, seg, q_out, k_out, v_out, p_out, vec_out, keep, send, first_out, norm_out, scale_out,
    slope, w_other, wide, pair_scr, acts, sems,
):
    c = core[0]
    copies = []
    for i in range(3):
        lanes = pl.ds(1024 * i, 1024)
        copies.append(pltpu.make_async_copy(w_far.at[:, lanes], w_other.at[:, lanes], sems.at[i]))
        copies[i].start()
    sides = ((c, w_own), (1 - c, w_other))
    vec = w_own[:, VEC_LANE:BLOCK].astype(F32).T[:16]
    vec_out[...] = vec
    moved = dot(vec[8:16].astype(BF), regroup())
    for part in range(4):
        for q in range(4):
            vec_out[8 + q : 9 + q, 128 * part : 128 * (part + 1)] = moved[part : part + 1, 128 * q : 128 * (q + 1)]
    tokens = x[...]
    pair_scr[0] = tokens
    names = jnp.broadcast_to(seg[...].astype(F32), (ROW, ROW))
    gap = names - names.T
    same = jnp.concatenate([gap, gap], axis=0) == 0.0
    for half, w in sides:
        if w is w_other:
            copies[0].wait()
        product = dot(tokens, w[:, 0:O_LANE])
        q = (product[:, 0:HALF] + vec_out[0:1, half_lanes(half, HALF)]).astype(BF)
        k = product[:, HALF : 2 * HALF].astype(BF)
        v = (product[:, 2 * HALF : O_LANE] + vec_out[1:2, half_lanes(half, HALF)]).astype(BF)
        for target, value in ((q_out, q), (k_out, k), (v_out, v)):
            target[:, half_lanes(half, HALF)] = value
        for pair in range(2):
            cols = slice(128 * pair, 128 * pair + 128)
            scores = dot_t(by_head(q[:, cols]), k[:, cols]) * (HD ** (-0.5))
            scores = jnp.where(same, scores, MASKED_SCORE)
            expo = jnp.exp(scores - jnp.max(scores, axis=-1, keepdims=True))
            soft = expo / jnp.sum(expo, axis=-1, keepdims=True)
            p_out[2 * half + pair] = soft
            attended = dot(abreast(soft.astype(BF)), by_head(v[:, cols]))
            lanes = pl.ds(pl.multiple_of(HALF * half + 128 * pair, 128), 128)
            pair_scr[1, :, lanes] = attended.astype(BF)
    for half, w in sides:
        wide[:, half_lanes(half, HALF)] = dot(pair_scr[1], w[:, O_LANE:UP_LANE])
    normed, scale = norm_parts(tokens.astype(F32) + wide[...] + vec[2:3])
    norm_out[...] = normed
    scale_out[...] = scale
    first = normed * vec[4:5] + vec[5:6]
    first_out[...] = first
    first_low = first.astype(BF)
    root = math.sqrt(2.0 / math.pi)
    copies[1].wait()
    for half, w in sides:
        for k in range(2):
            bias = vec_out[pl.ds(8 + 2 * half + k, 1), :]
            u = dot(first_low, w[:, UP_LANE + D * k : UP_LANE + D * (k + 1)]) + bias
            square = u * u
            tanh = jnp.tanh(root * (u + 0.044715 * (square * u)))
            gate = 0.5 * (1.0 + tanh)
            cols = pl.ds(pl.multiple_of(1024 * half + D * k, D), D)
            slope[:, cols] = gate + 0.5 * u * (1.0 - tanh * tanh) * (root * (1.0 + 3 * 0.044715 * square))
            acts[:, cols] = (u * gate).astype(BF)
    for target, half in ((keep, c), (send, 1 - c)):
        target[:, X0:A0] = tokens
        target[:, A0:H0] = pair_scr[half]
        target[:, H0:Z0] = first_low
        target[:, Z0 : Z0 + 1024] = acts[:, half_lanes(half, 1024)]
        target[:, Z0 + 1024 : ACTS] = jnp.zeros((ROW, ACTS - Z0 - 1024), BF)
    copies[2].wait()


def backward_kernel(
    core, x, acts_own, acts_sent, first, vec_in, w_own, w_other, cot, slope, normed_in, scale_in, q_in, k_in, v_in, p_in,
    out, base, y_scr, keep, send, vg, wide, du_scr, df_scr, do_scr,
):
    c = core[0]
    sides = ((c, w_own), (1 - c, w_other))
    vec = vec_in[...]
    dq_scr, dk_scr, dv_scr, da_scr = (y_scr.at[i] for i in range(4))
    for half, w in sides:
        feed = jnp.zeros((ROW, HALF), F32)
        for group, acts in ((c, acts_own), (1 - c, acts_sent)):
            for k in range(2):
                lanes = pl.ds(pl.multiple_of(DOWN_LANE + 2 * HALF * group + HALF * k, HALF), HALF)
                feed = feed + dot(acts[:, Z0 + D * k : Z0 + D * (k + 1)], w[:, lanes])
        wide[:, half_lanes(half, HALF)] = feed
    residual = wide[...] + vec[3:4] + first[...] + x[...].astype(F32)
    normed, scale = norm_parts(residual)
    out[...] = (normed * vec[6:7] + vec[7:8]).astype(BF)
    grad = cot[...].astype(F32)
    vg[...] = jnp.zeros((16, D), F32)
    vg[6:7, :] = jnp.sum(grad * normed, axis=0, keepdims=True)
    vg[7:8, :] = jnp.sum(grad, axis=0, keepdims=True)
    grad2 = norm_back(grad, vec[6:7], normed, scale)
    df_scr[...] = grad2.astype(BF)
    vg[3:4, :] = jnp.sum(df_scr[...].astype(F32), axis=0, keepdims=True)
    for q in range(4):
        lane = DOWN_LANE + HALF * q
        dz = dot_t(df_scr[:, half_lanes(c, HALF)], w_own[:, lane : lane + HALF])
        dz = dz + dot_t(df_scr[:, half_lanes(1 - c, HALF)], w_other[:, lane : lane + HALF])
        du = (dz * slope[:, D * q : D * (q + 1)]).astype(BF)
        du_scr[:, D * q : D * (q + 1)] = du
        vg[8 + q : 9 + q, :] = jnp.sum(du.astype(F32), axis=0, keepdims=True)
    dfirst = grad2
    for half, w in sides:
        dfirst = dfirst + dot_t(du_scr[:, half_lanes(half, 1024)], w[:, UP_LANE:DOWN_LANE])
    normed1 = normed_in[...]
    vg[4:5, :] = jnp.sum(dfirst * normed1, axis=0, keepdims=True)
    vg[5:6, :] = jnp.sum(dfirst, axis=0, keepdims=True)
    dres = norm_back(dfirst, vec[4:5], normed1, scale_in[...])
    da_scr[...] = dres.astype(BF)
    vg[2:3, :] = jnp.sum(da_scr[...].astype(F32), axis=0, keepdims=True)
    dattended = jnp.zeros((ROW, D), F32)
    for half, w in sides:
        dattended = dattended + dot_t(da_scr[:, half_lanes(half, HALF)], w[:, O_LANE:UP_LANE])
    do_scr[...] = dattended.astype(BF)
    share = HD ** (-0.5)
    pairs = [slice(128 * pair, 128 * pair + 128) for pair in range(H // 2)]
    dos = [by_head(do_scr[:, cols]) for cols in pairs]
    dsofts = [dot_t(do, v_in[:, cols]) for do, cols in zip(dos, pairs)]
    dss = []
    for pair, dsoft in enumerate(dsofts):
        soft = p_in[pair]
        dss.append((soft * (dsoft - jnp.sum(soft * dsoft, axis=-1, keepdims=True))).astype(BF))
    for pair, cols in enumerate(pairs):
        ds = dss[pair]
        dq_scr[:, cols] = (dot(abreast(ds), by_head(k_in[:, cols])) * share).astype(BF)
        dk_scr[:, cols] = (dot_in(ds, by_head(q_in[:, cols])) * share).astype(BF)
        dv_scr[:, cols] = dot_in(p_in[pair].astype(BF), dos[pair]).astype(BF)
    vg[0:1, :] = jnp.sum(dq_scr[...].astype(F32), axis=0, keepdims=True)
    vg[1:2, :] = jnp.sum(dv_scr[...].astype(F32), axis=0, keepdims=True)
    for target, half in ((keep, c), (send, 1 - c)):
        target[:, 0:D] = y_scr[half]
        target[:, D : 2 * D] = y_scr[2 + half]
        target[:, DU0:DF0] = du_scr[:, half_lanes(half, 1024)]
        target[:, DF0:GRADS] = df_scr[...]
    base[...] = grad2 + dres


def input_kernel(core, base, grads, w_own, w_other, out):
    total = base[...]
    for half, w in ((core[0], w_own), (1 - core[0], w_other)):
        for i in range(3):
            total = total + dot_t(grads[i, :, half_lanes(half, HALF)], w[:, HALF * i : HALF * (i + 1)])
    out[...] = total.astype(BF)


def weights_kernel(acts, acts_other, keep, got, vg, vg_other, out, vec):
    def both(one, two, first, last):
        return jnp.concatenate([one[:, first:last], two[:, first:last]], axis=0)

    out[:, UP_LANE:DOWN_LANE] = dot_in(both(acts, acts_other, H0, Z0), both(keep, got, DU0, DF0)).astype(BF)
    down = both(keep, got, DF0, GRADS)
    for k in range(2):
        lane = DOWN_LANE + D * k
        units = both(acts, acts_other, Z0 + D * k, Z0 + D * (k + 1))
        out[:, lane : lane + D] = dot_in(units, down).astype(BF)
    for k in range(2):
        left = both(acts, acts_other, D * k, D * (k + 1))
        out[:, D * k : D * (k + 1)] = dot_in(left, both(keep, got, D * k, D * (k + 1))).astype(BF)
    total = vg[...] + vg_other[...]
    vec[...] = jnp.zeros((128, D), F32)
    vec[0:8, :] = total[0:8]
    for part in range(4):
        for q in range(4):
            vec[8 + part : 9 + part, 128 * q : 128 * (q + 1)] = total[8 + q : 9 + q, 128 * part : 128 * (part + 1)]
    vec[8:16, :] = dot_t(vec[8:16, :].astype(BF), regroup())
    out[:, VEC_LANE:BLOCK] = vec[...].T.astype(BF)


def add_up(ref):
    total = ref[0].astype(F32)
    for i in range(1, 64):
        total = total + ref[i].astype(F32)
    return total


def split3(value):
    one = value.astype(BF)
    rest = value - one.astype(F32)
    two = rest.astype(BF)
    three = (rest - two.astype(F32)).astype(BF)
    return one, two, three


def reduce_kernel(got, grads, pay):
    grads[...] = add_up(got)
    own, vec = grads[:, 0:VEC_LANE], grads[:, VEC_LANE:BLOCK]
    square = jnp.sum(own * own) + 0.5 * jnp.sum(vec * vec)
    row = lax.broadcasted_iota(jnp.int32, (8, 128), 0)
    lane = lax.broadcasted_iota(jnp.int32, (8, 128), 1)
    full = jnp.full((8, 128), square, F32)
    one, two, three = split3(full)
    note = jnp.where(lane == 0, one.astype(F32), jnp.where(lane == 1, two.astype(F32), three.astype(F32)))
    note = jnp.where((row == 0) & (lane < 3), note, 0.0).astype(BF)
    rows = role_lanes(grads[:, 0:VEC_LANE].astype(BF), note)
    for i in range(64):
        pay[i] = rows[i % 4]


def halves(value):
    high = value.astype(BF)
    return high, (value - high.astype(F32)).astype(BF)


def fine(a, b):
    ah, al = a
    bh, bl = b
    return dot(jnp.concatenate([ah, ah, al], axis=1), jnp.concatenate([bh, bl, bh], axis=0))


TALL = 3 * HALF + 8


def near_kernel(far, near, sem):
    copy = pltpu.make_async_copy(far, near, sem)
    copy.start()
    copy.wait()


def note_kernel(got, note):
    note[...] = jnp.full((8, 128), jnp.sum(got[:, 1024:1152].astype(F32)), F32)


def gram_kernel(role_ref, got, mom, note, note_other, matrix, gram, clip_out, factor_out):
    role = role_ref[0]
    clip = jnp.sqrt(note[...] + note_other[...])
    factors = CLIP_LIMIT / jnp.maximum(clip, CLIP_LIMIT)
    clip_out[...] = clip[0:1, 0:1]
    factor_out[...] = factors
    factor = factors[0:1, 0:1]

    def make(k):
        cols = slice(D * k, D * (k + 1))
        value = MOMENTUM_DECAY * mom[:, cols].astype(F32) + factor * got[:, cols].astype(F32)
        value = value.astype(BF)
        matrix[k] = value
        value = value.astype(F32)
        return jnp.sum(value * value)

    def finish(product, parts, square):
        for i, (a, b) in enumerate(((0, 0), (0, 1), (1, 1))):
            total = product(a, b, 0)
            for k in range(1, parts):
                total = total + product(a, b, k)
            gram[HALF * i : HALF * (i + 1), :] = total
        gram[3 * HALF : TALL, :] = jnp.full((8, HALF), square, F32)

    def inner(a, b, k):
        return dot_in(matrix[k, :, HALF * a : HALF * (a + 1)], matrix[k, :, HALF * b : HALF * (b + 1)])

    def outer(a, b, k):
        return dot_t(matrix[k, HALF * a : HALF * (a + 1), :], matrix[k, HALF * b : HALF * (b + 1), :])

    @pl.when(role < 2)
    def _():
        square = make(0)
        finish(inner, 1, square)

    @pl.when(role == 2)
    def _():
        square = make(0) + make(1)
        finish(outer, 2, square)

    @pl.when(role == 3)
    def _():
        square = make(0) + make(1)
        finish(inner, 2, square)


def thin(rows, matrix):
    high, low = halves(rows)
    both = dot(jnp.concatenate([high, low], axis=0), matrix[0])
    return both[0 : rows.shape[0]] + (both[rows.shape[0] :] + dot(high, matrix[1]))


def newton_kernel(role_ref, plane_ref, matrix, gram_own, gram_other, out, gram, rows_scr):
    role, plane = role_ref[0], plane_ref[0]
    chips = pl.ds(pl.multiple_of(plane * 32, 32), 32)

    def scaled(total):
        size = jnp.sqrt(total[3 * HALF : 3 * HALF + 1, 0:1]) + 1e-07
        inverse = 1.0 / size
        total = total[0 : 3 * HALF] * (inverse * inverse)
        gram[0:HALF, 0:HALF] = total[0:HALF]
        gram[0:HALF, HALF:D] = total[HALF:D]
        gram[HALF:D, 0:HALF] = total[HALF:D].T
        gram[HALF:D, HALF:D] = total[D : 3 * HALF]
        return inverse

    def rows_of(k):
        return matrix[k, chips, :].astype(F32)

    @pl.when(role < 2)
    def _():
        inverse = scaled(gram_own[...])
        rows_scr[0:32, :] = rows_of(0) * inverse
        rows_scr[32:64, :] = jnp.zeros((32, D), F32)

    @pl.when(role == 2)
    def _():
        inverse = scaled(gram_own[...] + gram_other[...])
        here = lax.broadcasted_iota(jnp.int32, (32, D), 0) + 32 * plane
        there = lax.broadcasted_iota(jnp.int32, (32, D), 1)
        rows_scr[0:32, :] = jnp.where(here == there, 1.0, 0.0) * inverse
        rows_scr[32:64, :] = jnp.zeros((32, D), F32)

    @pl.when(role == 3)
    def _():
        inverse = scaled(gram_own[...] + gram_other[...])
        for k in range(2):
            rows_scr[32 * k : 32 * (k + 1), :] = rows_of(k) * inverse

    diagonal = (
        lax.broadcasted_iota(jnp.int32, (D, D), 0) == lax.broadcasted_iota(jnp.int32, (D, D), 1)
    )

    def polynomial(square):
        poly = NEWTON_SECOND * gram[...] + NEWTON_THIRD * square
        return jnp.where(diagonal, poly + NEWTON_FIRST, poly)

    def turn(_):
        own = halves(gram[...])
        poly = halves(polynomial(dot(own[0], own[0])))
        pairs = zip(halves(fine(poly, own)), halves(rows_scr[...]))
        both = fine(tuple(jnp.concatenate(pair, axis=0) for pair in pairs), poly)
        gram[...] = both[0:D]
        rows_scr[...] = both[D:]

    pl.loop(0, NS_ITERS - 2)(turn)
    own = halves(gram[...])
    poly = halves(polynomial(fine(own, own)))
    rows = thin(rows_scr[...], poly)

    def through(value):
        return thin(thin(thin(value, poly), poly), own)

    once = through(rows)
    twice = through(once)
    rows_scr[...] = NEWTON_FIRST * rows + NEWTON_SECOND * once + NEWTON_THIRD * twice

    def send(k, value):
        value = value.astype(BF).reshape(4, 8, D)
        out[:, 0, :, D * k : D * (k + 1)] = value
        out[:, 1, :, D * k : D * (k + 1)] = value

    @pl.when(role == 2)
    def _():
        high, low = halves(rows_scr[0:32, :])
        for k in range(2):
            send(k, dot(high, matrix[k]) + dot(low, matrix[k]))

    @pl.when(role != 2)
    def _():
        for k in range(2):
            send(k, rows_scr[32 * k : 32 * (k + 1), :])


def rows4(is_left, value):
    return jnp.where(is_left, value[0:4], value[4:8])


def natural(ups):
    parts = [
        jnp.concatenate([ups[:, D * q + 128 * part : D * q + 128 * (part + 1)] for q in range(4)], axis=1)
        for part in range(4)
    ]
    return dot_t(jnp.concatenate(parts, axis=0).astype(BF), regroup())


def momenta_kernel(
    core, grads, grads_other, factors, vec, attn_m, up_m, down_m, vec_m, vec_s,
    attn_mom, up_mom, down_mom, vec_mom, vec_sec, vec_new, vec_copy, ups, downs,
):
    is_left = core[0] == 0
    factor = factors[0:1, 0:1]

    def both(first, last):
        mine, other = grads[:, first:last], grads_other[:, first:last]
        left = jnp.where(is_left, mine, other)
        right = jnp.where(is_left, other, mine)
        return rows4(is_left, left), rows4(is_left, right)

    pairs = [both(D * k, D * (k + 1)) for k in range(2)]
    for m in range(4):
        attn_mom[m] = MOMENTUM_DECAY * attn_m[m] + factor * pairs[m // 2][m % 2]
    high, low = halves(jnp.concatenate(both(UP_LANE, DOWN_LANE), axis=1))
    ups[0:4, :] = high.astype(F32)
    ups[4:8, :] = low.astype(F32)
    moved = natural(ups)
    for part in range(4):
        cols = slice(D * part, D * (part + 1))
        grad = moved[8 * part : 8 * part + 4] + moved[8 * part + 4 : 8 * part + 8]
        up_mom[:, cols] = MOMENTUM_DECAY * up_m[:, cols] + factor * grad
    sides = both(DOWN_LANE, VEC_LANE)
    for q in range(4):
        grad = sides[q // 2][:, D * (q % 2) : D * (q % 2 + 1)]
        for i in range(4):
            downs[4 * i + q : 4 * i + q + 1, :] = grad[i : i + 1]
    down_mom[...] = MOMENTUM_DECAY * down_m[...] + factor * downs[...]
    clipped = factor * rows4(is_left, grads[:, VEC_LANE:BLOCK])[:, 0:12]
    first = BETA_FIRST * vec_m[...] + (1.0 - BETA_FIRST) * clipped
    second = BETA_SECOND * vec_s[...] + (1.0 - BETA_SECOND) * clipped * clipped
    vec_mom[...] = first
    vec_sec[...] = second
    first_hat = first / (1.0 - BETA_FIRST**STEP)
    second_hat = second / (1.0 - BETA_SECOND**STEP)
    new = vec[...] - RATE_VECTOR * first_hat / (jnp.sqrt(second_hat) + ADAM_EPSILON)
    vec_new[...] = new
    vec_copy[...] = new.astype(BF)


def update_kernel(
    core, got, attn, up, down, attn_new, up_new, down_new, attn_copy, up_copy, down_copy, ups, downs
):
    is_left = core[0] == 0
    keep_share = 1.0 - RATE_MATRIX * DECAY_MATRIX
    for m in range(4):
        new = attn[m] * keep_share - RATE_MATRIX * rows4(is_left, got[m, :, 0:512].astype(F32))
        attn_new[m] = new
        attn_copy[m] = new.astype(BF)
    ups[0:4, :] = rows4(is_left, jnp.concatenate([got[4].astype(F32), got[5].astype(F32)], axis=1))
    ups[4:8, :] = jnp.zeros((4, FF), F32)
    rate = RATE_MATRIX * math.sqrt(max(1.0, FF / D))
    moved = natural(ups)
    for part in range(4):
        cols = slice(D * part, D * (part + 1))
        up_new[:, cols] = up[:, cols] * keep_share - rate * moved[8 * part : 8 * part + 4]
    up_copy[...] = up_new[...].astype(BF)
    rate = RATE_MATRIX * math.sqrt(max(1.0, D / FF))
    for q in range(4):
        step = rows4(is_left, got[6 + q // 2, :, D * (q % 2) : D * (q % 2 + 1)].astype(F32))
        for i in range(4):
            downs[4 * i + q : 4 * i + q + 1, :] = step[i : i + 1]
    down_new[...] = down[...] * keep_share - rate * downs[...]
    down_copy[...] = down_new[...].astype(BF)


def swap(value):
    return lax.ppermute(value, "c", [(0, 1), (1, 0)])


def to_chips(value):
    return lax.all_to_all(value, CHIPS, 0, 0, tiled=True)


def body(
    block_input, cotangent, segment_ids, attn_master, up_master, down_master, vec_master,
    attn_moment, up_moment, down_moment, vec_moment, vec_second,
):
    c = lax.axis_index("c")
    core = c.reshape(1).astype(jnp.int32)
    role = lax.axis_index("y").reshape(1).astype(jnp.int32)
    plane = (lax.axis_index("x") * 4 + lax.axis_index("z")).reshape(1).astype(jnp.int32)
    core, role, plane = lax.optimization_barrier((core, role, plane))

    keep, send = call(
        pack_kernel,
        [((8, BLOCK), BF)] * 2,
        [core, attn_master, up_master, down_master, vec_master.T, attn_moment, up_moment, down_moment],
        scratch=[
            pltpu.VMEM((4, 4, D), F32), pltpu.VMEM((4, FF), F32), pltpu.VMEM((16, D), F32), pltpu.VMEM((4, 12), F32),
            pltpu.VMEM((4, 4, D), F32), pltpu.VMEM((4, FF), F32), pltpu.VMEM((16, D), F32),
            pltpu.VMEM((8, 3 * FF), F32), pltpu.VMEM((8, BLOCK), F32), pltpu.VMEM((32, D), F32),
            pltpu.SemaphoreType.DMA((7,)),
        ],
        smem=(0,),
        far=range(1, 8),
    )
    message, message_mom = call(
        spread_kernel, [((64, 8, BLOCK), BF), ((64, 8, 1024), BF)], [core, keep, swap(send)], smem=(0,)
    )
    own = to_chips(message)
    own, message_mom = lax.optimization_barrier((own, message_mom))
    other = swap(own)
    mom = to_chips(message_mom).reshape(D, 1024)
    own, other = own.reshape(D, BLOCK), other.reshape(D, BLOCK)
    q, k, v, soft, vec, acts_own, acts_sent, first, normed, scale, slope, other = call(
        forward_kernel,
        [((ROW, D), BF)] * 3
        + [((H // 2, 2 * ROW, ROW), F32), ((16, D), F32), ((ROW, ACTS), BF), ((ROW, ACTS), BF)]
        + [((ROW, D), F32), ((ROW, D), F32), ((ROW, 1), F32), ((ROW, FF), F32), ((D, 3072), BF)],
        [core, block_input, own, other, segment_ids],
        scratch=[
            pltpu.VMEM((ROW, D), F32), pltpu.VMEM((2, ROW, D), BF), pltpu.VMEM((ROW, FF), BF),
            pltpu.SemaphoreType.DMA((3,)),
        ],
        smem=(0,),
        args=(1, 4),
        far=(3,),
        flops=8 * 2 * ROW * D * D,
    )
    acts_other = swap(acts_sent)
    layer_out, base, ygrads, keep, send, vg = call(
        backward_kernel,
        [((ROW, D), BF), ((ROW, D), F32), ((4, ROW, D), BF), ((ROW, GRADS), BF), ((ROW, GRADS), BF), ((16, D), F32)],
        [
            core, block_input, acts_own, acts_sent, first, vec, own, other, cotangent, slope, normed, scale,
            q, k, v, soft,
        ],
        scratch=[
            pltpu.VMEM((ROW, D), F32), pltpu.VMEM((ROW, FF), BF), pltpu.VMEM((ROW, D), BF), pltpu.VMEM((ROW, D), BF),
        ],
        smem=(0,),
        args=(1, 8),
        results=(0,),
        flops=18 * 2 * ROW * D * D,
    )
    got, vg_other = swap(send), swap(vg)
    (input_grad,) = call(
        input_kernel,
        [((ROW, D), BF)],
        [core, base, ygrads, own, other],
        smem=(0,),
        results=(0,),
        flops=3 * 2 * ROW * D * D,
    )
    got, input_grad = lax.optimization_barrier((got, input_grad))
    (weights,) = call(
        weights_kernel,
        [((D, BLOCK), BF)],
        [acts_own, acts_other, keep, got, vg, vg_other],
        scratch=[pltpu.VMEM((128, D), F32)],
        flops=2 * 256 * 512 * 3072,
    )
    weights, mom = lax.optimization_barrier((weights, mom))
    weights = to_chips(weights.reshape(64, 8, BLOCK))
    grads, pay = call(reduce_kernel, [((8, BLOCK), F32), ((64, 8, 1152), BF)], [weights])
    pay = to_chips(pay)
    pay, mom, grads = lax.optimization_barrier((pay, mom, grads))
    (note,) = call(note_kernel, [((8, 128), F32)], [pay.reshape(D, 1152)])
    note_other, grads_other = swap(note), swap(grads)
    (mom,) = call(near_kernel, [((D, 1024), BF)], [mom], scratch=[pltpu.SemaphoreType.DMA], far=(0,))
    note_other, grads_other, mom = lax.optimization_barrier((note_other, grads_other, mom))
    matrix, gram, clip_norm, factors = call(
        gram_kernel,
        [((2, D, D), BF), ((TALL, HALF), F32), ((1, 1), F32), ((8, 128), F32)],
        [role, pay.reshape(D, 1152), mom, note, note_other],
        smem=(0,),
        results=(2,),
        flops=2 * 2 * D * D * D,
    )
    gram_other = swap(gram)
    *moms, vec_mom, vec_sec, vec_new, vec_copy = call(
        momenta_kernel,
        [((4, 4, D), F32), ((4, FF), F32), ((16, D), F32)] + [((4, 12), F32)] * 3 + [((4, 12), BF)],
        [
            core, grads, grads_other, factors, vec_master.T, attn_moment, up_moment, down_moment,
            vec_moment.T, vec_second.T,
        ],
        scratch=[pltpu.VMEM((8, FF), F32), pltpu.VMEM((16, D), F32)],
        smem=(0,),
        args=range(4, 10),
        results=range(7),
    )
    gram_other, *moms = lax.optimization_barrier((gram_other, *moms))
    vecs = [t.T for t in (vec_mom, vec_sec, vec_new, vec_copy)]
    (orth,) = call(
        newton_kernel,
        [((4, 2, 8, 1024), BF)],
        [role, plane, matrix, gram, gram_other],
        scratch=[pltpu.VMEM((D, D), F32), pltpu.VMEM((64, D), F32)],
        smem=(0, 1),
        flops=14 * 3 * 2 * D * D * D,
    )
    orth = orth.reshape(8, 8, 1024)
    orth = lax.all_to_all(orth, ("y", "c"), 0, 0, tiled=True)
    news = call(
        update_kernel,
        [((4, 4, D), F32), ((4, FF), F32), ((16, D), F32), ((4, 4, D), BF), ((4, FF), BF), ((16, D), BF)],
        [core, orth, attn_master, up_master, down_master],
        scratch=[pltpu.VMEM((8, FF), F32), pltpu.VMEM((16, D), F32)],
        smem=(0,),
        args=range(2, 5),
        results=range(6),
    )
    return (layer_out, input_grad, clip_norm[0, 0], *moms, *news, *vecs)


def solution(mesh):
    grid = Mesh(mesh.devices.reshape(4, 4, 4, 2), ("x", "z", "y", "c"))
    row, mat, vec = P(ALL, None), P(None, ALL, None), P(None, ALL)
    return jax.shard_map(
        body,
        mesh=grid,
        in_specs=(row, row, row, mat, row, row, vec, mat, row, row, vec, vec),
        out_specs=(row, row, P(), mat, row, row, mat, row, row, mat, row, row, vec, vec, vec, vec),
        check_vma=False,
    )
```

```python
import math

import jax
import jax.numpy as jnp
from jax import lax
from jax.experimental import pallas as pl
from jax.experimental.pallas import tpu as pltpu
from jax.sharding import Mesh, PartitionSpec as P

D = 512
FF = 2048
H = 8
HD = 64
ROW = 128
STEP = 10
NS_ITERS = 5
HALF = 256

MASKED_SCORE = -1e30
NORM_EPSILON = 1e-05
CLIP_LIMIT = 1.0
MOMENTUM_DECAY = 0.95
RATE_MATRIX = 0.5
DECAY_MATRIX = 0.01
BETA_FIRST = 0.9
BETA_SECOND = 0.999
RATE_VECTOR = 0.2
ADAM_EPSILON = 1e-08
NEWTON_FIRST = 3.4445
NEWTON_SECOND = -4.775
NEWTON_THIRD = 2.0315

CHIPS = ("x", "z", "y")
ALL = ("x", "z", "y", "c")
BF = jnp.bfloat16
F32 = jnp.float32
VMEM_LIMIT = 12 * 1024 * 1024


def call(kernel, outs, ins, scratch=(), smem=(), args=(), far=(), results=(), away=(), flops=0, limit=VMEM_LIMIT):
    spec = [
        pl.BlockSpec(memory_space=pltpu.SMEM if i in smem else pl.ANY if i in far else pltpu.VMEM)
        for i in range(len(ins))
    ]
    placed = [
        x if i in smem or i in args
        else pltpu.with_memory_space_constraint(x, pltpu.HBM if i in far else pltpu.VMEM)
        for i, x in enumerate(ins)
    ]
    shapes = [
        jax.ShapeDtypeStruct(s, t) if i in results else pltpu.HBM(s, t) if i in away else pltpu.VMEM(s, t)
        for i, (s, t) in enumerate(outs)
    ]
    moved = sum(math.prod(a.shape) * a.dtype.itemsize for a in ins)
    return pl.pallas_call(
        kernel,
        out_shape=shapes,
        in_specs=spec,
        out_specs=[
            pl.BlockSpec(memory_space=pl.ANY if i in away else pltpu.VMEM) for i in range(len(shapes))
        ],
        scratch_shapes=list(scratch),
        compiler_params=pltpu.CompilerParams(vmem_limit_bytes=limit),
        cost_estimate=pl.CostEstimate(flops=flops, bytes_accessed=moved, transcendentals=0),
    )(*placed)


def dot(a, b):
    return jnp.dot(a, b, preferred_element_type=F32)


def dot_t(a, b):
    return lax.dot_general(a, b, (((1,), (1,)), ((), ())), preferred_element_type=F32)


def dot_in(a, b):
    return lax.dot_general(a, b, (((0,), (0,)), ((), ())), preferred_element_type=F32)


O_LANE, UP_LANE, DOWN_LANE, VEC_LANE, BLOCK = 768, 1024, 2048, 3072, 3200
X0, A0, H0, Z0, ACTS = 0, 512, 1024, 1536, 3328
Y0, DU0, DF0, GRADS = 0, 1024, 2048, 2560


def half_lanes(half, size):
    return pl.ds(pl.multiple_of(half * size, size), size)


def regroup():
    source = lax.broadcasted_iota(jnp.int32, (D, D), 0)
    target = lax.broadcasted_iota(jnp.int32, (D, D), 1)
    return jnp.where(target == (source & 3) * 128 + (source >> 2), 1.0, 0.0).astype(BF)


def pack_kernel(
    core, attn, up, down, vec, attn_m, up_m, down_m, keep, send,
    attn_v, up_v, down_v, vec_v, attn_mv, up_mv, down_mv, full, block, stage, sems,
):
    c = core[0]
    copies = [
        pltpu.make_async_copy(source, target, sems.at[i])
        for i, (source, target) in enumerate(
            [(attn, attn_v), (up, up_v), (down, down_v), (vec, vec_v), (attn_m, attn_mv), (up_m, up_mv), (down_m, down_mv)]
        )
    ]
    for copy in copies:
        copy.start()
    move = regroup()
    for copy in copies:
        copy.wait()
    for first, attn_one, up_one, down_one in ((0, attn_v, up_v, down_v), (4, attn_mv, up_mv, down_mv)):
        rows = slice(first, first + 4)
        for m in range(4):
            full[rows, D * m : D * (m + 1)] = attn_one[m]
        for part in range(4):
            row = 8 * part + first
            stage[row : row + 4, :] = up_one[:, D * part : D * (part + 1)]
        for i in range(4):
            for q in range(4):
                lane = 2 * FF + D * q
                full[first + i : first + i + 1, lane : lane + D] = down_one[4 * i + q : 4 * i + q + 1, :]
    moved = dot(stage[...].astype(BF), move)
    for part in range(4):
        for q in range(4):
            lane = FF + D * q + 128 * part
            full[:, lane : lane + 128] = moved[8 * part : 8 * (part + 1), 128 * q : 128 * (q + 1)]
    for target, half in ((keep, c), (send, 1 - c)):
        for m in range(4):
            lanes = pl.ds(pl.multiple_of(D * m + HALF * half, HALF), HALF)
            block[0:4, HALF * m : HALF * (m + 1)] = full[0:4, lanes]
        for m in range(2):
            lanes = pl.ds(pl.multiple_of(2 * D * m + D * half, D), D)
            block[4:8, D * m : D * (m + 1)] = full[4:8, lanes]
        block[:, UP_LANE:DOWN_LANE] = full[:, pl.ds(pl.multiple_of(FF + 1024 * half, 1024), 1024)]
        for q in range(4):
            lanes = pl.ds(pl.multiple_of(2 * FF + D * q + HALF * half, HALF), HALF)
            lane = DOWN_LANE + HALF * q
            block[0:4, lane : lane + HALF] = full[0:4, lanes]
        lanes = pl.ds(pl.multiple_of(2 * FF + 1024 * half, 1024), 1024)
        block[4:8, DOWN_LANE:VEC_LANE] = full[4:8, lanes]
        block[:, VEC_LANE:BLOCK] = jnp.zeros((8, 128), F32)
        block[0:4, VEC_LANE : VEC_LANE + 12] = vec_v[...]
        target[...] = block[...].astype(BF)


def role_lanes(block, note):
    gap = jnp.zeros((8, 512), block.dtype)
    tail = [] if note is None else [note]
    return [
        jnp.concatenate([block[:, 0:512], gap] + tail, axis=1),
        jnp.concatenate([block[:, 512:1024], gap] + tail, axis=1),
        jnp.concatenate([block[:, UP_LANE:DOWN_LANE]] + tail, axis=1),
        jnp.concatenate([block[:, DOWN_LANE:VEC_LANE]] + tail, axis=1),
    ]


def spread_kernel(core, keep, got, message, message_mom):
    mine, other = keep[...].astype(F32), got[...].astype(F32)
    is_left = core[0] == 0
    left, right = jnp.where(is_left, mine, other), jnp.where(is_left, other, mine)
    block = jnp.concatenate([left[0:4], right[0:4]], axis=0).astype(BF)
    moms = role_lanes(jnp.concatenate([left[4:8], right[4:8]], axis=0).astype(BF), None)
    for i in range(64):
        message[i] = block
        message_mom[i] = moms[i % 4]


def by_head(pair):
    low = (lax.broadcasted_iota(jnp.int32, (ROW, ROW), 1) < HD).astype(F32)
    return jnp.concatenate([pair * low.astype(BF), pair * (1.0 - low).astype(BF)], axis=0)


def abreast(stacked):
    return jnp.concatenate([stacked[0:ROW], stacked[ROW:]], axis=1)


def norm_parts(values):
    centred = values - jnp.mean(values, axis=-1, keepdims=True)
    scale = lax.rsqrt(jnp.mean(centred * centred, axis=-1, keepdims=True) + NORM_EPSILON)
    return centred * scale, scale


def norm_back(grad, gain, normed, scale):
    grad = grad * gain
    return scale * (
        grad
        - jnp.mean(grad, axis=-1, keepdims=True)
        - normed * jnp.mean(grad * normed, axis=-1, keepdims=True)
    )


def forward_kernel(
    core, x, w_own, w_far, seg, q_out, k_out, v_out, p_out, vec_out, keep, send, first_out, norm_out, scale_out,
    slope, w_other, wide, pair_scr, acts, sems,
):
    c = core[0]
    copies = []
    for i in range(3):
        lanes = pl.ds(1024 * i, 1024)
        copies.append(pltpu.make_async_copy(w_far.at[:, lanes], w_other.at[:, lanes], sems.at[i]))
        copies[i].start()
    sides = ((c, w_own), (1 - c, w_other))
    vec = w_own[:, VEC_LANE:BLOCK].astype(F32).T[:16]
    vec_out[...] = vec
    moved = dot(vec[8:16].astype(BF), regroup())
    for part in range(4):
        for q in range(4):
            vec_out[8 + q : 9 + q, 128 * part : 128 * (part + 1)] = moved[part : part + 1, 128 * q : 128 * (q + 1)]
    tokens = x[...]
    pair_scr[0] = tokens
    names = jnp.broadcast_to(seg[...].astype(F32), (ROW, ROW))
    gap = names - names.T
    same = jnp.concatenate([gap, gap], axis=0) == 0.0
    for half, w in sides:
        if w is w_other:
            copies[0].wait()
        product = dot(tokens, w[:, 0:O_LANE])
        q = (product[:, 0:HALF] + vec_out[0:1, half_lanes(half, HALF)]).astype(BF)
        k = product[:, HALF : 2 * HALF].astype(BF)
        v = (product[:, 2 * HALF : O_LANE] + vec_out[1:2, half_lanes(half, HALF)]).astype(BF)
        for target, value in ((q_out, q), (k_out, k), (v_out, v)):
            target[:, half_lanes(half, HALF)] = value
        for pair in range(2):
            cols = slice(128 * pair, 128 * pair + 128)
            scores = dot_t(by_head(q[:, cols]), k[:, cols]) * (HD ** (-0.5))
            scores = jnp.where(same, scores, MASKED_SCORE)
            expo = jnp.exp(scores - jnp.max(scores, axis=-1, keepdims=True))
            soft = expo / jnp.sum(expo, axis=-1, keepdims=True)
            p_out[2 * half + pair] = soft
            attended = dot(abreast(soft.astype(BF)), by_head(v[:, cols]))
            lanes = pl.ds(pl.multiple_of(HALF * half + 128 * pair, 128), 128)
            pair_scr[1, :, lanes] = attended.astype(BF)
    for half, w in sides:
        wide[:, half_lanes(half, HALF)] = dot(pair_scr[1], w[:, O_LANE:UP_LANE])
    normed, scale = norm_parts(tokens.astype(F32) + wide[...] + vec[2:3])
    norm_out[...] = normed
    scale_out[...] = scale
    first = normed * vec[4:5] + vec[5:6]
    first_out[...] = first
    first_low = first.astype(BF)
    root = math.sqrt(2.0 / math.pi)
    copies[1].wait()
    for half, w in sides:
        for k in range(2):
            bias = vec_out[pl.ds(8 + 2 * half + k, 1), :]
            u = dot(first_low, w[:, UP_LANE + D * k : UP_LANE + D * (k + 1)]) + bias
            square = u * u
            tanh = jnp.tanh(root * (u + 0.044715 * (square * u)))
            gate = 0.5 * (1.0 + tanh)
            cols = pl.ds(pl.multiple_of(1024 * half + D * k, D), D)
            slope[:, cols] = gate + 0.5 * u * (1.0 - tanh * tanh) * (root * (1.0 + 3 * 0.044715 * square))
            acts[:, cols] = (u * gate).astype(BF)
    for target, half in ((keep, c), (send, 1 - c)):
        target[:, X0:A0] = tokens
        target[:, A0:H0] = pair_scr[half]
        target[:, H0:Z0] = first_low
        target[:, Z0 : Z0 + 1024] = acts[:, half_lanes(half, 1024)]
        target[:, Z0 + 1024 : ACTS] = jnp.zeros((ROW, ACTS - Z0 - 1024), BF)
    copies[2].wait()


def backward_kernel(
    core, x, acts_own, acts_sent, first, vec_in, w_own, w_other, cot, slope, normed_in, scale_in, q_in, k_in, v_in, p_in,
    out, base, y_scr, keep, send, vg, wide, du_scr, df_scr, do_scr,
):
    c = core[0]
    sides = ((c, w_own), (1 - c, w_other))
    vec = vec_in[...]
    dq_scr, dk_scr, dv_scr, da_scr = (y_scr.at[i] for i in range(4))
    for half, w in sides:
        feed = jnp.zeros((ROW, HALF), F32)
        for group, acts in ((c, acts_own), (1 - c, acts_sent)):
            for k in range(2):
                lanes = pl.ds(pl.multiple_of(DOWN_LANE + 2 * HALF * group + HALF * k, HALF), HALF)
                feed = feed + dot(acts[:, Z0 + D * k : Z0 + D * (k + 1)], w[:, lanes])
        wide[:, half_lanes(half, HALF)] = feed
    residual = wide[...] + vec[3:4] + first[...] + x[...].astype(F32)
    normed, scale = norm_parts(residual)
    out[...] = (normed * vec[6:7] + vec[7:8]).astype(BF)
    grad = cot[...].astype(F32)
    vg[...] = jnp.zeros((16, D), F32)
    vg[6:7, :] = jnp.sum(grad * normed, axis=0, keepdims=True)
    vg[7:8, :] = jnp.sum(grad, axis=0, keepdims=True)
    grad2 = norm_back(grad, vec[6:7], normed, scale)
    df_scr[...] = grad2.astype(BF)
    vg[3:4, :] = jnp.sum(df_scr[...].astype(F32), axis=0, keepdims=True)
    for q in range(4):
        lane = DOWN_LANE + HALF * q
        dz = dot_t(df_scr[:, half_lanes(c, HALF)], w_own[:, lane : lane + HALF])
        dz = dz + dot_t(df_scr[:, half_lanes(1 - c, HALF)], w_other[:, lane : lane + HALF])
        du = (dz * slope[:, D * q : D * (q + 1)]).astype(BF)
        du_scr[:, D * q : D * (q + 1)] = du
        vg[8 + q : 9 + q, :] = jnp.sum(du.astype(F32), axis=0, keepdims=True)
    dfirst = grad2
    for half, w in sides:
        dfirst = dfirst + dot_t(du_scr[:, half_lanes(half, 1024)], w[:, UP_LANE:DOWN_LANE])
    normed1 = normed_in[...]
    vg[4:5, :] = jnp.sum(dfirst * normed1, axis=0, keepdims=True)
    vg[5:6, :] = jnp.sum(dfirst, axis=0, keepdims=True)
    dres = norm_back(dfirst, vec[4:5], normed1, scale_in[...])
    da_scr[...] = dres.astype(BF)
    vg[2:3, :] = jnp.sum(da_scr[...].astype(F32), axis=0, keepdims=True)
    dattended = jnp.zeros((ROW, D), F32)
    for half, w in sides:
        dattended = dattended + dot_t(da_scr[:, half_lanes(half, HALF)], w[:, O_LANE:UP_LANE])
    do_scr[...] = dattended.astype(BF)
    share = HD ** (-0.5)
    pairs = [slice(128 * pair, 128 * pair + 128) for pair in range(H // 2)]
    dos = [by_head(do_scr[:, cols]) for cols in pairs]
    dsofts = [dot_t(do, v_in[:, cols]) for do, cols in zip(dos, pairs)]
    dss = []
    for pair, dsoft in enumerate(dsofts):
        soft = p_in[pair]
        dss.append((soft * (dsoft - jnp.sum(soft * dsoft, axis=-1, keepdims=True))).astype(BF))
    for pair, cols in enumerate(pairs):
        ds = dss[pair]
        dq_scr[:, cols] = (dot(abreast(ds), by_head(k_in[:, cols])) * share).astype(BF)
        dk_scr[:, cols] = (dot_in(ds, by_head(q_in[:, cols])) * share).astype(BF)
        dv_scr[:, cols] = dot_in(p_in[pair].astype(BF), dos[pair]).astype(BF)
    vg[0:1, :] = jnp.sum(dq_scr[...].astype(F32), axis=0, keepdims=True)
    vg[1:2, :] = jnp.sum(dv_scr[...].astype(F32), axis=0, keepdims=True)
    for target, half in ((keep, c), (send, 1 - c)):
        target[:, 0:D] = y_scr[half]
        target[:, D : 2 * D] = y_scr[2 + half]
        target[:, DU0:DF0] = du_scr[:, half_lanes(half, 1024)]
        target[:, DF0:GRADS] = df_scr[...]
    base[...] = grad2 + dres


def input_kernel(core, base, grads, w_own, w_other, out):
    total = base[...]
    for half, w in ((core[0], w_own), (1 - core[0], w_other)):
        for i in range(3):
            total = total + dot_t(grads[i, :, half_lanes(half, HALF)], w[:, HALF * i : HALF * (i + 1)])
    out[...] = total.astype(BF)


def weights_kernel(acts, acts_other, keep, got, vg, vg_other, out, vec):
    def both(one, two, first, last):
        return jnp.concatenate([one[:, first:last], two[:, first:last]], axis=0)

    out[:, UP_LANE:DOWN_LANE] = dot_in(both(acts, acts_other, H0, Z0), both(keep, got, DU0, DF0)).astype(BF)
    down = both(keep, got, DF0, GRADS)
    for k in range(2):
        lane = DOWN_LANE + D * k
        units = both(acts, acts_other, Z0 + D * k, Z0 + D * (k + 1))
        out[:, lane : lane + D] = dot_in(units, down).astype(BF)
    for k in range(2):
        left = both(acts, acts_other, D * k, D * (k + 1))
        out[:, D * k : D * (k + 1)] = dot_in(left, both(keep, got, D * k, D * (k + 1))).astype(BF)
    total = vg[...] + vg_other[...]
    vec[...] = jnp.zeros((128, D), F32)
    vec[0:8, :] = total[0:8]
    for part in range(4):
        for q in range(4):
            vec[8 + part : 9 + part, 128 * q : 128 * (q + 1)] = total[8 + q : 9 + q, 128 * part : 128 * (part + 1)]
    vec[8:16, :] = dot_t(vec[8:16, :].astype(BF), regroup())
    out[:, VEC_LANE:BLOCK] = vec[...].T.astype(BF)


def add_up(ref):
    total = ref[0].astype(F32)
    for i in range(1, 64):
        total = total + ref[i].astype(F32)
    return total


def split3(value):
    one = value.astype(BF)
    rest = value - one.astype(F32)
    two = rest.astype(BF)
    three = (rest - two.astype(F32)).astype(BF)
    return one, two, three


def reduce_kernel(got, grads, pay):
    grads[...] = add_up(got)
    own, vec = grads[:, 0:VEC_LANE], grads[:, VEC_LANE:BLOCK]
    square = jnp.sum(own * own) + 0.5 * jnp.sum(vec * vec)
    row = lax.broadcasted_iota(jnp.int32, (8, 128), 0)
    lane = lax.broadcasted_iota(jnp.int32, (8, 128), 1)
    full = jnp.full((8, 128), square, F32)
    one, two, three = split3(full)
    note = jnp.where(lane == 0, one.astype(F32), jnp.where(lane == 1, two.astype(F32), three.astype(F32)))
    note = jnp.where((row == 0) & (lane < 3), note, 0.0).astype(BF)
    rows = role_lanes(grads[:, 0:VEC_LANE].astype(BF), note)
    for i in range(64):
        pay[i] = rows[i % 4]


def halves(value):
    high = value.astype(BF)
    return high, (value - high.astype(F32)).astype(BF)


def fine(a, b):
    ah, al = a
    bh, bl = b
    return dot(jnp.concatenate([ah, ah, al], axis=1), jnp.concatenate([bh, bl, bh], axis=0))


TALL = 3 * HALF + 8


def near_kernel(far, near, sem):
    copy = pltpu.make_async_copy(far, near, sem)
    copy.start()
    copy.wait()


def note_kernel(got, note):
    note[...] = jnp.full((8, 128), jnp.sum(got[:, 1024:1152].astype(F32)), F32)


def gram_kernel(role_ref, got, mom, note, note_other, matrix, gram, clip_out, factor_out):
    role = role_ref[0]
    clip = jnp.sqrt(note[...] + note_other[...])
    factors = CLIP_LIMIT / jnp.maximum(clip, CLIP_LIMIT)
    clip_out[...] = clip[0:1, 0:1]
    factor_out[...] = factors
    factor = factors[0:1, 0:1]

    def make(k):
        cols = slice(D * k, D * (k + 1))
        value = MOMENTUM_DECAY * mom[:, cols].astype(F32) + factor * got[:, cols].astype(F32)
        value = value.astype(BF)
        matrix[k] = value
        value = value.astype(F32)
        return jnp.sum(value * value)

    def finish(product, parts, square):
        for i, (a, b) in enumerate(((0, 0), (0, 1), (1, 1))):
            total = product(a, b, 0)
            for k in range(1, parts):
                total = total + product(a, b, k)
            gram[HALF * i : HALF * (i + 1), :] = total
        gram[3 * HALF : TALL, :] = jnp.full((8, HALF), square, F32)

    def inner(a, b, k):
        return dot_in(matrix[k, :, HALF * a : HALF * (a + 1)], matrix[k, :, HALF * b : HALF * (b + 1)])

    def outer(a, b, k):
        return dot_t(matrix[k, HALF * a : HALF * (a + 1), :], matrix[k, HALF * b : HALF * (b + 1), :])

    @pl.when(role < 2)
    def _():
        square = make(0)
        finish(inner, 1, square)

    @pl.when(role == 2)
    def _():
        square = make(0) + make(1)
        finish(outer, 2, square)

    @pl.when(role == 3)
    def _():
        square = make(0) + make(1)
        finish(inner, 2, square)


def thin(rows, matrix):
    high, low = halves(rows)
    both = dot(jnp.concatenate([high, low], axis=0), matrix[0])
    return both[0 : rows.shape[0]] + (both[rows.shape[0] :] + dot(high, matrix[1]))


def newton_kernel(role_ref, plane_ref, matrix, gram_own, gram_other, out, gram, rows_scr):
    role, plane = role_ref[0], plane_ref[0]
    chips = pl.ds(pl.multiple_of(plane * 32, 32), 32)

    def scaled(total):
        size = jnp.sqrt(total[3 * HALF : 3 * HALF + 1, 0:1]) + 1e-07
        inverse = 1.0 / size
        total = total[0 : 3 * HALF] * (inverse * inverse)
        gram[0:HALF, 0:HALF] = total[0:HALF]
        gram[0:HALF, HALF:D] = total[HALF:D]
        gram[HALF:D, 0:HALF] = total[HALF:D].T
        gram[HALF:D, HALF:D] = total[D : 3 * HALF]
        return inverse

    def rows_of(k):
        return matrix[k, chips, :].astype(F32)

    @pl.when(role < 2)
    def _():
        inverse = scaled(gram_own[...])
        rows_scr[0:32, :] = rows_of(0) * inverse
        rows_scr[32:64, :] = jnp.zeros((32, D), F32)

    @pl.when(role == 2)
    def _():
        inverse = scaled(gram_own[...] + gram_other[...])
        here = lax.broadcasted_iota(jnp.int32, (32, D), 0) + 32 * plane
        there = lax.broadcasted_iota(jnp.int32, (32, D), 1)
        rows_scr[0:32, :] = jnp.where(here == there, 1.0, 0.0) * inverse
        rows_scr[32:64, :] = jnp.zeros((32, D), F32)

    @pl.when(role == 3)
    def _():
        inverse = scaled(gram_own[...] + gram_other[...])
        for k in range(2):
            rows_scr[32 * k : 32 * (k + 1), :] = rows_of(k) * inverse

    diagonal = (
        lax.broadcasted_iota(jnp.int32, (D, D), 0) == lax.broadcasted_iota(jnp.int32, (D, D), 1)
    )

    def polynomial(square):
        poly = NEWTON_SECOND * gram[...] + NEWTON_THIRD * square
        return jnp.where(diagonal, poly + NEWTON_FIRST, poly)

    def turn(_):
        own = halves(gram[...])
        poly = halves(polynomial(dot(own[0], own[0])))
        pairs = zip(halves(fine(poly, own)), halves(rows_scr[...]))
        both = fine(tuple(jnp.concatenate(pair, axis=0) for pair in pairs), poly)
        gram[...] = both[0:D]
        rows_scr[...] = both[D:]

    pl.loop(0, NS_ITERS - 2)(turn)
    own = halves(gram[...])
    poly = halves(polynomial(fine(own, own)))
    rows = thin(rows_scr[...], poly)

    def through(value):
        return thin(thin(thin(value, poly), poly), own)

    once = through(rows)
    twice = through(once)
    rows_scr[...] = NEWTON_FIRST * rows + NEWTON_SECOND * once + NEWTON_THIRD * twice

    def send(k, value):
        value = value.reshape(4, 8, D)
        for half in range(2):
            out[:, half, :, D * k : D * (k + 1)] = value[:, 4 * half : 4 * (half + 1)].astype(BF)

    @pl.when(role == 2)
    def _():
        high, low = halves(rows_scr[0:32, :])
        for k in range(2):
            send(k, dot(high, matrix[k]) + dot(low, matrix[k]))

    @pl.when(role != 2)
    def _():
        for k in range(2):
            send(k, rows_scr[32 * k : 32 * (k + 1), :])


def rows4(is_left, value):
    return jnp.where(is_left, value[0:4], value[4:8])


def natural(ups):
    parts = [
        jnp.concatenate([ups[:, D * q + 128 * part : D * q + 128 * (part + 1)] for q in range(4)], axis=1)
        for part in range(4)
    ]
    return dot_t(jnp.concatenate(parts, axis=0).astype(BF), regroup())


def momenta_kernel(
    core, grads, grads_other, factors, vec, attn_m, up_m, down_m, vec_m, vec_s,
    attn_mom, up_mom, down_mom, vec_mom, vec_sec, vec_new, vec_copy, ups, downs,
):
    is_left = core[0] == 0
    factor = factors[0:1, 0:1]

    def both(first, last):
        mine, other = grads[:, first:last], grads_other[:, first:last]
        left = jnp.where(is_left, mine, other)
        right = jnp.where(is_left, other, mine)
        return rows4(is_left, left), rows4(is_left, right)

    pairs = [both(D * k, D * (k + 1)) for k in range(2)]
    for m in range(4):
        attn_mom[m] = MOMENTUM_DECAY * attn_m[m] + factor * pairs[m // 2][m % 2]
    high, low = halves(jnp.concatenate(both(UP_LANE, DOWN_LANE), axis=1))
    ups[0:4, :] = high.astype(F32)
    ups[4:8, :] = low.astype(F32)
    moved = natural(ups)
    for part in range(4):
        cols = slice(D * part, D * (part + 1))
        grad = moved[8 * part : 8 * part + 4] + moved[8 * part + 4 : 8 * part + 8]
        up_mom[:, cols] = MOMENTUM_DECAY * up_m[:, cols] + factor * grad
    sides = both(DOWN_LANE, VEC_LANE)
    for q in range(4):
        grad = sides[q // 2][:, D * (q % 2) : D * (q % 2 + 1)]
        for i in range(4):
            downs[4 * i + q : 4 * i + q + 1, :] = grad[i : i + 1]
    down_mom[...] = MOMENTUM_DECAY * down_m[...] + factor * downs[...]
    clipped = factor * rows4(is_left, grads[:, VEC_LANE:BLOCK])[:, 0:12]
    first = BETA_FIRST * vec_m[...] + (1.0 - BETA_FIRST) * clipped
    second = BETA_SECOND * vec_s[...] + (1.0 - BETA_SECOND) * clipped * clipped
    vec_mom[...] = first
    vec_sec[...] = second
    first_hat = first / (1.0 - BETA_FIRST**STEP)
    second_hat = second / (1.0 - BETA_SECOND**STEP)
    new = vec[...] - RATE_VECTOR * first_hat / (jnp.sqrt(second_hat) + ADAM_EPSILON)
    vec_new[...] = new
    vec_copy[...] = new.astype(BF)


def update_kernel(
    got, attn, up, down, attn_new, up_new, down_new, attn_copy, up_copy, down_copy, ups, downs
):
    keep_share = 1.0 - RATE_MATRIX * DECAY_MATRIX
    for m in range(4):
        new = attn[m] * keep_share - RATE_MATRIX * got[m, :, 0:512].astype(F32)
        attn_new[m] = new
        attn_copy[m] = new.astype(BF)
    ups[0:4, :] = jnp.concatenate([got[4].astype(F32), got[5].astype(F32)], axis=1)
    ups[4:8, :] = jnp.zeros((4, FF), F32)
    rate = RATE_MATRIX * math.sqrt(max(1.0, FF / D))
    moved = natural(ups)
    for part in range(4):
        cols = slice(D * part, D * (part + 1))
        up_new[:, cols] = up[:, cols] * keep_share - rate * moved[8 * part : 8 * part + 4]
    up_copy[...] = up_new[...].astype(BF)
    rate = RATE_MATRIX * math.sqrt(max(1.0, D / FF))
    for q in range(4):
        step = got[6 + q // 2, :, D * (q % 2) : D * (q % 2 + 1)].astype(F32)
        for i in range(4):
            downs[4 * i + q : 4 * i + q + 1, :] = step[i : i + 1]
    down_new[...] = down[...] * keep_share - rate * downs[...]
    down_copy[...] = down_new[...].astype(BF)


def swap(value):
    return lax.ppermute(value, "c", [(0, 1), (1, 0)])


def to_chips(value):
    return lax.all_to_all(value, CHIPS, 0, 0, tiled=True)


def body(
    block_input, cotangent, segment_ids, attn_master, up_master, down_master, vec_master,
    attn_moment, up_moment, down_moment, vec_moment, vec_second,
):
    c = lax.axis_index("c")
    core = c.reshape(1).astype(jnp.int32)
    role = lax.axis_index("y").reshape(1).astype(jnp.int32)
    plane = (lax.axis_index("x") * 4 + lax.axis_index("z")).reshape(1).astype(jnp.int32)
    core, role, plane = lax.optimization_barrier((core, role, plane))

    keep, send = call(
        pack_kernel,
        [((8, BLOCK), BF)] * 2,
        [core, attn_master, up_master, down_master, vec_master.T, attn_moment, up_moment, down_moment],
        scratch=[
            pltpu.VMEM((4, 4, D), F32), pltpu.VMEM((4, FF), F32), pltpu.VMEM((16, D), F32), pltpu.VMEM((4, 12), F32),
            pltpu.VMEM((4, 4, D), F32), pltpu.VMEM((4, FF), F32), pltpu.VMEM((16, D), F32),
            pltpu.VMEM((8, 3 * FF), F32), pltpu.VMEM((8, BLOCK), F32), pltpu.VMEM((32, D), F32),
            pltpu.SemaphoreType.DMA((7,)),
        ],
        smem=(0,),
        far=range(1, 8),
    )
    message, message_mom = call(
        spread_kernel, [((64, 8, BLOCK), BF), ((64, 8, 1024), BF)], [core, keep, swap(send)], smem=(0,)
    )
    own = to_chips(message)
    own, message_mom = lax.optimization_barrier((own, message_mom))
    other = swap(own)
    mom = to_chips(message_mom).reshape(D, 1024)
    own, other = own.reshape(D, BLOCK), other.reshape(D, BLOCK)
    q, k, v, soft, vec, acts_own, acts_sent, first, normed, scale, slope, other = call(
        forward_kernel,
        [((ROW, D), BF)] * 3
        + [((H // 2, 2 * ROW, ROW), F32), ((16, D), F32), ((ROW, ACTS), BF), ((ROW, ACTS), BF)]
        + [((ROW, D), F32), ((ROW, D), F32), ((ROW, 1), F32), ((ROW, FF), F32), ((D, 3072), BF)],
        [core, block_input, own, other, segment_ids],
        scratch=[
            pltpu.VMEM((ROW, D), F32), pltpu.VMEM((2, ROW, D), BF), pltpu.VMEM((ROW, FF), BF),
            pltpu.SemaphoreType.DMA((3,)),
        ],
        smem=(0,),
        args=(1, 4),
        far=(3,),
        flops=8 * 2 * ROW * D * D,
    )
    acts_other = swap(acts_sent)
    layer_out, base, ygrads, keep, send, vg = call(
        backward_kernel,
        [((ROW, D), BF), ((ROW, D), F32), ((4, ROW, D), BF), ((ROW, GRADS), BF), ((ROW, GRADS), BF), ((16, D), F32)],
        [
            core, block_input, acts_own, acts_sent, first, vec, own, other, cotangent, slope, normed, scale,
            q, k, v, soft,
        ],
        scratch=[
            pltpu.VMEM((ROW, D), F32), pltpu.VMEM((ROW, FF), BF), pltpu.VMEM((ROW, D), BF), pltpu.VMEM((ROW, D), BF),
        ],
        smem=(0,),
        args=(1, 8),
        results=(0,),
        flops=18 * 2 * ROW * D * D,
    )
    got, vg_other = swap(send), swap(vg)
    (input_grad,) = call(
        input_kernel,
        [((ROW, D), BF)],
        [core, base, ygrads, own, other],
        smem=(0,),
        results=(0,),
        flops=3 * 2 * ROW * D * D,
    )
    got, input_grad = lax.optimization_barrier((got, input_grad))
    (weights,) = call(
        weights_kernel,
        [((D, BLOCK), BF)],
        [acts_own, acts_other, keep, got, vg, vg_other],
        scratch=[pltpu.VMEM((128, D), F32)],
        flops=2 * 256 * 512 * 3072,
    )
    weights, mom = lax.optimization_barrier((weights, mom))
    weights = to_chips(weights.reshape(64, 8, BLOCK))
    grads, pay = call(reduce_kernel, [((8, BLOCK), F32), ((64, 8, 1152), BF)], [weights])
    pay = to_chips(pay)
    pay, mom, grads = lax.optimization_barrier((pay, mom, grads))
    (note,) = call(note_kernel, [((8, 128), F32)], [pay.reshape(D, 1152)])
    note_other, grads_other = swap(note), swap(grads)
    (mom,) = call(near_kernel, [((D, 1024), BF)], [mom], scratch=[pltpu.SemaphoreType.DMA], far=(0,))
    note_other, grads_other, mom = lax.optimization_barrier((note_other, grads_other, mom))
    matrix, gram, clip_norm, factors = call(
        gram_kernel,
        [((2, D, D), BF), ((TALL, HALF), F32), ((1, 1), F32), ((8, 128), F32)],
        [role, pay.reshape(D, 1152), mom, note, note_other],
        smem=(0,),
        results=(2,),
        flops=2 * 2 * D * D * D,
    )
    gram_other = swap(gram)
    *moms, vec_mom, vec_sec, vec_new, vec_copy = call(
        momenta_kernel,
        [((4, 4, D), F32), ((4, FF), F32), ((16, D), F32)] + [((4, 12), F32)] * 3 + [((4, 12), BF)],
        [
            core, grads, grads_other, factors, vec_master.T, attn_moment, up_moment, down_moment,
            vec_moment.T, vec_second.T,
        ],
        scratch=[pltpu.VMEM((8, FF), F32), pltpu.VMEM((16, D), F32)],
        smem=(0,),
        args=range(4, 10),
        results=range(7),
    )
    gram_other, *moms = lax.optimization_barrier((gram_other, *moms))
    vecs = [t.T for t in (vec_mom, vec_sec, vec_new, vec_copy)]
    (orth,) = call(
        newton_kernel,
        [((4, 2, 4, 1024), BF)],
        [role, plane, matrix, gram, gram_other],
        scratch=[pltpu.VMEM((D, D), F32), pltpu.VMEM((64, D), F32)],
        smem=(0, 1),
        flops=14 * 3 * 2 * D * D * D,
    )
    orth = orth.reshape(8, 4, 1024)
    orth = lax.all_to_all(orth, ("y", "c"), 0, 0, tiled=True)
    news = call(
        update_kernel,
        [((4, 4, D), F32), ((4, FF), F32), ((16, D), F32), ((4, 4, D), BF), ((4, FF), BF), ((16, D), BF)],
        [orth, attn_master, up_master, down_master],
        scratch=[pltpu.VMEM((8, FF), F32), pltpu.VMEM((16, D), F32)],
        args=range(1, 4),
        results=range(6),
    )
    return (layer_out, input_grad, clip_norm[0, 0], *moms, *news, *vecs)


def solution(mesh):
    grid = Mesh(mesh.devices.reshape(4, 4, 4, 2), ("x", "z", "y", "c"))
    row, mat, vec = P(ALL, None), P(None, ALL, None), P(None, ALL)
    return jax.shard_map(
        body,
        mesh=grid,
        in_specs=(row, row, row, mat, row, row, vec, mat, row, row, vec, vec),
        out_specs=(row, row, P(), mat, row, row, mat, row, row, mat, row, row, vec, vec, vec, vec),
        check_vma=False,
    )
```
